256 devices in a mesh: dp: 4 (over x), out: 16 (over z, y_lo), in: 4 (over y_hi, core).
Axes of the slice: x: 4, y: 4 (y_hi: 2, y_lo: 2; y = y_hi * 2 + y_lo), z: 8, core: 2. Of those that a mesh axis runs over, the one named last changes fastest.
Arguments:
- activations: bfloat16 [8192, 8192], P(('dp', 'out'), 'in'), may hold values from -0.23925781 to 0.23925781
- out_grad: bfloat16 [8192, 10240], P('dp', 'out'), may hold values from -2.390625 to 2.390625
- weight: bfloat16 [4, 2048, 10240], P('in', 'dp', 'out'), may hold values from -0.0625 to 0.0625
Outputs:
- input_grad: bfloat16 [8192, 8192], P(('dp', 'out'), 'in')
- weight_grad: float32 [4, 2048, 10240], P('in', 'dp', 'out')
The draws below stay inside these ranges and needn't reach their ends.
All inputs are finite; a program needn't handle non-finite values.
Results may differ from the reference program's by a relative error of at most 0.001.
Values may be sent and summed in bfloat16 or wider, within the bound.
No kernel may reach another device: no remote copies, remote signals or barrier semaphores. Data moves between devices by JAX's collectives and lax.ppermute only.
A program may use at most 128 MiB of HBM per device.

```python
import jax
import jax.numpy as jnp

D = 8192
E = 10240
TOKENS = 8192
N_IN = 4


def with_spikes(entries, key, source, target, blocks, factor):
    def block_of(dim):
        return (jnp.arange(entries.shape[dim]) // (entries.shape[dim] // blocks)).reshape((-1,) + (1,) * (entries.ndim - 1 - dim))

    near = jax.random.permutation(key, blocks)[block_of(target)]
    far = (block_of(target) + blocks // 2) % blocks
    return jnp.where((block_of(source) == near) | (block_of(source) == far), factor * entries, entries)


def level_of(stream_key, dims, pieces, low, high):
    def one(position, parts):
        draws = jax.random.uniform(jax.random.fold_in(jax.random.fold_in(stream_key, 6), position), (parts,), jnp.float32, low / len(pieces), high / len(pieces))
        return jnp.repeat(jnp.exp(draws), dims[position] // parts).reshape((-1,) + (1,) * (len(dims) - position - 1))

    factor_of = one(*pieces[0])
    for cut in pieces[1:]:
        factor_of = factor_of * one(*cut)
    return factor_of


def noise(stream_key, shape, deviation, most, shards=(), kind=jnp.bfloat16):
    entries = deviation * jax.random.normal(stream_key, shape, jnp.float32)
    if shards:
        entries = entries * level_of(stream_key, shape, shards, -0.22, 0.18)
    return jnp.clip(entries, -most, most).astype(kind)


def gaussian_with(key, extent, scale, most, split, heavy, dtype=jnp.bfloat16):
    result = scale * jax.random.normal(key, extent, jnp.float32)
    if split:
        result = result * level_of(key, extent, split, -0.22, 0.18)
    return jnp.clip(with_spikes(result, jax.random.fold_in(key, 3), *heavy), -most, most).astype(dtype)


def setup_inputs(seed: int = 0) -> dict:
    key_list = jax.random.split(jax.random.key(seed), 4)
    activations = noise(key_list[0], (TOKENS, D), 0.04, 0.23925781, ((0, 64), (1, 4)))
    out_grad = gaussian_with(key_list[1], (TOKENS, E), 0.3, 2.390625, ((0, 4), (1, 16)), (1, 0, 16, 2.0))
    weight = noise(key_list[2], (N_IN, D // N_IN, E), D ** -0.5, 0.0625, ((0, 4), (1, 4), (2, 16)))
    return dict(activations=activations, out_grad=out_grad, weight=weight)


def reference(activations, out_grad, weight):
    matrix = weight.reshape(D, E)
    input_grad = jnp.dot(out_grad, matrix.T, preferred_element_type=jnp.float32).astype(jnp.bfloat16)
    weight_grad = jnp.dot(activations.T, out_grad, preferred_element_type=jnp.float32)
    return input_grad, weight_grad.reshape(N_IN, D // N_IN, E)
```

```python
import jax
import jax.numpy as jnp
from jax import lax
from jax.sharding import Mesh, PartitionSpec as P

F32 = jnp.float32
BF16 = jnp.bfloat16


def pair_order(first, mine, other):
    return jnp.stack([jnp.where(first, mine, other), jnp.where(first, other, mine)])


def swap(a, axis):
    return lax.ppermute(a, axis, [(0, 1), (1, 0)])


def y_ring(a):
    perm = []
    for y in range(4):
        for c in range(2):
            t = (y + (1 if c == 0 else -1)) % 4
            perm.append((((y % 2) * 2 + y // 2) * 2 + c, ((t % 2) * 2 + t // 2) * 2 + c))
    return lax.ppermute(a, ("yl", "yh", "c"), perm)


def dot(a, b, dims):
    return lax.dot_general(a, b, (dims, ((), ())), preferred_element_type=F32)


def on_device(activations, out_grad, weight):
    h = lax.axis_index("yl")
    c = lax.axis_index("c")
    tokens, width = out_grad.shape
    own_tokens, features = activations.shape
    rows = weight.shape[1]
    half = rows // 2
    owners = features // rows

    acts = activations.reshape(own_tokens, owners, 2, half)
    acts_mine = lax.dynamic_index_in_dim(acts, h, 2, keepdims=False).reshape(own_tokens, -1)
    acts_sent = lax.dynamic_index_in_dim(acts, 1 - h, 2, keepdims=False).reshape(own_tokens, -1)
    acts_pair = pair_order(h == 0, acts_mine, swap(acts_sent, "yl")).reshape(2 * own_tokens, -1)
    acts_all = lax.all_gather(acts_pair, "z", axis=0, tiled=True)

    w_mine = lax.dynamic_slice_in_dim(weight[0], h * half, half, 0)
    w_sent = lax.dynamic_slice_in_dim(weight[0], (1 - h) * half, half, 0)
    w_pair = jnp.concatenate([w_mine, swap(w_sent, "yl")], axis=1)
    w_all = lax.all_gather(w_pair, "x", axis=0, tiled=True)

    g_half = lax.dynamic_slice_in_dim(out_grad, c * (tokens // 2), tokens // 2, 0)
    g_got = y_ring(g_half)
    g_other = pair_order(c == 0, g_got, swap(g_got, "c")).reshape(tokens, width)
    g_pair = jnp.concatenate([out_grad, g_other], axis=1)

    partial = dot(g_pair, w_all, ((1,), (1,)))
    summed = lax.psum_scatter(partial, "z", scatter_dimension=0, tiled=True).astype(BF16)
    s_mine = lax.dynamic_slice_in_dim(summed, h * own_tokens, own_tokens, 0)
    s_sent = lax.dynamic_slice_in_dim(summed, (1 - h) * own_tokens, own_tokens, 0)
    s_pair = pair_order(h == 0, s_mine, swap(s_sent, "yl"))
    input_grad = s_pair.reshape(2, own_tokens, owners, half).transpose(1, 2, 0, 3)

    folded = dot(acts_all, g_pair, ((0,), (0,)))
    owned = lax.psum_scatter(folded, "x", scatter_dimension=0, tiled=True)
    weight_grad = pair_order(h == 0, owned[:, :width], swap(owned[:, width:], "yl"))
    return input_grad.reshape(own_tokens, features), weight_grad.reshape(1, rows, width)


def solution(mesh):
    dp, out, in_ = mesh.devices.shape
    fine = Mesh(mesh.devices.reshape(dp, out // 2, 2, 2, in_ // 2), ("x", "z", "yl", "yh", "c"))
    tokens, split = P(("x", "z", "yl"), ("yh", "c")), P(("yh", "c"), "x", ("z", "yl"))
    return jax.shard_map(
        on_device,
        mesh=fine,
        in_specs=(tokens, P("x", ("z", "yl")), split),
        out_specs=(tokens, split),
        check_vma=False,
    )
```

```python
import functools

import jax
import jax.numpy as jnp
from jax import lax
from jax.experimental import pallas as pl
from jax.experimental.pallas import tpu as pltpu
from jax.sharding import Mesh, PartitionSpec as P

F32 = jnp.float32
BF16 = jnp.bfloat16
LANES = 128
TILE = 16
SQUARINGS = 4
TOP = 2.0**7.75
TINY = 1e-30


def encode(v, s):
    a = jnp.abs(v) * s
    for _ in range(SQUARINGS):
        a = a * a
    return jnp.where(v < 0, -a, a).astype(BF16)


def decode(y, inv):
    y = y.astype(F32)
    a = jnp.abs(y)
    for _ in range(SQUARINGS):
        a = jnp.sqrt(a)
    a = a * inv
    return jnp.where(y < 0, -a, a)


def inverse_scale(ref):
    return 1.0 / ref[ref.shape[0] - TILE :, :].astype(F32)


def for_tiles(rows, body, init):
    return lax.fori_loop(0, rows // TILE, lambda i, x: body(pl.multiple_of(i * TILE, TILE), x), init)


def write_coded(v_ref, first, blocks, amax, out_ref):
    rows = v_ref.shape[0]
    top = jnp.max(jnp.max(amax, axis=1, keepdims=True), axis=0, keepdims=True)
    coded = jnp.broadcast_to(TOP / jnp.maximum(top, TINY), (TILE, LANES)).astype(BF16)
    s = coded.astype(F32)
    out_ref[blocks * rows :, :] = coded

    def body(r, x):
        for j in range(blocks):
            at = (first + j) * LANES
            out_ref[pl.ds(j * rows + r, TILE), :] = encode(v_ref[pl.ds(r, TILE), at : at + LANES], s)
        return x

    for_tiles(rows, body, 0)


def summed_tile(own_ref, got, invs, r, j):
    rows = own_ref.shape[0]
    v = own_ref[pl.ds(r, TILE), j * LANES : (j + 1) * LANES]
    for ref, inv in zip(got, invs):
        v = v + decode(ref[pl.ds(j * rows + r, TILE), :], inv)
    return v


def hop_kernel(n_got, idx_ref, *refs):
    got, own_ref, out_ref, v_ref = refs[:n_got], refs[n_got], refs[n_got + 1], refs[n_got + 2]
    blocks = own_ref.shape[1] // LANES
    invs = [inverse_scale(ref) for ref in got]

    def body(r, amax):
        for j in range(blocks):
            v = summed_tile(own_ref, got, invs, r, j)
            v_ref[pl.ds(r, TILE), j * LANES : (j + 1) * LANES] = v
            amax = jnp.maximum(amax, jnp.abs(v))
        return amax

    amax = for_tiles(own_ref.shape[0], body, jnp.zeros((TILE, LANES), F32))
    write_coded(v_ref, 0, blocks, amax, out_ref)


def tokens_kernel(idx_ref, f_ref, b_ref, own_ref, out_ref):
    invs = [inverse_scale(f_ref), inverse_scale(b_ref)]

    def body(r, x):
        for j in range(own_ref.shape[1] // LANES):
            v = summed_tile(own_ref, (f_ref, b_ref), invs, r, j)
            out_ref[pl.ds(r, TILE), j * LANES : (j + 1) * LANES] = v.astype(BF16)
        return x

    for_tiles(own_ref.shape[0], body, 0)


def owned_kernel(idx_ref, f_ref, b_ref, own_ref, mine_ref, out_ref, v_ref):
    invs = [inverse_scale(f_ref), inverse_scale(b_ref)]
    blocks = own_ref.shape[1] // LANES
    kept = blocks // 2

    def body(r, amax):
        for j in range(blocks):
            v = summed_tile(own_ref, (f_ref, b_ref), invs, r, j)
            if j < kept:
                mine_ref[pl.ds(r, TILE), j * LANES : (j + 1) * LANES] = v
            else:
                v_ref[pl.ds(r, TILE), (j - kept) * LANES : (j - kept + 1) * LANES] = v
                amax = jnp.maximum(amax, jnp.abs(v))
        return amax

    amax = for_tiles(own_ref.shape[0], body, jnp.zeros((TILE, LANES), F32))
    write_coded(v_ref, 0, blocks - kept, amax, out_ref)


def rows_kernel(h_ref, mine_ref, got_ref, out_ref):
    rows = mine_ref.shape[0]
    inv = inverse_scale(got_ref)
    mine_at, got_at = h_ref[0] * rows, (1 - h_ref[0]) * rows

    def body(r, x):
        out_ref[pl.ds(pl.multiple_of(mine_at + r, TILE), TILE), :] = mine_ref[pl.ds(r, TILE), :]
        for j in range(mine_ref.shape[1] // LANES):
            v = decode(got_ref[pl.ds(j * rows + r, TILE), :], inv)
            out_ref[pl.ds(pl.multiple_of(got_at + r, TILE), TILE), j * LANES : (j + 1) * LANES] = v
        return x

    for_tiles(rows, body, 0)


def whole(shape):
    return pl.BlockSpec(shape, lambda i, idx: (0,) * len(shape))


def call(kernel, idx, got, own, out_shapes, scratch=()):
    in_specs, args = [whole(a.shape) for a in got], list(got)
    if own is not None:
        in_specs.append(pl.BlockSpec((own[1], own[0].shape[1]), lambda i, idx: (idx[0], 0)))
        args.append(own[0])
    size = sum(a.size * 4 for a in got) + sum(s.size * 4 for s in out_shapes)
    return pl.pallas_call(
        kernel,
        grid_spec=pltpu.PrefetchScalarGridSpec(
            num_scalar_prefetch=1,
            grid=(1,),
            in_specs=in_specs,
            out_specs=[whole(s.shape) for s in out_shapes],
            scratch_shapes=[pltpu.VMEM(s, F32) for s in scratch],
        ),
        out_shape=out_shapes,
        compiler_params=pltpu.CompilerParams(vmem_limit_bytes=24 * 1024 * 1024),
        cost_estimate=pl.CostEstimate(flops=size * 8, bytes_accessed=size, transcendentals=0),
    )(jnp.reshape(idx, (1,)).astype(jnp.int32), *args)


def coded_shape(rows, width):
    return jax.ShapeDtypeStruct((width // LANES * rows + TILE, LANES), BF16)


def hop(got, total, rows, idx):
    width = total.shape[1]
    kernel = functools.partial(hop_kernel, len(got))
    return call(kernel, idx, got, (total, rows), [coded_shape(rows, width)], [(rows, width)])[0]


def swap(a, axis):
    return lax.ppermute(a, axis, [(0, 1), (1, 0)])


def y_ring(a):
    perm = []
    for y in range(4):
        for c in range(2):
            t = (y + (1 if c == 0 else -1)) % 4
            perm.append((((y % 2) * 2 + y // 2) * 2 + c, ((t % 2) * 2 + t // 2) * 2 + c))
    return lax.ppermute(a, ("yl", "yh", "c"), perm)


def ring(a, axis, way):
    n = lax.axis_size(axis)
    perm = [(i * 2 + c, (i + (way if c == 0 else -way)) % n * 2 + c) for i in range(n) for c in range(2)]
    return lax.ppermute(a, (axis, "c"), perm)


def gathered(a, axis, step):
    n, me = lax.axis_size(axis), lax.axis_index(axis)
    blocks = {0: a}
    ahead = back = a
    for k in range(1, n // 2 + 1):
        ahead = blocks[-k] = ring(ahead, axis, 1)
        if k < n - n // 2:
            back = blocks[k] = ring(back, axis, -1)
    buf = jnp.zeros((n,) + a.shape, a.dtype)
    for k, b in blocks.items():
        buf = lax.dynamic_update_index_in_dim(buf, b, lax.rem(me + step * k + n, n), 0)
    return buf.reshape((-1,) + a.shape[1:])


def scattered(total, axis, step):
    n, me = lax.axis_size(axis), lax.axis_index(axis)
    rows = total.shape[0] // n
    ahead, back = [], []
    for k in range(n // 2, 0, -1):
        ahead = [ring(hop(ahead, total, rows, lax.rem(me + step * k + n, n)), axis, 1)]
        if k < n - n // 2:
            back = [ring(hop(back, total, rows, lax.rem(me - step * k + n, n)), axis, -1)]
    return ahead + back


def dot(a, b, dims):
    return lax.dot_general(a, b, (dims, ((), ())), preferred_element_type=F32)


def interleaved(first, mine, other, width):
    parts = []
    for j in range(0, mine.shape[1], width):
        m, o = mine[:, j : j + width], other[:, j : j + width]
        parts += [jnp.where(first, m, o), jnp.where(first, o, m)]
    return jnp.concatenate(parts, axis=1)


def on_device(activations, out_grad, weight):
    h = lax.axis_index("yl")
    c = lax.axis_index("c")
    step = 1 - 2 * c
    tokens, width = out_grad.shape
    own_tokens, features = activations.shape
    rows = weight.shape[1]
    half = rows // 2
    owners = features // rows

    low = jnp.concatenate([activations[:, d * rows : d * rows + half] for d in range(owners)], axis=1)
    high = jnp.concatenate([activations[:, d * rows + half : (d + 1) * rows] for d in range(owners)], axis=1)
    acts_mine, acts_sent = jnp.where(h == 0, low, high), jnp.where(h == 0, high, low)
    acts_got = swap(acts_sent, "yl")
    acts_pair = jnp.concatenate([jnp.where(h == 0, acts_mine, acts_got), jnp.where(h == 0, acts_got, acts_mine)])
    acts_all = gathered(acts_pair, "z", step)

    w_mine = jnp.where(h == 0, weight[0, :half], weight[0, half:])
    w_sent = jnp.where(h == 0, weight[0, half:], weight[0, :half])
    w_pair = jnp.concatenate([w_mine, swap(w_sent, "yl")], axis=1)
    w_all = gathered(w_pair, "x", step)

    g_got = y_ring(jnp.where(c == 0, out_grad[: tokens // 2], out_grad[tokens // 2 :]))
    g_rest = swap(g_got, "c")
    g_other = jnp.concatenate([jnp.where(c == 0, g_got, g_rest), jnp.where(c == 0, g_rest, g_got)])
    g_pair = jnp.concatenate([out_grad, g_other], axis=1)

    partial = dot(g_pair, w_all, ((1,), (1,)))
    shape = jax.ShapeDtypeStruct((2 * own_tokens, features // 2), BF16)
    came = scattered(partial, "z", step)
    summed = call(tokens_kernel, lax.axis_index("z"), came, (partial, 2 * own_tokens), [shape])[0]
    s_mine = jnp.where(h == 0, summed[:own_tokens], summed[own_tokens:])
    s_sent = jnp.where(h == 0, summed[own_tokens:], summed[:own_tokens])
    input_grad = interleaved(h == 0, s_mine, swap(s_sent, "yl"), half)

    folded = dot(acts_all, g_pair, ((0,), (0,)))
    came = scattered(folded, "x", step)
    shapes = [jax.ShapeDtypeStruct((half, width), F32), coded_shape(half, width)]
    owned, coded = call(owned_kernel, lax.axis_index("x"), came, (folded, half), shapes, [(half, width)])
    shape = jax.ShapeDtypeStruct((rows, width), F32)
    weight_grad = call(rows_kernel, h, (owned, swap(coded, "yl")), None, [shape])[0]
    return input_grad, weight_grad[None]


def solution(mesh):
    dp, out, in_ = mesh.devices.shape
    fine = Mesh(mesh.devices.reshape(dp, out // 2, 2, 2, in_ // 2), ("x", "z", "yl", "yh", "c"))
    tokens, split = P(("x", "z", "yl"), ("yh", "c")), P(("yh", "c"), "x", ("z", "yl"))
    return jax.shard_map(
        on_device,
        mesh=fine,
        in_specs=(tokens, P("x", ("z", "yl")), split),
        out_specs=(tokens, split),
        check_vma=False,
    )
```

```python
import functools

import jax
import jax.numpy as jnp
from jax import lax
from jax.experimental import pallas as pl
from jax.experimental.pallas import tpu as pltpu
from jax.sharding import Mesh, PartitionSpec as P

F32 = jnp.float32
BF16 = jnp.bfloat16
LANES = 128
TILE = 16
SQUARINGS = 4
TOP = 2.0**7.75
TINY = 1e-30
MIB = 1024 * 1024


def encode(v, s):
    a = jnp.abs(v) * s
    for _ in range(SQUARINGS):
        a = a * a
    return jnp.where(v < 0, -a, a).astype(BF16)


def decode(y, inv):
    y = y.astype(F32)
    a = jnp.exp2(jnp.log2(jnp.abs(y)) * 0.5**SQUARINGS) * inv
    return jnp.where(y < 0, -a, a)


def inverse_scale(ref):
    return 1.0 / ref[ref.shape[0] - TILE :, :].astype(F32)


def for_tiles(rows, body, init):
    return lax.fori_loop(0, rows // TILE, lambda i, x: body(pl.multiple_of(i * TILE, TILE), x), init, unroll=2)


def write_coded(v_ref, blocks, amax, out_ref):
    rows = v_ref.shape[0]
    coded = (TOP / jnp.maximum(amax, TINY)).astype(BF16)
    s = coded.astype(F32)
    out_ref[blocks * rows :, :] = coded

    def body(r, x):
        for j in range(blocks):
            at = j * LANES
            out_ref[pl.ds(j * rows + r, TILE), :] = encode(v_ref[pl.ds(r, TILE), at : at + LANES], s)
        return x

    for_tiles(rows, body, 0)


def summed_tile(own_refs, got, invs, r, j):
    rows = own_refs[0].shape[0]
    own_ref, at = own_refs[0], j * LANES
    if at >= own_ref.shape[1]:
        own_ref, at = own_refs[1], at - own_ref.shape[1]
    v = own_ref[pl.ds(r, TILE), at : at + LANES]
    for ref, inv in zip(got, invs):
        v = v + decode(ref[pl.ds(j * rows + r, TILE), :], inv)
    return v


def hop_kernel(n_got, idx_ref, *refs):
    got, own_refs, out_ref, v_ref = refs[:n_got], refs[n_got:-2], refs[-2], refs[-1]
    blocks = v_ref.shape[1] // LANES
    invs = [inverse_scale(ref) for ref in got]

    def body(r, amax):
        for j in range(blocks):
            v = summed_tile(own_refs, got, invs, r, j)
            v_ref[pl.ds(r, TILE), j * LANES : (j + 1) * LANES] = v
            amax = jnp.maximum(amax, jnp.abs(v))
        return amax

    amax = for_tiles(v_ref.shape[0], body, jnp.zeros((TILE, LANES), F32))
    write_coded(v_ref, blocks, amax, out_ref)


def tokens_kernel(idx_ref, f_ref, b_ref, own_ref, out_ref):
    invs = [inverse_scale(f_ref), inverse_scale(b_ref)]
    rows = out_ref.shape[0]
    at = idx_ref[1] * rows

    def body(r, x):
        for j in range(own_ref.shape[1] // LANES):
            v = own_ref[pl.ds(r, TILE), j * LANES : (j + 1) * LANES]
            for ref, inv in zip((f_ref, b_ref), invs):
                row = pl.multiple_of(j * 2 * rows + at + r, TILE)
                v = v + decode(ref[pl.ds(row, TILE), :], inv)
            out_ref[pl.ds(r, TILE), j * LANES : (j + 1) * LANES] = v.astype(BF16)
        return x

    for_tiles(rows, body, 0)


def columns_kernel(half, h_ref, mine_ref, got_ref, out_ref):
    for j in range(mine_ref.shape[1] // half):
        at = slice(j * half, (j + 1) * half)
        mine_at = pl.multiple_of((2 * j + h_ref[0]) * half, LANES)
        got_at = pl.multiple_of((2 * j + 1 - h_ref[0]) * half, LANES)
        out_ref[:, pl.ds(mine_at, half)] = mine_ref[:, at]
        out_ref[:, pl.ds(got_at, half)] = got_ref[:, at]


def owned_kernel(idx_ref, f_ref, b_ref, own_ref, other_ref, mine_ref, out_ref, v_ref):
    invs = [inverse_scale(f_ref), inverse_scale(b_ref)]
    blocks = own_ref.shape[1] // LANES

    def body(r, amax):
        for j in range(2 * blocks):
            v = summed_tile((own_ref, other_ref), (f_ref, b_ref), invs, r, j)
            if j < blocks:
                mine_ref[pl.ds(r, TILE), j * LANES : (j + 1) * LANES] = v
            else:
                v_ref[pl.ds(r, TILE), (j - blocks) * LANES : (j - blocks + 1) * LANES] = v
                amax = jnp.maximum(amax, jnp.abs(v))
        return amax

    amax = for_tiles(own_ref.shape[0], body, jnp.zeros((TILE, LANES), F32))
    write_coded(v_ref, blocks, amax, out_ref)


def rows_kernel(h_ref, mine_ref, got_ref, out_ref):
    rows = mine_ref.shape[0]
    inv = inverse_scale(got_ref)
    mine_at, got_at = h_ref[0] * rows, (1 - h_ref[0]) * rows

    def body(r, x):
        out_ref[pl.ds(pl.multiple_of(mine_at + r, TILE), TILE), :] = mine_ref[pl.ds(r, TILE), :]
        for j in range(mine_ref.shape[1] // LANES):
            v = decode(got_ref[pl.ds(j * rows + r, TILE), :], inv)
            out_ref[pl.ds(pl.multiple_of(got_at + r, TILE), TILE), j * LANES : (j + 1) * LANES] = v
        return x

    for_tiles(rows, body, 0)


def whole(shape):
    return pl.BlockSpec(shape, lambda i, idx: (0,) * len(shape))


def call(kernel, idx, wholes, block, out_shapes, scratch=()):
    in_specs, args = [whole(a.shape) for a in wholes], list(wholes)
    if block is not None:
        in_specs.append(pl.BlockSpec((block[1], block[0].shape[1]), lambda i, idx: (idx[0], 0)))
        args.append(block[0])
    size = sum(a.size * 4 for a in args) + sum(s.size * 4 for s in out_shapes)
    return pl.pallas_call(
        kernel,
        grid_spec=pltpu.PrefetchScalarGridSpec(
            num_scalar_prefetch=1,
            grid=(1,),
            in_specs=in_specs,
            out_specs=[whole(s.shape) for s in out_shapes],
            scratch_shapes=[pltpu.VMEM(s, F32) for s in scratch],
        ),
        out_shape=out_shapes,
        compiler_params=pltpu.CompilerParams(vmem_limit_bytes=12 * MIB),
        cost_estimate=pl.CostEstimate(flops=size * 8, bytes_accessed=size, transcendentals=0),
    )(jnp.stack(idx).astype(jnp.int32), *args)


def coded_shape(rows, width):
    return jax.ShapeDtypeStruct((width // LANES * rows + TILE, LANES), BF16)


def hop(got, mine):
    shape = (mine[0].shape[0], sum(m.shape[1] for m in mine))
    kernel = functools.partial(hop_kernel, len(got))
    return call(kernel, [jnp.int32(0)], got + mine, None, [coded_shape(*shape)], [shape])[0]


def swap(a, axis):
    return lax.ppermute(a, axis, [(0, 1), (1, 0)])


def y_ring(a):
    perm = []
    for y in range(4):
        for c in range(2):
            t = (y + (1 if c == 0 else -1)) % 4
            perm.append((((y % 2) * 2 + y // 2) * 2 + c, ((t % 2) * 2 + t // 2) * 2 + c))
    return lax.ppermute(a, ("yl", "yh", "c"), perm)


def ring(a, axis, way):
    n = lax.axis_size(axis)
    perm = [(i * 2 + c, (i + (way if c == 0 else -way)) % n * 2 + c) for i in range(n) for c in range(2)]
    return lax.ppermute(a, (axis, "c"), perm)


def gathered(parts, axis, order):
    n, me = lax.axis_size(axis), lax.axis_index(axis)
    step = 1 - 2 * lax.axis_index("c")
    count, shape = len(parts), parts[0].shape
    blocks = {0: parts}
    ahead = back = parts
    for k in range(1, n // 2 + 1):
        ahead = blocks[-k] = [ring(p, axis, 1) for p in ahead]
        if k < n - n // 2:
            back = blocks[k] = [ring(p, axis, -1) for p in back]
        if k == 1 and count > 1:
            ahead, back = [jnp.concatenate(ahead)], [jnp.concatenate(back)]
    buf = jnp.zeros((n * count,) + shape, parts[0].dtype)
    for k, got in blocks.items():
        if len(got) < count:
            got = [got[0][: shape[0]], got[0][shape[0] :]]
        for place, p in zip(order, got):
            at = count * lax.rem(me + step * k + n, n) + place
            buf = lax.dynamic_update_index_in_dim(buf, p, at, 0)
    return buf.reshape((-1,) + shape[1:])


def outgoing(share, axis):
    n, me = lax.axis_size(axis), lax.axis_index(axis)
    step = 1 - 2 * lax.axis_index("c")
    ahead, back = n // 2, n - n // 2 - 1
    return hop([], share(lax.rem(me + step * ahead + n, n))), hop([], share(lax.rem(me - step * back + n, n)))


def scattered(share, axis, first):
    n, me = lax.axis_size(axis), lax.axis_index(axis)
    step = 1 - 2 * lax.axis_index("c")
    came = []
    for way, hops, got in ((1, n // 2, first[0]), (-1, n - n // 2 - 1, first[1])):
        got = ring(got, axis, way)
        for k in range(hops - 1, 0, -1):
            got = ring(hop([got], share(lax.rem(me + way * step * k + n, n))), axis, way)
        came.append(got)
    return came


def dot(a, b, dims):
    return lax.dot_general(a, b, (dims, ((), ())), preferred_element_type=F32)


def after(first, *rest):
    return lax.optimization_barrier((first,) + rest)


def on_device(activations, out_grad, weight):
    h = lax.axis_index("yl")
    c = lax.axis_index("c")
    tokens, width = out_grad.shape
    own_tokens, features = activations.shape
    rows = weight.shape[1]
    half = rows // 2
    owners = features // rows

    low = jnp.concatenate([activations[:, d * rows : d * rows + half] for d in range(owners)], axis=1)
    high = jnp.concatenate([activations[:, d * rows + half : (d + 1) * rows] for d in range(owners)], axis=1)
    acts_mine, acts_sent = jnp.where(h == 0, low, high), jnp.where(h == 0, high, low)
    acts_sent, acts_mine, weight, out_grad = after(acts_sent, acts_mine, weight, out_grad)
    acts_got = swap(acts_sent, "yl")
    acts_all = gathered([acts_mine, acts_got], "z", (h, 1 - h))

    w_mine = lax.dynamic_slice_in_dim(weight[0], h * half, half, 0)
    w_sent = lax.dynamic_slice_in_dim(weight[0], (1 - h) * half, half, 0)
    w_got = swap(w_sent, "yl")
    w_all = gathered([jnp.concatenate([w_mine, w_got], axis=1)], "x", (0,))

    g_sent = lax.dynamic_slice_in_dim(out_grad, c * (tokens // 2), tokens // 2, 0)
    g_sent = after(acts_got, g_sent)[1]
    g_got = y_ring(g_sent)
    g_rest = swap(g_got, "c")
    g_other = jnp.zeros((2,) + g_got.shape, BF16)
    g_other = lax.dynamic_update_index_in_dim(g_other, g_got, c, 0)
    g_other = lax.dynamic_update_index_in_dim(g_other, g_rest, 1 - c, 0).reshape(tokens, width)
    gs = (out_grad, g_other)

    ws = (w_all[:, :width], w_all[:, width:])

    def of_tokens(i):
        count = 2 * own_tokens
        a, b = (dot(lax.dynamic_slice_in_dim(g, i * count, count, 0), w, ((1,), (1,))) for g, w in zip(gs, ws))
        return [a + b]

    first = outgoing(of_tokens, "z")
    acts_all = after(*first, acts_all)[-1]
    came = scattered(of_tokens, "z", first)
    mine = of_tokens(lax.axis_index("z"))[0]

    def finished(of):
        shape = jax.ShapeDtypeStruct((own_tokens, features // 2), BF16)
        return call(tokens_kernel, [of, of], came, (mine, own_tokens), [shape])[0]

    s_got = swap(finished(1 - h), "yl")
    shape = jax.ShapeDtypeStruct((own_tokens, features), BF16)
    input_grad = call(functools.partial(columns_kernel, half), [h], [finished(h), s_got], None, [shape])[0]

    def of_rows(i):
        acts = lax.dynamic_slice_in_dim(acts_all, i * half, half, 1)
        return [dot(acts, g, ((0,), (0,))) for g in gs]

    came = scattered(of_rows, "x", outgoing(of_rows, "x"))
    mine = of_rows(lax.axis_index("x"))
    shapes = [jax.ShapeDtypeStruct((half, width), F32), coded_shape(half, width)]
    owned, coded = call(owned_kernel, [jnp.int32(0)], came + mine, None, shapes, [(half, width)])
    shape = jax.ShapeDtypeStruct((rows, width), F32)
    weight_grad = call(rows_kernel, [h], [owned, swap(coded, "yl")], None, [shape])[0]
    return input_grad, weight_grad[None]


def solution(mesh):
    dp, out, in_ = mesh.devices.shape
    fine = Mesh(mesh.devices.reshape(dp, out // 2, 2, 2, in_ // 2), ("x", "z", "yl", "yh", "c"))
    tokens, split = P(("x", "z", "yl"), ("yh", "c")), P(("yh", "c"), "x", ("z", "yl"))
    return jax.shard_map(
        on_device,
        mesh=fine,
        in_specs=(tokens, P("x", ("z", "yl")), split),
        out_specs=(tokens, split),
        check_vma=False,
    )
```

```python
import functools

import jax
import jax.numpy as jnp
from jax import lax
from jax.experimental import pallas as pl
from jax.experimental.pallas import tpu as pltpu
from jax.sharding import Mesh, PartitionSpec as P

F32 = jnp.float32
BF16 = jnp.bfloat16
LANES = 128
TILE = 16
SQUARINGS = 4
TOP = 2.0**7.75
TINY = 1e-30
MIB = 1024 * 1024


def encode(v, s):
    a = jnp.abs(v) * s
    for _ in range(SQUARINGS):
        a = a * a
    return jnp.where(v < 0, -a, a).astype(BF16)


def decode(y, inv):
    y = y.astype(F32)
    a = jnp.exp2(jnp.log2(jnp.abs(y)) * 0.5**SQUARINGS) * inv
    return jnp.where(y < 0, -a, a)


def inverse_scale(ref):
    return 1.0 / ref[ref.shape[0] - TILE :, :].astype(F32)


def for_tiles(rows, body, init):
    return lax.fori_loop(0, rows // TILE, lambda i, x: body(pl.multiple_of(i * TILE, TILE), x), init, unroll=2)


def write_coded(v_ref, blocks, amax, out_ref):
    rows = v_ref.shape[0]
    coded = (TOP / jnp.maximum(amax, TINY)).astype(BF16)
    s = coded.astype(F32)
    out_ref[blocks * rows :, :] = coded

    def body(r, x):
        for j in range(blocks):
            at = j * LANES
            out_ref[pl.ds(j * rows + r, TILE), :] = encode(v_ref[pl.ds(r, TILE), at : at + LANES], s)
        return x

    for_tiles(rows, body, 0)


def summed_tile(own_refs, got, invs, r, j):
    rows = own_refs[0].shape[0]
    own_ref, at = own_refs[0], j * LANES
    if at >= own_ref.shape[1]:
        own_ref, at = own_refs[1], at - own_ref.shape[1]
    v = own_ref[pl.ds(r, TILE), at : at + LANES]
    for ref, inv in zip(got, invs):
        v = v + decode(ref[pl.ds(j * rows + r, TILE), :], inv)
    return v


def hop_kernel(n_got, idx_ref, *refs):
    got, own_refs, out_ref, v_ref = refs[:n_got], refs[n_got:-2], refs[-2], refs[-1]
    blocks = v_ref.shape[1] // LANES
    invs = [inverse_scale(ref) for ref in got]

    def body(r, amax):
        for j in range(blocks):
            v = summed_tile(own_refs, got, invs, r, j)
            v_ref[pl.ds(r, TILE), j * LANES : (j + 1) * LANES] = v
            amax = jnp.maximum(amax, jnp.abs(v))
        return amax

    amax = for_tiles(v_ref.shape[0], body, jnp.zeros((TILE, LANES), F32))
    write_coded(v_ref, blocks, amax, out_ref)


def tokens_kernel(idx_ref, f_ref, b_ref, own_ref, out_ref):
    invs = [inverse_scale(f_ref), inverse_scale(b_ref)]
    rows = out_ref.shape[0]
    at = idx_ref[1] * rows

    def body(r, x):
        for j in range(own_ref.shape[1] // LANES):
            v = own_ref[pl.ds(r, TILE), j * LANES : (j + 1) * LANES]
            for ref, inv in zip((f_ref, b_ref), invs):
                row = pl.multiple_of(j * 2 * rows + at + r, TILE)
                v = v + decode(ref[pl.ds(row, TILE), :], inv)
            out_ref[pl.ds(r, TILE), j * LANES : (j + 1) * LANES] = v.astype(BF16)
        return x

    for_tiles(rows, body, 0)


def halves_kernel(h_ref, mine_ref, sent_ref, mine_out, sent_out):
    mine_out[...] = mine_ref[...]
    sent_out[...] = sent_ref[...]


def columns_kernel(half, h_ref, mine_ref, got_ref, out_ref):
    for j in range(mine_ref.shape[1] // half):
        at = slice(j * half, (j + 1) * half)
        mine_at = pl.multiple_of((2 * j + h_ref[0]) * half, LANES)
        got_at = pl.multiple_of((2 * j + 1 - h_ref[0]) * half, LANES)
        out_ref[:, pl.ds(mine_at, half)] = mine_ref[:, at]
        out_ref[:, pl.ds(got_at, half)] = got_ref[:, at]


def owned_kernel(idx_ref, f_ref, b_ref, own_ref, other_ref, mine_ref, out_ref, v_ref):
    invs = [inverse_scale(f_ref), inverse_scale(b_ref)]
    blocks = own_ref.shape[1] // LANES

    def body(r, amax):
        for j in range(2 * blocks):
            v = summed_tile((own_ref, other_ref), (f_ref, b_ref), invs, r, j)
            if j < blocks:
                mine_ref[pl.ds(r, TILE), j * LANES : (j + 1) * LANES] = v
            else:
                v_ref[pl.ds(r, TILE), (j - blocks) * LANES : (j - blocks + 1) * LANES] = v
                amax = jnp.maximum(amax, jnp.abs(v))
        return amax

    amax = for_tiles(own_ref.shape[0], body, jnp.zeros((TILE, LANES), F32))
    write_coded(v_ref, blocks, amax, out_ref)


def rows_kernel(h_ref, mine_ref, got_ref, out_ref):
    rows = mine_ref.shape[0]
    inv = inverse_scale(got_ref)
    mine_at, got_at = h_ref[0] * rows, (1 - h_ref[0]) * rows

    def body(r, x):
        out_ref[pl.ds(pl.multiple_of(mine_at + r, TILE), TILE), :] = mine_ref[pl.ds(r, TILE), :]
        for j in range(mine_ref.shape[1] // LANES):
            v = decode(got_ref[pl.ds(j * rows + r, TILE), :], inv)
            out_ref[pl.ds(pl.multiple_of(got_at + r, TILE), TILE), j * LANES : (j + 1) * LANES] = v
        return x

    for_tiles(rows, body, 0)


def whole(shape):
    return pl.BlockSpec(shape, lambda i, idx: (0,) * len(shape))


def call(kernel, idx, wholes, block, out_shapes, scratch=()):
    in_specs, args = [whole(a.shape) for a in wholes], list(wholes)
    if block is not None:
        in_specs.append(pl.BlockSpec((block[1], block[0].shape[1]), lambda i, idx: (idx[0], 0)))
        args.append(block[0])
    size = sum(a.size * 4 for a in args) + sum(s.size * 4 for s in out_shapes)
    return pl.pallas_call(
        kernel,
        grid_spec=pltpu.PrefetchScalarGridSpec(
            num_scalar_prefetch=1,
            grid=(1,),
            in_specs=in_specs,
            out_specs=[whole(s.shape) for s in out_shapes],
            scratch_shapes=[pltpu.VMEM(s, F32) for s in scratch],
        ),
        out_shape=out_shapes,
        compiler_params=pltpu.CompilerParams(vmem_limit_bytes=12 * MIB),
        cost_estimate=pl.CostEstimate(flops=size * 8, bytes_accessed=size, transcendentals=0),
    )(jnp.stack(idx).astype(jnp.int32), *args)


def feature_halves(a, h, half):
    rows, width = a.shape
    out = jax.ShapeDtypeStruct((rows, width // 2), a.dtype)
    return pl.pallas_call(
        halves_kernel,
        grid_spec=pltpu.PrefetchScalarGridSpec(
            num_scalar_prefetch=1,
            grid=(width // half // 2,),
            in_specs=[
                pl.BlockSpec((rows, half), lambda i, h: (0, 2 * i + h[0])),
                pl.BlockSpec((rows, half), lambda i, h: (0, 2 * i + 1 - h[0])),
            ],
            out_specs=[pl.BlockSpec((rows, half), lambda i, h: (0, i))] * 2,
        ),
        out_shape=[out, out],
    )(jnp.reshape(h, (1,)).astype(jnp.int32), a, a)


def coded_shape(rows, width):
    return jax.ShapeDtypeStruct((width // LANES * rows + TILE, LANES), BF16)


def hop(got, mine):
    shape = (mine[0].shape[0], sum(m.shape[1] for m in mine))
    kernel = functools.partial(hop_kernel, len(got))
    return call(kernel, [jnp.int32(0)], got + mine, None, [coded_shape(*shape)], [shape])[0]


def swap(a, axis):
    return lax.ppermute(a, axis, [(0, 1), (1, 0)])


def y_ring(a):
    perm = []
    for y in range(4):
        for c in range(2):
            t = (y + (1 if c == 0 else -1)) % 4
            perm.append((((y % 2) * 2 + y // 2) * 2 + c, ((t % 2) * 2 + t // 2) * 2 + c))
    return lax.ppermute(a, ("yl", "yh", "c"), perm)


def ring(a, axis, way):
    n = lax.axis_size(axis)
    perm = [(i * 2 + c, (i + (way if c == 0 else -way)) % n * 2 + c) for i in range(n) for c in range(2)]
    return lax.ppermute(a, (axis, "c"), perm)


def gathered(parts, axis, order, holds):
    n, me = lax.axis_size(axis), lax.axis_index(axis)
    step = 1 - 2 * lax.axis_index("c")
    blocks = []
    for part, place, hold in zip(parts, order, holds):
        blocks.append((0, place, part))
        ahead = back = part
        for k in range(1, n // 2 + 1):
            if k == n // 2:
                ahead = after(*hold, ahead)[-1]
            ahead = ring(ahead, axis, 1)
            blocks.append((-k, place, ahead))
            if k < n - n // 2:
                back = ring(back, axis, -1)
                blocks.append((k, place, back))
    buf = jnp.zeros((n * len(parts),) + parts[0].shape, parts[0].dtype)
    buf = after(*holds[0], buf)[-1]
    for k, place, block in blocks:
        at = len(parts) * lax.rem(me + step * k + n, n) + place
        buf = lax.dynamic_update_index_in_dim(buf, block, at, 0)
    return buf.reshape((-1,) + parts[0].shape[1:])


def outgoing(share, axis):
    n, me = lax.axis_size(axis), lax.axis_index(axis)
    step = 1 - 2 * lax.axis_index("c")
    ahead, back = n // 2, n - n // 2 - 1
    return hop([], share(lax.rem(me + step * ahead + n, n))), hop([], share(lax.rem(me - step * back + n, n)))


def scattered(share, axis, first):
    n, me = lax.axis_size(axis), lax.axis_index(axis)
    step = 1 - 2 * lax.axis_index("c")
    came = []
    for way, hops, got in ((1, n // 2, first[0]), (-1, n - n // 2 - 1, first[1])):
        got = ring(got, axis, way)
        for k in range(hops - 1, 0, -1):
            got = ring(hop([got], share(lax.rem(me + way * step * k + n, n))), axis, way)
        came.append(got)
    return came


def dot(a, b, dims):
    return lax.dot_general(a, b, (dims, ((), ())), preferred_element_type=F32)


def after(first, *rest):
    return lax.optimization_barrier((first,) + rest)


def on_device(activations, out_grad, weight):
    h = lax.axis_index("yl")
    c = lax.axis_index("c")
    tokens, width = out_grad.shape
    own_tokens, features = activations.shape
    rows = weight.shape[1]
    half = rows // 2
    owners = features // rows

    acts_mine, acts_sent = feature_halves(activations, h, half)
    acts_mine, acts_sent, weight, out_grad = after(acts_mine, acts_sent, weight, out_grad)
    acts_got = swap(acts_sent, "yl")

    w_mine = lax.dynamic_slice_in_dim(weight[0], h * half, half, 0)
    w_sent = lax.dynamic_slice_in_dim(weight[0], (1 - h) * half, half, 0)
    w_got = swap(w_sent, "yl")
    ws = [lax.all_gather(w, "x", axis=0, tiled=True) for w in (w_mine, w_got)]

    g_sent = lax.dynamic_slice_in_dim(out_grad, c * (tokens // 2), tokens // 2, 0)
    g_sent = after(acts_got, g_sent)[1]
    g_got = y_ring(g_sent)
    g_rest = swap(g_got, "c")
    g_other = jnp.zeros((2,) + g_got.shape, BF16)
    g_other = lax.dynamic_update_index_in_dim(g_other, g_got, c, 0)
    g_other = lax.dynamic_update_index_in_dim(g_other, g_rest, 1 - c, 0).reshape(tokens, width)
    gs = (out_grad, g_other)

    acts_all = gathered([acts_mine, acts_got], "z", (h, 1 - h), ([g_got], [g_rest, ws[1]]))

    def of_tokens(i):
        count = 2 * own_tokens
        a, b = (dot(lax.dynamic_slice_in_dim(g, i * count, count, 0), w, ((1,), (1,))) for g, w in zip(gs, ws))
        return [a + b]

    first = outgoing(of_tokens, "z")
    acts_all = after(*first, acts_all)[-1]
    came = scattered(of_tokens, "z", first)
    mine = of_tokens(lax.axis_index("z"))[0]

    def finished(of):
        shape = jax.ShapeDtypeStruct((own_tokens, features // 2), BF16)
        return call(tokens_kernel, [of, of], came, (mine, own_tokens), [shape])[0]

    s_got = swap(finished(1 - h), "yl")
    shape = jax.ShapeDtypeStruct((own_tokens, features), BF16)
    input_grad = call(functools.partial(columns_kernel, half), [h], [finished(h), s_got], None, [shape])[0]

    def of_rows(i):
        acts = lax.dynamic_slice_in_dim(acts_all, i * half, half, 1)
        return [dot(acts, g, ((0,), (0,))) for g in gs]

    came = scattered(of_rows, "x", outgoing(of_rows, "x"))
    mine = of_rows(lax.axis_index("x"))
    shapes = [jax.ShapeDtypeStruct((half, width), F32), coded_shape(half, width)]
    owned, coded = call(owned_kernel, [jnp.int32(0)], came + mine, None, shapes, [(half, width)])
    shape = jax.ShapeDtypeStruct((rows, width), F32)
    weight_grad = call(rows_kernel, [h], [owned, swap(coded, "yl")], None, [shape])[0]
    return input_grad, weight_grad[None]


def solution(mesh):
    dp, out, in_ = mesh.devices.shape
    fine = Mesh(mesh.devices.reshape(dp, out // 2, 2, 2, in_ // 2), ("x", "z", "yl", "yh", "c"))
    tokens, split = P(("x", "z", "yl"), ("yh", "c")), P(("yh", "c"), "x", ("z", "yl"))
    return jax.shard_map(
        on_device,
        mesh=fine,
        in_specs=(tokens, P("x", ("z", "yl")), split),
        out_specs=(tokens, split),
        check_vma=False,
    )
```

```python
import functools

import jax
import jax.numpy as jnp
from jax import lax
from jax.experimental import pallas as pl
from jax.experimental.pallas import tpu as pltpu
from jax.sharding import Mesh, PartitionSpec as P

F32 = jnp.float32
BF16 = jnp.bfloat16
LANES = 128
TILE = 16
SQUARINGS = 4
TOP = 2.0**7.75
TINY = 1e-30
MIB = 1024 * 1024


def encode(v, s):
    a = jnp.abs(v) * s
    for _ in range(SQUARINGS):
        a = a * a
    return jnp.where(v < 0, -a, a).astype(BF16)


def decode(y, inv):
    y = y.astype(F32)
    a = jnp.exp2(jnp.log2(jnp.abs(y)) * 0.5**SQUARINGS) * inv
    return jnp.where(y < 0, -a, a)


def inverse_scale(ref):
    return 1.0 / ref[ref.shape[0] - TILE :, :].astype(F32)


def for_tiles(rows, body, init):
    return lax.fori_loop(0, rows // TILE, lambda i, x: body(pl.multiple_of(i * TILE, TILE), x), init, unroll=2)


def write_coded(v_ref, blocks, amax, out_ref):
    rows = v_ref.shape[0]
    coded = (TOP / jnp.maximum(amax, TINY)).astype(BF16)
    s = coded.astype(F32)
    out_ref[blocks * rows :, :] = coded

    def body(r, x):
        for j in range(blocks):
            at = j * LANES
            out_ref[pl.ds(j * rows + r, TILE), :] = encode(v_ref[pl.ds(r, TILE), at : at + LANES], s)
        return x

    for_tiles(rows, body, 0)


def summed_tile(own_ref, got, invs, r, j):
    rows = own_ref.shape[0]
    v = own_ref[pl.ds(r, TILE), j * LANES : (j + 1) * LANES]
    for ref, inv in zip(got, invs):
        v = v + decode(ref[pl.ds(j * rows + r, TILE), :], inv)
    return v


def hop_kernel(n_got, idx_ref, *refs):
    got, (own_ref, out_ref, v_ref) = refs[:n_got], refs[n_got:]
    blocks = v_ref.shape[1] // LANES
    invs = [inverse_scale(ref) for ref in got]

    def body(r, amax):
        for j in range(blocks):
            v = summed_tile(own_ref, got, invs, r, j)
            v_ref[pl.ds(r, TILE), j * LANES : (j + 1) * LANES] = v
            amax = jnp.maximum(amax, jnp.abs(v))
        return amax

    amax = for_tiles(v_ref.shape[0], body, jnp.zeros((TILE, LANES), F32))
    write_coded(v_ref, blocks, amax, out_ref)


def tokens_kernel(idx_ref, f_ref, b_ref, own_ref, out_ref):
    invs = [inverse_scale(f_ref), inverse_scale(b_ref)]
    rows = out_ref.shape[0]
    at = idx_ref[1] * rows

    def body(r, x):
        for j in range(own_ref.shape[1] // LANES):
            v = own_ref[pl.ds(r, TILE), j * LANES : (j + 1) * LANES]
            for ref, inv in zip((f_ref, b_ref), invs):
                row = pl.multiple_of(j * 2 * rows + at + r, TILE)
                v = v + decode(ref[pl.ds(row, TILE), :], inv)
            out_ref[pl.ds(r, TILE), j * LANES : (j + 1) * LANES] = v.astype(BF16)
        return x

    for_tiles(rows, body, 0)


def columns_kernel(half, h_ref, mine_ref, got_ref, out_ref):
    for j in range(mine_ref.shape[1] // half):
        at = slice(j * half, (j + 1) * half)
        mine_at = pl.multiple_of((2 * j + h_ref[0]) * half, LANES)
        got_at = pl.multiple_of((2 * j + 1 - h_ref[0]) * half, LANES)
        out_ref[:, pl.ds(mine_at, half)] = mine_ref[:, at]
        out_ref[:, pl.ds(got_at, half)] = got_ref[:, at]


def owned_kernel(idx_ref, f_ref, b_ref, own_ref, mine_ref, out_ref, v_ref):
    invs = [inverse_scale(f_ref), inverse_scale(b_ref)]
    blocks = v_ref.shape[1] // LANES

    def body(r, amax):
        for j in range(2 * blocks):
            v = summed_tile(own_ref, (f_ref, b_ref), invs, r, j)
            if j < blocks:
                mine_ref[pl.ds(r, TILE), j * LANES : (j + 1) * LANES] = v
            else:
                v_ref[pl.ds(r, TILE), (j - blocks) * LANES : (j - blocks + 1) * LANES] = v
                amax = jnp.maximum(amax, jnp.abs(v))
        return amax

    amax = for_tiles(own_ref.shape[0], body, jnp.zeros((TILE, LANES), F32))
    write_coded(v_ref, blocks, amax, out_ref)


def rows_kernel(h_ref, mine_ref, got_ref, out_ref):
    rows = mine_ref.shape[0]
    inv = inverse_scale(got_ref)
    mine_at, got_at = h_ref[0] * rows, (1 - h_ref[0]) * rows

    def body(r, x):
        out_ref[pl.ds(pl.multiple_of(mine_at + r, TILE), TILE), :] = mine_ref[pl.ds(r, TILE), :]
        for j in range(mine_ref.shape[1] // LANES):
            v = decode(got_ref[pl.ds(j * rows + r, TILE), :], inv)
            out_ref[pl.ds(pl.multiple_of(got_at + r, TILE), TILE), j * LANES : (j + 1) * LANES] = v
        return x

    for_tiles(rows, body, 0)


def whole(shape):
    return pl.BlockSpec(shape, lambda i, idx: (0,) * len(shape))


def call(kernel, idx, wholes, block, out_shapes, scratch=()):
    in_specs, args = [whole(a.shape) for a in wholes], list(wholes)
    if block is not None:
        in_specs.append(pl.BlockSpec((block[1], block[0].shape[1]), lambda i, idx: (idx[0], 0)))
        args.append(block[0])
    size = sum(a.size * 4 for a in args) + sum(s.size * 4 for s in out_shapes)
    return pl.pallas_call(
        kernel,
        grid_spec=pltpu.PrefetchScalarGridSpec(
            num_scalar_prefetch=1,
            grid=(1,),
            in_specs=in_specs,
            out_specs=[whole(s.shape) for s in out_shapes],
            scratch_shapes=[pltpu.VMEM(s, F32) for s in scratch],
        ),
        out_shape=out_shapes,
        compiler_params=pltpu.CompilerParams(vmem_limit_bytes=10 * MIB),
        cost_estimate=pl.CostEstimate(flops=size * 8, bytes_accessed=size, transcendentals=0),
    )(jnp.stack(idx).astype(jnp.int32), *args)


def placed_kernel(pieces, at_ref, *refs):
    srcs, out_ref, sems = refs[:-2], refs[-2], refs[-1]
    copies = []
    for i, (src, row, rows, col) in enumerate(pieces):
        ref = srcs[src]
        to = out_ref.at[pl.ds(pl.multiple_of(at_ref[i], LANES), rows), col : col + ref.shape[1]]
        copies.append(pltpu.make_async_copy(ref.at[row : row + rows], to, sems.at[i]))
    for copy in copies:
        copy.start()
    for copy in copies:
        copy.wait()


def placed(arrays, pieces, shape):
    fixed = [p[:4] for p in pieces]
    size = 2 * shape[0] * shape[1]
    return pl.pallas_call(
        functools.partial(placed_kernel, fixed),
        grid_spec=pltpu.PrefetchScalarGridSpec(
            num_scalar_prefetch=1,
            grid=(1,),
            in_specs=[pl.BlockSpec(memory_space=pltpu.VMEM)] * len(arrays),
            out_specs=pl.BlockSpec(memory_space=pltpu.VMEM),
            scratch_shapes=[pltpu.SemaphoreType.DMA((len(pieces),))],
        ),
        out_shape=jax.ShapeDtypeStruct(shape, BF16),
        compiler_params=pltpu.CompilerParams(vmem_limit_bytes=4 * MIB),
        cost_estimate=pl.CostEstimate(flops=0, bytes_accessed=2 * size, transcendentals=0),
    )(jnp.stack([jnp.int32(p[4]) for p in pieces]), *arrays)


def coded_shape(rows, width):
    return jax.ShapeDtypeStruct((width // LANES * rows + TILE, LANES), BF16)


def hop(got, mine):
    kernel = functools.partial(hop_kernel, len(got))
    return call(kernel, [jnp.int32(0)], got + [mine], None, [coded_shape(*mine.shape)], [mine.shape])[0]


def swap(a, axis):
    return lax.ppermute(a, axis, [(0, 1), (1, 0)])


def y_ring(a):
    perm = []
    for y in range(4):
        for c in range(2):
            t = (y + (1 if c == 0 else -1)) % 4
            perm.append((((y % 2) * 2 + y // 2) * 2 + c, ((t % 2) * 2 + t // 2) * 2 + c))
    return lax.ppermute(a, ("yl", "yh", "c"), perm)


def ring(a, axis, way):
    n = lax.axis_size(axis)
    perm = [(i * 2 + c, (i + (way if c == 0 else -way)) % n * 2 + c) for i in range(n) for c in range(2)]
    return lax.ppermute(a, (axis, "c"), perm)


def gathered(parts, axis, order, joint, hold=()):
    n, me = lax.axis_size(axis), lax.axis_index(axis)
    step = 1 - 2 * lax.axis_index("c")
    count, (rows, width) = len(parts), parts[0].shape
    blocks = {0: parts}
    ahead = back = parts
    for k in range(1, n // 2 + 1):
        if k == joint:
            ahead, back = [jnp.concatenate(ahead)], [jnp.concatenate(back)]
            hold = after(*ahead, *back, *hold)[2:]
        ahead = blocks[-k] = [ring(p, axis, 1) for p in ahead]
        if k < n - n // 2:
            back = blocks[k] = [ring(p, axis, -1) for p in back]
    arrays, pieces = [], []
    for k, got in blocks.items():
        at = lax.rem(me + step * k + n, n) * count
        for i, place in enumerate(order):
            src, row = (i, 0) if len(got) == count else (0, i * rows)
            pieces.append((len(arrays) + src, row, rows, 0, (at + place) * rows))
        arrays += got
    return arrays, pieces, (n * count * rows, width), hold


def outgoing(share, axis):
    n, me = lax.axis_size(axis), lax.axis_index(axis)
    step = 1 - 2 * lax.axis_index("c")
    ahead, back = n // 2, n - n // 2 - 1
    return hop([], share(lax.rem(me + step * ahead + n, n))), hop([], share(lax.rem(me - step * back + n, n)))


def scattered(share, axis, first):
    n, me = lax.axis_size(axis), lax.axis_index(axis)
    step = 1 - 2 * lax.axis_index("c")
    came = []
    for way, hops, got in ((1, n // 2, first[0]), (-1, n - n // 2 - 1, first[1])):
        got = ring(got, axis, way)
        for k in range(hops - 1, 0, -1):
            got = ring(hop([got], share(lax.rem(me + way * step * k + n, n))), axis, way)
        came.append(got)
    return came


def dot(a, b, dims):
    return lax.dot_general(a, b, (dims, ((), ())), preferred_element_type=F32)


def after(first, *rest):
    return lax.optimization_barrier((first,) + rest)


def on_device(activations, out_grad, weight):
    h = lax.axis_index("yl")
    c = lax.axis_index("c")
    tokens, width = out_grad.shape
    own_tokens, features = activations.shape
    rows = weight.shape[1]
    half = rows // 2
    owners = features // rows

    low = jnp.concatenate([activations[:, d * rows : d * rows + half] for d in range(owners)], axis=1)
    high = jnp.concatenate([activations[:, d * rows + half : (d + 1) * rows] for d in range(owners)], axis=1)
    acts_mine, acts_sent = jnp.where(h == 0, low, high), jnp.where(h == 0, high, low)
    acts_sent, acts_mine, weight, out_grad = after(acts_sent, acts_mine, weight, out_grad)
    acts_got = swap(acts_sent, "yl")

    w_mine = lax.dynamic_slice_in_dim(weight[0], h * half, half, 0)
    w_sent = lax.dynamic_slice_in_dim(weight[0], (1 - h) * half, half, 0)
    w_got = swap(w_sent, "yl")
    w_all = placed(*gathered([jnp.concatenate([w_mine, w_got], axis=1)], "x", (0,), 0)[:3])

    part = tokens // 2
    g_sent = lax.dynamic_slice_in_dim(out_grad, c * part, part, 0)
    hold = [y_ring(g_sent)]
    arrays, acts_pieces, shape, (g_got,) = gathered([acts_mine, acts_got], "z", (h, 1 - h), 3, hold)
    g_rest = swap(g_got, "c")
    pieces = [(0, 0, tokens, 0, 0), (1, 0, part, width, c * part), (2, 0, part, width, (1 - c) * part)]
    g_pair = placed([out_grad, g_got, g_rest], pieces, (tokens, 2 * width))

    def of_tokens(i):
        count = 2 * own_tokens
        return dot(lax.dynamic_slice_in_dim(g_pair, i * count, count, 0), w_all, ((1,), (1,)))

    first = outgoing(of_tokens, "z")
    acts_all = placed(after(*first, *arrays)[2:], acts_pieces, shape)
    came = scattered(of_tokens, "z", first)
    mine = of_tokens(lax.axis_index("z"))

    def finished(of):
        shape = jax.ShapeDtypeStruct((own_tokens, features // 2), BF16)
        return call(tokens_kernel, [of, of], came, (mine, own_tokens), [shape])[0]

    s_got = swap(finished(1 - h), "yl")
    shape = jax.ShapeDtypeStruct((own_tokens, features), BF16)
    input_grad = call(functools.partial(columns_kernel, half), [h], [finished(h), s_got], None, [shape])[0]

    def of_rows(i):
        acts = lax.dynamic_slice_in_dim(acts_all, i * half, half, 1)
        return dot(acts, g_pair, ((0,), (0,)))

    came = scattered(of_rows, "x", outgoing(of_rows, "x"))
    mine = of_rows(lax.axis_index("x"))
    shapes = [jax.ShapeDtypeStruct((half, width), F32), coded_shape(half, width)]
    owned, coded = call(owned_kernel, [jnp.int32(0)], came + [mine], None, shapes, [(half, width)])
    shape = jax.ShapeDtypeStruct((rows, width), F32)
    weight_grad = call(rows_kernel, [h], [owned, swap(coded, "yl")], None, [shape])[0]
    return input_grad, weight_grad[None]


def solution(mesh):
    dp, out, in_ = mesh.devices.shape
    fine = Mesh(mesh.devices.reshape(dp, out // 2, 2, 2, in_ // 2), ("x", "z", "yl", "yh", "c"))
    tokens, split = P(("x", "z", "yl"), ("yh", "c")), P(("yh", "c"), "x", ("z", "yl"))
    return jax.shard_map(
        on_device,
        mesh=fine,
        in_specs=(tokens, P("x", ("z", "yl")), split),
        out_specs=(tokens, split),
        check_vma=False,
    )
```

```python
import functools

import jax
import jax.numpy as jnp
from jax import lax
from jax.experimental import pallas as pl
from jax.experimental.pallas import tpu as pltpu
from jax.sharding import Mesh, PartitionSpec as P

F32 = jnp.float32
BF16 = jnp.bfloat16
LANES = 128
TILE = 16
SQUARINGS = 4
TOP = 2.0**7.75
TINY = 1e-30
MIB = 1024 * 1024


def encode(v, s):
    a = jnp.abs(v) * s
    for _ in range(SQUARINGS):
        a = a * a
    return jnp.where(v < 0, -a, a).astype(BF16)


def decode(y, inv):
    y = y.astype(F32)
    a = jnp.exp2(jnp.log2(jnp.abs(y)) * 0.5**SQUARINGS) * inv
    return jnp.where(y < 0, -a, a)


def inverse_scale(ref):
    return 1.0 / ref[ref.shape[0] - TILE :, :].astype(F32)


def for_tiles(rows, body, init):
    return lax.fori_loop(0, rows // TILE, lambda i, x: body(pl.multiple_of(i * TILE, TILE), x), init, unroll=2)


def write_coded(v_ref, blocks, amax, out_ref):
    rows = v_ref.shape[0]
    coded = (TOP / jnp.maximum(amax, TINY)).astype(BF16)
    s = coded.astype(F32)
    out_ref[blocks * rows :, :] = coded

    def body(r, x):
        for j in range(blocks):
            at = j * LANES
            out_ref[pl.ds(j * rows + r, TILE), :] = encode(v_ref[pl.ds(r, TILE), at : at + LANES], s)
        return x

    for_tiles(rows, body, 0)


def fetch(at_ref, own_ref, v_ref, sem):
    rows = pl.ds(pl.multiple_of(at_ref[0], LANES), v_ref.shape[0])
    copy = pltpu.make_async_copy(own_ref.at[rows], v_ref, sem)
    copy.start()
    copy.wait()


def summed_tile(v_ref, got, invs, r, j):
    rows = v_ref.shape[0]
    v = v_ref[pl.ds(r, TILE), j * LANES : (j + 1) * LANES]
    for ref, inv in zip(got, invs):
        v = v + decode(ref[pl.ds(j * rows + r, TILE), :], inv)
    return v


def hop_kernel(n_got, at_ref, *refs):
    got, (own_ref, out_ref, v_ref, sem) = refs[:n_got], refs[n_got:]
    blocks = v_ref.shape[1] // LANES
    invs = [inverse_scale(ref) for ref in got]
    fetch(at_ref, own_ref, v_ref, sem)

    def body(r, amax):
        for j in range(blocks):
            v = summed_tile(v_ref, got, invs, r, j)
            if got:
                v_ref[pl.ds(r, TILE), j * LANES : (j + 1) * LANES] = v
            amax = jnp.maximum(amax, jnp.abs(v))
        return amax

    amax = for_tiles(v_ref.shape[0], body, jnp.zeros((TILE, LANES), F32))
    write_coded(v_ref, blocks, amax, out_ref)


def tokens_kernel(at_ref, f_ref, b_ref, own_ref, out_ref, v_ref, sem):
    invs = [inverse_scale(f_ref), inverse_scale(b_ref)]
    rows = out_ref.shape[0]
    fetch(at_ref, own_ref, v_ref, sem)

    def body(r, x):
        for j in range(v_ref.shape[1] // LANES):
            v = v_ref[pl.ds(r, TILE), j * LANES : (j + 1) * LANES]
            for ref, inv in zip((f_ref, b_ref), invs):
                row = pl.multiple_of(j * 2 * rows + at_ref[1] + r, TILE)
                v = v + decode(ref[pl.ds(row, TILE), :], inv)
            out_ref[pl.ds(r, TILE), j * LANES : (j + 1) * LANES] = v.astype(BF16)
        return x

    for_tiles(rows, body, 0)


def columns_kernel(half, h_ref, mine_ref, got_ref, out_ref):
    for j in range(mine_ref.shape[1] // half):
        at = slice(j * half, (j + 1) * half)
        mine_at = pl.multiple_of((2 * j + h_ref[0]) * half, LANES)
        got_at = pl.multiple_of((2 * j + 1 - h_ref[0]) * half, LANES)
        out_ref[:, pl.ds(mine_at, half)] = mine_ref[:, at]
        out_ref[:, pl.ds(got_at, half)] = got_ref[:, at]


def owned_kernel(at_ref, f_ref, b_ref, own_ref, mine_ref, out_ref, v_ref, sem):
    invs = [inverse_scale(f_ref), inverse_scale(b_ref)]
    blocks = v_ref.shape[1] // LANES
    kept = blocks // 2
    fetch(at_ref, own_ref, v_ref, sem)

    def body(r, amax):
        for j in range(blocks):
            v = summed_tile(v_ref, (f_ref, b_ref), invs, r, j)
            if j < kept:
                mine_ref[pl.ds(r, TILE), j * LANES : (j + 1) * LANES] = v
            else:
                v_ref[pl.ds(r, TILE), (j - kept) * LANES : (j - kept + 1) * LANES] = v
                amax = jnp.maximum(amax, jnp.abs(v))
        return amax

    amax = for_tiles(v_ref.shape[0], body, jnp.zeros((TILE, LANES), F32))
    write_coded(v_ref, blocks - kept, amax, out_ref)


def rows_kernel(h_ref, mine_ref, got_ref, out_ref):
    rows = mine_ref.shape[0]
    inv = inverse_scale(got_ref)
    mine_at, got_at = h_ref[0] * rows, (1 - h_ref[0]) * rows

    def body(r, x):
        out_ref[pl.ds(pl.multiple_of(mine_at + r, TILE), TILE), :] = mine_ref[pl.ds(r, TILE), :]
        for j in range(mine_ref.shape[1] // LANES):
            v = decode(got_ref[pl.ds(j * rows + r, TILE), :], inv)
            out_ref[pl.ds(pl.multiple_of(got_at + r, TILE), TILE), j * LANES : (j + 1) * LANES] = v
        return x

    for_tiles(rows, body, 0)


def whole(shape):
    return pl.BlockSpec(shape, lambda i, idx: (0,) * len(shape))


def call(kernel, at, wholes, own, out_shapes, rows=0):
    in_specs, args, scratch = [whole(a.shape) for a in wholes], list(wholes), []
    if own is not None:
        in_specs.append(pl.BlockSpec(memory_space=pl.ANY))
        args.append(own)
        scratch = [pltpu.VMEM((rows, own.shape[1]), F32), pltpu.SemaphoreType.DMA]
    size = sum(a.size * 4 for a in wholes) + sum(s.size * 4 for s in out_shapes)
    return pl.pallas_call(
        kernel,
        grid_spec=pltpu.PrefetchScalarGridSpec(
            num_scalar_prefetch=1,
            grid=(1,),
            in_specs=in_specs,
            out_specs=[whole(s.shape) for s in out_shapes],
            scratch_shapes=scratch,
        ),
        out_shape=out_shapes,
        compiler_params=pltpu.CompilerParams(vmem_limit_bytes=10 * MIB),
        cost_estimate=pl.CostEstimate(flops=size * 8, bytes_accessed=size, transcendentals=0),
    )(jnp.stack([jnp.int32(i) for i in at]), *args)


def placed_kernel(pieces, at_ref, *refs):
    srcs, out_ref, sems = refs[:-2], refs[-2], refs[-1]

    def place(i, j, size):
        fixed = pieces[i][1 + j]
        if fixed is None:
            fixed = pl.multiple_of(at_ref[i], LANES)
        return pl.ds(fixed, size)

    copies = []
    for i, (src, _, _, _, _, rows, cols) in enumerate(pieces):
        here = srcs[src].at[place(i, 0, rows), place(i, 1, cols)]
        there = out_ref.at[place(i, 2, rows), place(i, 3, cols)]
        copies.append(pltpu.make_async_copy(here, there, sems.at[i]))
    for copy in copies:
        copy.start()
    for copy in copies:
        copy.wait()


def placed(arrays, pieces, shape, space=pltpu.VMEM):
    known = [tuple(None if isinstance(p, jax.Array) else p for p in piece) for piece in pieces]
    at = [next((p for p in piece if isinstance(p, jax.Array)), jnp.int32(0)) for piece in pieces]
    size = 2 * shape[0] * shape[1]
    return pl.pallas_call(
        functools.partial(placed_kernel, known),
        grid_spec=pltpu.PrefetchScalarGridSpec(
            num_scalar_prefetch=1,
            grid=(1,),
            in_specs=[pl.BlockSpec(memory_space=space)] * len(arrays),
            out_specs=pl.BlockSpec(memory_space=pltpu.VMEM),
            scratch_shapes=[pltpu.SemaphoreType.DMA((len(pieces),))],
        ),
        out_shape=jax.ShapeDtypeStruct(shape, BF16),
        compiler_params=pltpu.CompilerParams(vmem_limit_bytes=4 * MIB),
        cost_estimate=pl.CostEstimate(flops=0, bytes_accessed=2 * size, transcendentals=0),
    )(jnp.stack(at), *arrays)


def coded_shape(rows, width):
    return jax.ShapeDtypeStruct((width // LANES * rows + TILE, LANES), BF16)


def hop(got, shares, at, rows):
    shape = (rows, shares.shape[1])
    return call(functools.partial(hop_kernel, len(got)), [at], got, shares, [coded_shape(*shape)], rows)[0]


def swap(a, axis):
    return lax.ppermute(a, axis, [(0, 1), (1, 0)])


def y_ring(a):
    perm = []
    for y in range(4):
        for c in range(2):
            t = (y + (1 if c == 0 else -1)) % 4
            perm.append((((y % 2) * 2 + y // 2) * 2 + c, ((t % 2) * 2 + t // 2) * 2 + c))
    return lax.ppermute(a, ("yl", "yh", "c"), perm)


def ring(a, axis, way):
    n = lax.axis_size(axis)
    perm = [(i * 2 + c, (i + (way if c == 0 else -way)) % n * 2 + c) for i in range(n) for c in range(2)]
    return lax.ppermute(a, (axis, "c"), perm)


def block_at(axis, k):
    n = lax.axis_size(axis)
    return lax.rem(lax.axis_index(axis) + (1 - 2 * lax.axis_index("c")) * k + n, n)


def around(parts, axis, joint, before):
    n = lax.axis_size(axis)
    blocks = {0: parts}
    ahead = back = parts
    for k in range(1, n // 2 + 1):
        if k == joint:
            ahead, back = [jnp.concatenate(ahead)], [jnp.concatenate(back)]
        for held in before.get(k, []):
            *ahead, held = after(*ahead, held)
            *back, held = after(*back, held)
        ahead = blocks[-k] = [ring(p, axis, 1) for p in ahead]
        if k < n - n // 2:
            back = blocks[k] = [ring(p, axis, -1) for p in back]
    return blocks


def scattered(share, axis, first):
    n = lax.axis_size(axis)
    came = []
    for way, hops, got in ((1, n // 2, first[0]), (-1, n - n // 2 - 1, first[1])):
        got = ring(got, axis, way)
        for k in range(hops - 1, 0, -1):
            got = ring(share([got], way * k), axis, way)
        came.append(got)
    return came


def dot_kernel(dims, a_ref, b_ref, out_ref):
    out_ref[...] = lax.dot_general(a_ref[...], b_ref[...], (dims, ((), ())), preferred_element_type=F32)


def blocked_dot(a, block, at, count, b, dims):
    rows, cols = block[1 - dims[0][0]], b.shape[1 - dims[1][0]]
    along = [i for i in range(2) if i != dims[0][0]][0]
    size = 2 * count * block[0] * block[1] + 2 * b.size + 4 * count * rows * cols
    return pl.pallas_call(
        functools.partial(dot_kernel, dims),
        grid=(count,),
        in_specs=[
            pl.BlockSpec(block, lambda i: (at + i, 0) if along == 0 else (0, at + i)),
            pl.BlockSpec(memory_space=pltpu.VMEM),
        ],
        out_specs=pl.BlockSpec((rows, cols), lambda i: (i, 0)),
        out_shape=jax.ShapeDtypeStruct((count * rows, cols), F32),
        compiler_params=pltpu.CompilerParams(vmem_limit_bytes=16 * MIB),
        cost_estimate=pl.CostEstimate(
            flops=2 * count * rows * cols * block[dims[0][0]], bytes_accessed=size, transcendentals=0
        ),
    )(a, b)


def after(first, *rest):
    return lax.optimization_barrier((first,) + rest)


def on_device(activations, out_grad, weight):
    h = lax.axis_index("yl")
    c = lax.axis_index("c")
    tokens, width = out_grad.shape
    own_tokens, features = activations.shape
    rows = weight.shape[1]
    half = rows // 2
    owners = features // rows

    def acts_half(i):
        return [(0, 0, (2 * d + i) * half, 0, d * half, own_tokens, half) for d in range(owners)]

    weight = weight[0]
    split = features // 2
    cuts = half // own_tokens
    pieces = acts_half(1 - h)
    for j in range(cuts):
        pieces.append((1, (1 - h) * half + j * own_tokens, 0, 0, split + j * width, own_tokens, width))
    sent = placed([activations, weight], pieces, (own_tokens, split + cuts * width), pltpu.HBM)
    acts_mine = placed([activations], acts_half(h), (own_tokens, split), pltpu.HBM)
    sent, acts_mine, weight, out_grad = after(sent, acts_mine, weight, out_grad)
    got = swap(sent, "yl")

    w_mine = placed([weight], [(0, h * half, 0, 0, 0, half, width)], (half, width), pltpu.HBM)
    w_own = around([w_mine], "x", 0, {})
    acts_ahead = ring(acts_mine, "z", 1)
    acts_back = ring(acts_mine, "z", -1)
    blocks = {0: [acts_mine], -1: [acts_ahead], 1: [acts_back]}
    acts_ahead, acts_back = ring(acts_ahead, "z", 1), ring(acts_back, "z", -1)
    blocks[-2], blocks[2] = [acts_ahead], [acts_back]
    got = after(acts_ahead, acts_back, w_own[-1][0], w_own[1][0], got)[-1]

    pieces = [(0, 0, split + j * width, j * own_tokens, 0, own_tokens, width) for j in range(cuts)]
    w_other = around([placed([got], pieces, (half, width))], "x", 0, {})
    acts_got = got[:, :split]
    other_ahead, other_back = ring(acts_got, "z", 1), ring(acts_got, "z", -1)
    blocks[0], blocks[-1], blocks[1] = (blocks[k] + [p] for k, p in ((0, acts_got), (-1, other_ahead), (1, other_back)))
    other_ahead, other_back, *held = after(other_ahead, other_back, w_own[-2][0])
    other_ahead, other_back = ring(other_ahead, "z", 1), ring(other_back, "z", -1)
    blocks[-2], blocks[2] = blocks[-2] + [other_ahead], blocks[2] + [other_back]
    ahead, back = jnp.concatenate(blocks[-2]), jnp.concatenate(blocks[2])

    part = tokens // 2
    g_sent = after(acts_got, out_grad)[1]
    g_got = y_ring(placed([g_sent], [(0, c * part, 0, 0, 0, part, width)], (part, width), pltpu.HBM))
    g_got = after(ahead, back, w_other[-1][0], w_other[1][0], g_got)[-1]
    g_rest = swap(g_got, "c")

    ahead, back, *held = after(ahead, back, w_other[-1][0], w_other[1][0])
    ahead, back = ring(ahead, "z", 1), ring(back, "z", -1)
    blocks[-3], blocks[3] = [ahead], [back]
    blocks[-4] = [ring(after(w_other[-2][0], ahead)[-1], "z", 1)]

    arrays, pieces = [], []
    for col, of in ((0, w_own), (width, w_other)):
        for k, (block,) in of.items():
            pieces.append((len(arrays), 0, 0, block_at("x", k) * half, col, half, width))
            arrays.append(block)
    w_all = placed(arrays, pieces, (owners * half, 2 * width))

    count = 2 * own_tokens
    order = [4, -3, 3, -2, 2, -1, 1, 0]
    pieces = []
    for i, k in enumerate(order):
        at = block_at("z", k) * count
        pieces.append((0, at, 0, i * count, 0, count, width))
    other = placed([g_got, g_rest], [(0, 0, 0, c * part, 0, part, width), (1, 0, 0, (1 - c) * part, 0, part, width)], (tokens, width))
    for i, k in enumerate(order):
        at = block_at("z", k) * count
        pieces.append((1, at, 0, i * count, width, count, width))
    g_pair = placed([out_grad, other], pieces, (tokens, 2 * width))

    block = (count, 2 * width)
    shares = [blocked_dot(g_pair, block, at, n, w_all, ((1,), (1,))) for at, n in ((0, 2), (2, len(order) - 2))]

    def of_tokens(got, k):
        i = order.index(k)
        return hop(got, shares[i >= 2], (i - 2 * (i >= 2)) * count, count)

    first = [of_tokens([], k) for k in order[:2]]
    came = scattered(of_tokens, "z", first)

    def finished(of):
        shape = jax.ShapeDtypeStruct((own_tokens, split), BF16)
        at = [(order.index(0) - 2) * count + of * own_tokens, of * own_tokens]
        return call(tokens_kernel, at, came, shares[1], [shape], own_tokens)[0]

    s_got = swap(finished(1 - h), "yl")
    shape = jax.ShapeDtypeStruct((own_tokens, features), BF16)
    input_grad = call(functools.partial(columns_kernel, half), [h], [finished(h), s_got], None, [shape])[0]

    arrays, pieces = [], []
    for k, parts in blocks.items():
        at = order.index(k if k != -4 else 4) * count
        for i, place in enumerate((h, 1 - h)):
            src, row = (i, 0) if len(parts) == 2 else (0, i * own_tokens)
            pieces.append((len(arrays) + src, row, 0, at + place * own_tokens, 0, own_tokens, split))
        arrays += parts
    acts_all = placed(after(*first, *arrays)[2:], pieces, (tokens, split))
    folded = blocked_dot(acts_all, (tokens, half), 0, owners, g_pair, ((0,), (0,)))

    def of_rows(got, k):
        return hop(got, folded, block_at("x", k) * half, half)

    came = scattered(of_rows, "x", [of_rows([], 2), of_rows([], -1)])
    shapes = [jax.ShapeDtypeStruct((half, width), F32), coded_shape(half, width)]
    owned, coded = call(owned_kernel, [block_at("x", 0) * half], came, folded, shapes, half)
    shape = jax.ShapeDtypeStruct((rows, width), F32)
    weight_grad = call(rows_kernel, [h], [owned, swap(coded, "yl")], None, [shape])[0]
    return input_grad, weight_grad[None]


def solution(mesh):
    dp, out, in_ = mesh.devices.shape
    fine = Mesh(mesh.devices.reshape(dp, out // 2, 2, 2, in_ // 2), ("x", "z", "yl", "yh", "c"))
    tokens, split = P(("x", "z", "yl"), ("yh", "c")), P(("yh", "c"), "x", ("z", "yl"))
    return jax.shard_map(
        on_device,
        mesh=fine,
        in_specs=(tokens, P("x", ("z", "yl")), split),
        out_specs=(tokens, split),
        check_vma=False,
    )
```

```python
import functools

import jax
import jax.numpy as jnp
from jax import lax
from jax.experimental import pallas as pl
from jax.experimental.pallas import tpu as pltpu
from jax.sharding import Mesh, PartitionSpec as P

F32 = jnp.float32
BF16 = jnp.bfloat16
LANES = 128
TILE = 16
SQUARINGS = 4
TOP = 2.0**7.75
TINY = 1e-30
MIB = 1024 * 1024


def encode(v, s):
    a = jnp.abs(v) * s
    for _ in range(SQUARINGS):
        a = a * a
    return jnp.where(v < 0, -a, a).astype(BF16)


def decode(y, inv):
    y = y.astype(F32)
    a = jnp.exp2(jnp.log2(jnp.abs(y)) * 0.5**SQUARINGS) * inv
    return jnp.where(y < 0, -a, a)


def inverse_scale(ref):
    return 1.0 / ref[ref.shape[0] - TILE :, :].astype(F32)


def for_tiles(rows, body, init):
    return lax.fori_loop(0, rows // TILE, lambda i, x: body(pl.multiple_of(i * TILE, TILE), x), init, unroll=2)


def write_coded(v_ref, blocks, amax, out_ref):
    rows = v_ref.shape[0]
    coded = (TOP / jnp.maximum(amax, TINY)).astype(BF16)
    s = coded.astype(F32)
    out_ref[blocks * rows :, :] = coded

    def body(r, x):
        for j in range(blocks):
            at = j * LANES
            out_ref[pl.ds(j * rows + r, TILE), :] = encode(v_ref[pl.ds(r, TILE), at : at + LANES], s)
        return x

    for_tiles(rows, body, 0)


def summed_tile(own_ref, got, invs, r, j):
    rows = own_ref.shape[0]
    v = own_ref[pl.ds(r, TILE), j * LANES : (j + 1) * LANES]
    for ref, inv in zip(got, invs):
        v = v + decode(ref[pl.ds(j * rows + r, TILE), :], inv)
    return v


def hop_kernel(n_got, idx_ref, *refs):
    got, (own_ref, out_ref, v_ref) = refs[:n_got], refs[n_got:]
    blocks = v_ref.shape[1] // LANES
    invs = [inverse_scale(ref) for ref in got]

    def body(r, amax):
        for j in range(blocks):
            v = summed_tile(own_ref, got, invs, r, j)
            v_ref[pl.ds(r, TILE), j * LANES : (j + 1) * LANES] = v
            amax = jnp.maximum(amax, jnp.abs(v))
        return amax

    amax = for_tiles(v_ref.shape[0], body, jnp.zeros((TILE, LANES), F32))
    write_coded(v_ref, blocks, amax, out_ref)


def tokens_kernel(idx_ref, f_ref, b_ref, own_ref, out_ref):
    invs = [inverse_scale(f_ref), inverse_scale(b_ref)]
    rows = out_ref.shape[0]
    at = idx_ref[1] * rows

    def body(r, x):
        for j in range(own_ref.shape[1] // LANES):
            v = own_ref[pl.ds(r, TILE), j * LANES : (j + 1) * LANES]
            for ref, inv in zip((f_ref, b_ref), invs):
                row = pl.multiple_of(j * 2 * rows + at + r, TILE)
                v = v + decode(ref[pl.ds(row, TILE), :], inv)
            out_ref[pl.ds(r, TILE), j * LANES : (j + 1) * LANES] = v.astype(BF16)
        return x

    for_tiles(rows, body, 0)


def columns_kernel(half, h_ref, mine_ref, got_ref, out_ref):
    for j in range(mine_ref.shape[1] // half):
        at = slice(j * half, (j + 1) * half)
        mine_at = pl.multiple_of((2 * j + h_ref[0]) * half, LANES)
        got_at = pl.multiple_of((2 * j + 1 - h_ref[0]) * half, LANES)
        out_ref[:, pl.ds(mine_at, half)] = mine_ref[:, at]
        out_ref[:, pl.ds(got_at, half)] = got_ref[:, at]


def owned_kernel(idx_ref, f_ref, b_ref, own_ref, mine_ref, out_ref, v_ref):
    invs = [inverse_scale(f_ref), inverse_scale(b_ref)]
    blocks = v_ref.shape[1] // LANES

    def body(r, amax):
        for j in range(2 * blocks):
            v = summed_tile(own_ref, (f_ref, b_ref), invs, r, j)
            if j < blocks:
                mine_ref[pl.ds(r, TILE), j * LANES : (j + 1) * LANES] = v
            else:
                v_ref[pl.ds(r, TILE), (j - blocks) * LANES : (j - blocks + 1) * LANES] = v
                amax = jnp.maximum(amax, jnp.abs(v))
        return amax

    amax = for_tiles(own_ref.shape[0], body, jnp.zeros((TILE, LANES), F32))
    write_coded(v_ref, blocks, amax, out_ref)


def rows_kernel(h_ref, mine_ref, got_ref, out_ref):
    rows = mine_ref.shape[0]
    inv = inverse_scale(got_ref)
    mine_at, got_at = h_ref[0] * rows, (1 - h_ref[0]) * rows

    def body(r, x):
        out_ref[pl.ds(pl.multiple_of(mine_at + r, TILE), TILE), :] = mine_ref[pl.ds(r, TILE), :]
        for j in range(mine_ref.shape[1] // LANES):
            v = decode(got_ref[pl.ds(j * rows + r, TILE), :], inv)
            out_ref[pl.ds(pl.multiple_of(got_at + r, TILE), TILE), j * LANES : (j + 1) * LANES] = v
        return x

    for_tiles(rows, body, 0)


def whole(shape):
    return pl.BlockSpec(shape, lambda i, idx: (0,) * len(shape))


def call(kernel, idx, wholes, block, out_shapes, scratch=()):
    in_specs, args = [whole(a.shape) for a in wholes], list(wholes)
    if block is not None:
        in_specs.append(pl.BlockSpec((block[1], block[0].shape[1]), lambda i, idx: (idx[0], 0)))
        args.append(block[0])
    size = sum(a.size * 4 for a in args) + sum(s.size * 4 for s in out_shapes)
    return pl.pallas_call(
        kernel,
        grid_spec=pltpu.PrefetchScalarGridSpec(
            num_scalar_prefetch=1,
            grid=(1,),
            in_specs=in_specs,
            out_specs=[whole(s.shape) for s in out_shapes],
            scratch_shapes=[pltpu.VMEM(s, F32) for s in scratch],
        ),
        out_shape=out_shapes,
        compiler_params=pltpu.CompilerParams(vmem_limit_bytes=10 * MIB),
        cost_estimate=pl.CostEstimate(flops=size * 8, bytes_accessed=size, transcendentals=0),
    )(jnp.stack(idx).astype(jnp.int32), *args)


def placed_kernel(pieces, at_ref, *refs):
    srcs, out_ref, sems = refs[:-2], refs[-2], refs[-1]
    copies = []
    for i, (src, row, rows, col) in enumerate(pieces):
        ref = srcs[src]
        to = out_ref.at[pl.ds(pl.multiple_of(at_ref[i], LANES), rows), col : col + ref.shape[1]]
        copies.append(pltpu.make_async_copy(ref.at[row : row + rows], to, sems.at[i]))
    for copy in copies:
        copy.start()
    for copy in copies:
        copy.wait()


def placed(arrays, pieces, shape):
    fixed = [p[:4] for p in pieces]
    size = 2 * shape[0] * shape[1]
    return pl.pallas_call(
        functools.partial(placed_kernel, fixed),
        grid_spec=pltpu.PrefetchScalarGridSpec(
            num_scalar_prefetch=1,
            grid=(1,),
            in_specs=[pl.BlockSpec(memory_space=pltpu.VMEM)] * len(arrays),
            out_specs=pl.BlockSpec(memory_space=pltpu.VMEM),
            scratch_shapes=[pltpu.SemaphoreType.DMA((len(pieces),))],
        ),
        out_shape=jax.ShapeDtypeStruct(shape, BF16),
        compiler_params=pltpu.CompilerParams(vmem_limit_bytes=4 * MIB),
        cost_estimate=pl.CostEstimate(flops=0, bytes_accessed=2 * size, transcendentals=0),
    )(jnp.stack([jnp.int32(p[4]) for p in pieces]), *arrays)


def coded_shape(rows, width):
    return jax.ShapeDtypeStruct((width // LANES * rows + TILE, LANES), BF16)


def hop(got, mine):
    kernel = functools.partial(hop_kernel, len(got))
    return call(kernel, [jnp.int32(0)], got + [mine], None, [coded_shape(*mine.shape)], [mine.shape])[0]


def swap(a, axis):
    return lax.ppermute(a, axis, [(0, 1), (1, 0)])


def y_ring(a):
    perm = []
    for y in range(4):
        for c in range(2):
            t = (y + (1 if c == 0 else -1)) % 4
            perm.append((((y % 2) * 2 + y // 2) * 2 + c, ((t % 2) * 2 + t // 2) * 2 + c))
    return lax.ppermute(a, ("yl", "yh", "c"), perm)


def ring(a, axis, way):
    n = lax.axis_size(axis)
    perm = [(i * 2 + c, (i + (way if c == 0 else -way)) % n * 2 + c) for i in range(n) for c in range(2)]
    return lax.ppermute(a, (axis, "c"), perm)


def gathered(parts, axis, order, joint, before, out=()):
    n, me = lax.axis_size(axis), lax.axis_index(axis)
    step = 1 - 2 * lax.axis_index("c")
    count, (rows, width) = len(parts), parts[0].shape
    blocks = {0: parts}
    ahead = back = parts
    for k in range(1, n // 2 + 1):
        if k == joint:
            ahead, back = [jnp.concatenate(ahead)], [jnp.concatenate(back)]
        if k in before:
            ahead, back, *_ = after(*ahead, *back, *before[k])
            ahead, back = [ahead], [back]
        if k == 1 and count == 2:
            ahead, back = blocks[-1], blocks[1] = [[f, ring(parts[1], axis, w)] for f, w in zip(out, (1, -1))]
            continue
        ahead = blocks[-k] = [ring(p, axis, 1) for p in ahead]
        if k < n - n // 2:
            back = blocks[k] = [ring(p, axis, -1) for p in back]
    arrays, pieces = [], []
    for k, got in blocks.items():
        at = lax.rem(me + step * k + n, n) * count
        for i, place in enumerate(order):
            src, row = (i, 0) if len(got) == count else (0, i * rows)
            pieces.append((len(arrays) + src, row, rows, 0, (at + place) * rows))
        arrays += got
    return arrays, pieces, (n * count * rows, width), blocks


def outgoing(share, axis):
    n, me = lax.axis_size(axis), lax.axis_index(axis)
    step = 1 - 2 * lax.axis_index("c")
    ahead, back = n // 2, n - n // 2 - 1
    return hop([], share(lax.rem(me + step * ahead + n, n))), hop([], share(lax.rem(me - step * back + n, n)))


def scattered(share, axis, first):
    n, me = lax.axis_size(axis), lax.axis_index(axis)
    step = 1 - 2 * lax.axis_index("c")
    came = []
    for way, hops, got in ((1, n // 2, first[0]), (-1, n - n // 2 - 1, first[1])):
        got = ring(got, axis, way)
        for k in range(hops - 1, 0, -1):
            got = ring(hop([got], share(lax.rem(me + way * step * k + n, n))), axis, way)
        came.append(got)
    return came


def dot(a, b, dims):
    return lax.dot_general(a, b, (dims, ((), ())), preferred_element_type=F32)


def after(first, *rest):
    return lax.optimization_barrier((first,) + rest)


def on_device(activations, out_grad, weight):
    h = lax.axis_index("yl")
    c = lax.axis_index("c")
    tokens, width = out_grad.shape
    own_tokens, features = activations.shape
    rows = weight.shape[1]
    half = rows // 2
    owners = features // rows

    low = jnp.concatenate([activations[:, d * rows : d * rows + half] for d in range(owners)], axis=1)
    high = jnp.concatenate([activations[:, d * rows + half : (d + 1) * rows] for d in range(owners)], axis=1)
    acts_mine, acts_sent = jnp.where(h == 0, low, high), jnp.where(h == 0, high, low)
    acts_sent, acts_mine, weight, out_grad = after(acts_sent, acts_mine, weight, out_grad)
    acts_got = swap(acts_sent, "yl")

    w_mine = lax.dynamic_slice_in_dim(weight[0], h * half, half, 0)
    w_sent = lax.dynamic_slice_in_dim(weight[0], (1 - h) * half, half, 0)
    out = [ring(acts_mine, "z", 1), ring(acts_mine, "z", -1)]
    *_, acts_got, w_got = after(*out, acts_got, swap(w_sent, "yl"))
    arrays, pieces, shape, blocks = gathered([jnp.concatenate([w_mine, w_got], axis=1)], "x", (0,), 0, {2: []})
    w_all = placed(arrays, pieces, shape)

    before = {2: [w_got], 3: [blocks[-1][0], blocks[1][0]]}
    arrays, acts_pieces, shape, blocks = gathered([acts_mine, acts_got], "z", (h, 1 - h), 2, before, out)

    part = tokens // 2
    g_sent = lax.dynamic_slice_in_dim(out_grad, c * part, part, 0)
    g_sent = after(acts_got, w_got, g_sent)[2]
    g_got = after(*blocks[-2], *blocks[2], y_ring(g_sent))[-1]
    g_rest = swap(g_got, "c")
    pieces = [(0, 0, tokens, 0, 0), (1, 0, part, width, c * part), (2, 0, part, width, (1 - c) * part)]
    g_pair = placed([out_grad, g_got, g_rest], pieces, (tokens, 2 * width))

    def of_tokens(i):
        count = 2 * own_tokens
        return dot(lax.dynamic_slice_in_dim(g_pair, i * count, count, 0), w_all, ((1,), (1,)))

    first = outgoing(of_tokens, "z")
    acts_all = placed(after(*first, *arrays)[2:], acts_pieces, shape)
    came = scattered(of_tokens, "z", first)
    mine = of_tokens(lax.axis_index("z"))

    def finished(of):
        shape = jax.ShapeDtypeStruct((own_tokens, features // 2), BF16)
        return call(tokens_kernel, [of, of], came, (mine, own_tokens), [shape])[0]

    s_got = swap(finished(1 - h), "yl")
    shape = jax.ShapeDtypeStruct((own_tokens, features), BF16)
    input_grad = call(functools.partial(columns_kernel, half), [h], [finished(h), s_got], None, [shape])[0]

    def of_rows(i):
        acts = lax.dynamic_slice_in_dim(acts_all, i * half, half, 1)
        return dot(acts, g_pair, ((0,), (0,)))

    came = scattered(of_rows, "x", outgoing(of_rows, "x"))
    mine = of_rows(lax.axis_index("x"))
    shapes = [jax.ShapeDtypeStruct((half, width), F32), coded_shape(half, width)]
    owned, coded = call(owned_kernel, [jnp.int32(0)], came + [mine], None, shapes, [(half, width)])
    shape = jax.ShapeDtypeStruct((rows, width), F32)
    weight_grad = call(rows_kernel, [h], [owned, swap(coded, "yl")], None, [shape])[0]
    return input_grad, weight_grad[None]


def solution(mesh):
    dp, out, in_ = mesh.devices.shape
    fine = Mesh(mesh.devices.reshape(dp, out // 2, 2, 2, in_ // 2), ("x", "z", "yl", "yh", "c"))
    tokens, split = P(("x", "z", "yl"), ("yh", "c")), P(("yh", "c"), "x", ("z", "yl"))
    return jax.shard_map(
        on_device,
        mesh=fine,
        in_specs=(tokens, P("x", ("z", "yl")), split),
        out_specs=(tokens, split),
        check_vma=False,
    )
```

```python
import functools

import jax
import jax.numpy as jnp
from jax import lax
from jax.experimental import pallas as pl
from jax.experimental.pallas import tpu as pltpu
from jax.sharding import Mesh, PartitionSpec as P

F32 = jnp.float32
BF16 = jnp.bfloat16
LANES = 128
TILE = 16
SQUARINGS = 4
TOP = 2.0**7.75
TINY = 1e-30
MIB = 1024 * 1024


def encode(v, s):
    a = jnp.abs(v) * s
    for _ in range(SQUARINGS):
        a = a * a
    return jnp.where(v < 0, -a, a).astype(BF16)


def decode(y, inv):
    y = y.astype(F32)
    a = jnp.exp2(jnp.log2(jnp.abs(y)) * 0.5**SQUARINGS) * inv
    return jnp.where(y < 0, -a, a)


def inverse_scale(ref):
    return 1.0 / ref[ref.shape[0] - TILE :, :].astype(F32)


def for_tiles(rows, body, init):
    return lax.fori_loop(0, rows // TILE, lambda i, x: body(pl.multiple_of(i * TILE, TILE), x), init, unroll=2)


def write_coded(v_ref, blocks, amax, out_ref):
    rows = v_ref.shape[0]
    coded = (TOP / jnp.maximum(amax, TINY)).astype(BF16)
    s = coded.astype(F32)
    out_ref[blocks * rows :, :] = coded

    def body(r, x):
        for j in range(blocks):
            at = j * LANES
            out_ref[pl.ds(j * rows + r, TILE), :] = encode(v_ref[pl.ds(r, TILE), at : at + LANES], s)
        return x

    for_tiles(rows, body, 0)


def summed_tile(own_ref, got, invs, r, j):
    rows = own_ref.shape[0]
    v = own_ref[pl.ds(r, TILE), j * LANES : (j + 1) * LANES]
    for ref, inv in zip(got, invs):
        v = v + decode(ref[pl.ds(j * rows + r, TILE), :], inv)
    return v


def hop_kernel(n_got, idx_ref, *refs):
    got, (own_ref, out_ref, v_ref) = refs[:n_got], refs[n_got:]
    blocks = v_ref.shape[1] // LANES
    invs = [inverse_scale(ref) for ref in got]

    def body(r, amax):
        for j in range(blocks):
            v = summed_tile(own_ref, got, invs, r, j)
            v_ref[pl.ds(r, TILE), j * LANES : (j + 1) * LANES] = v
            amax = jnp.maximum(amax, jnp.abs(v))
        return amax

    amax = for_tiles(v_ref.shape[0], body, jnp.zeros((TILE, LANES), F32))
    write_coded(v_ref, blocks, amax, out_ref)


def tokens_kernel(idx_ref, f_ref, b_ref, own_ref, out_ref):
    invs = [inverse_scale(f_ref), inverse_scale(b_ref)]
    rows = out_ref.shape[0]
    at = idx_ref[1] * rows

    def body(r, x):
        for j in range(own_ref.shape[1] // LANES):
            v = own_ref[pl.ds(r, TILE), j * LANES : (j + 1) * LANES]
            for ref, inv in zip((f_ref, b_ref), invs):
                row = pl.multiple_of(j * 2 * rows + at + r, TILE)
                v = v + decode(ref[pl.ds(row, TILE), :], inv)
            out_ref[pl.ds(r, TILE), j * LANES : (j + 1) * LANES] = v.astype(BF16)
        return x

    for_tiles(rows, body, 0)


def columns_kernel(half, at_ref, mine_ref, got_ref, out_ref):
    for j in range(mine_ref.shape[1] // half):
        at = slice(j * half, (j + 1) * half)
        mine_at = pl.multiple_of((2 * at_ref[1 + j] + at_ref[0]) * half, LANES)
        got_at = pl.multiple_of((2 * at_ref[1 + j] + 1 - at_ref[0]) * half, LANES)
        out_ref[:, pl.ds(mine_at, half)] = mine_ref[:, at]
        out_ref[:, pl.ds(got_at, half)] = got_ref[:, at]


def first_kernel(at_ref, own_ref, got_ref, rest_ref, *refs):
    ws, (out_ref, other_ref, v_ref) = refs[:-3], refs[-3:]
    width, half = own_ref.shape[1], ws[0].shape[0]

    @pl.when(at_ref[2] == 1)
    def _():
        other_ref[...] = got_ref[...]

    @pl.when(at_ref[2] != 1)
    def _():
        other_ref[...] = rest_ref[...]

    for j, w in enumerate(ws):
        v_ref[:, j * half : (j + 1) * half] = dot(own_ref[...], w[:, :width], ((1,), (1,))) + dot(
            other_ref[...], w[:, width:], ((1,), (1,))
        )

    def body(r, amax):
        for j in range(v_ref.shape[1] // LANES):
            amax = jnp.maximum(amax, jnp.abs(v_ref[pl.ds(r, TILE), j * LANES : (j + 1) * LANES]))
        return amax

    amax = for_tiles(v_ref.shape[0], body, jnp.zeros((TILE, LANES), F32))
    write_coded(v_ref, v_ref.shape[1] // LANES, amax, out_ref)


def first_sum(i, rows, core, own, got, rest, ws):
    per = got.shape[0] // rows
    width = own.shape[1]
    shape = (rows, len(ws) * ws[0].shape[0])
    out = coded_shape(*shape)
    vmem = pl.BlockSpec(memory_space=pltpu.VMEM)
    part = pl.BlockSpec((rows, width), lambda j, at: (at[1], 0))
    at = [i, lax.rem(i, per), jnp.where(lax.div(i, per) == core, 1, 0)]
    return pl.pallas_call(
        first_kernel,
        grid_spec=pltpu.PrefetchScalarGridSpec(
            num_scalar_prefetch=1,
            grid=(1,),
            in_specs=[pl.BlockSpec((rows, width), lambda j, at: (at[0], 0)), part, part] + [vmem] * len(ws),
            out_specs=whole(out.shape),
            scratch_shapes=[pltpu.VMEM((rows, width), BF16), pltpu.VMEM(shape, F32)],
        ),
        out_shape=out,
        compiler_params=pltpu.CompilerParams(vmem_limit_bytes=10 * MIB),
        cost_estimate=pl.CostEstimate(
            flops=4 * width * shape[0] * shape[1], bytes_accessed=4 * out.size, transcendentals=0
        ),
    )(jnp.stack([jnp.int32(k) for k in at]), own, got, rest, *ws)


def owned_kernel(idx_ref, f_ref, b_ref, own_ref, mine_ref, out_ref, v_ref):
    invs = [inverse_scale(f_ref), inverse_scale(b_ref)]
    blocks = v_ref.shape[1] // LANES

    def body(r, amax):
        for j in range(2 * blocks):
            v = summed_tile(own_ref, (f_ref, b_ref), invs, r, j)
            if j < blocks:
                mine_ref[pl.ds(r, TILE), j * LANES : (j + 1) * LANES] = v
            else:
                v_ref[pl.ds(r, TILE), (j - blocks) * LANES : (j - blocks + 1) * LANES] = v
                amax = jnp.maximum(amax, jnp.abs(v))
        return amax

    amax = for_tiles(own_ref.shape[0], body, jnp.zeros((TILE, LANES), F32))
    write_coded(v_ref, blocks, amax, out_ref)


def rows_kernel(h_ref, mine_ref, got_ref, out_ref):
    rows = mine_ref.shape[0]
    inv = inverse_scale(got_ref)
    mine_at, got_at = h_ref[0] * rows, (1 - h_ref[0]) * rows

    def body(r, x):
        out_ref[pl.ds(pl.multiple_of(mine_at + r, TILE), TILE), :] = mine_ref[pl.ds(r, TILE), :]
        for j in range(mine_ref.shape[1] // LANES):
            v = decode(got_ref[pl.ds(j * rows + r, TILE), :], inv)
            out_ref[pl.ds(pl.multiple_of(got_at + r, TILE), TILE), j * LANES : (j + 1) * LANES] = v
        return x

    for_tiles(rows, body, 0)


def whole(shape):
    return pl.BlockSpec(shape, lambda i, idx: (0,) * len(shape))


def call(kernel, idx, wholes, block, out_shapes, scratch=()):
    in_specs, args = [whole(a.shape) for a in wholes], list(wholes)
    if block is not None:
        in_specs.append(pl.BlockSpec((block[1], block[0].shape[1]), lambda i, idx: (idx[0], 0)))
        args.append(block[0])
    size = sum(a.size * 4 for a in args) + sum(s.size * 4 for s in out_shapes)
    return pl.pallas_call(
        kernel,
        grid_spec=pltpu.PrefetchScalarGridSpec(
            num_scalar_prefetch=1,
            grid=(1,),
            in_specs=in_specs,
            out_specs=[whole(s.shape) for s in out_shapes],
            scratch_shapes=[pltpu.VMEM(s, F32) for s in scratch],
        ),
        out_shape=out_shapes,
        compiler_params=pltpu.CompilerParams(vmem_limit_bytes=10 * MIB),
        cost_estimate=pl.CostEstimate(flops=size * 8, bytes_accessed=size, transcendentals=0),
    )(jnp.stack([jnp.int32(i) for i in idx]), *args)


def placed_kernel(pieces, at_ref, *refs):
    srcs, out_ref, sems = refs[:-2], refs[-2], refs[-1]
    copies = []
    for i, (src, row, rows, col) in enumerate(pieces):
        ref = srcs[src]
        to = out_ref.at[pl.ds(pl.multiple_of(at_ref[i], LANES), rows), col : col + ref.shape[1]]
        copies.append(pltpu.make_async_copy(ref.at[row : row + rows], to, sems.at[i]))
    for copy in copies:
        copy.start()
    for copy in copies:
        copy.wait()


def placed(arrays, pieces, shape):
    fixed = [p[:4] for p in pieces]
    size = 2 * shape[0] * shape[1]
    return pl.pallas_call(
        functools.partial(placed_kernel, fixed),
        grid_spec=pltpu.PrefetchScalarGridSpec(
            num_scalar_prefetch=1,
            grid=(1,),
            in_specs=[pl.BlockSpec(memory_space=pltpu.VMEM)] * len(arrays),
            out_specs=pl.BlockSpec(memory_space=pltpu.VMEM),
            scratch_shapes=[pltpu.SemaphoreType.DMA((len(pieces),))],
        ),
        out_shape=jax.ShapeDtypeStruct(shape, BF16),
        compiler_params=pltpu.CompilerParams(vmem_limit_bytes=4 * MIB),
        cost_estimate=pl.CostEstimate(flops=0, bytes_accessed=2 * size, transcendentals=0),
    )(jnp.stack([jnp.int32(p[4]) for p in pieces]), *arrays)


def coded_shape(rows, width):
    return jax.ShapeDtypeStruct((width // LANES * rows + TILE, LANES), BF16)


def hop(got, mine):
    kernel = functools.partial(hop_kernel, len(got))
    return call(kernel, [jnp.int32(0)], got + [mine], None, [coded_shape(*mine.shape)], [mine.shape])[0]


def swap(a, axis):
    return lax.ppermute(a, axis, [(0, 1), (1, 0)])


def y_ring(a):
    perm = []
    for y in range(4):
        for c in range(2):
            t = (y + (1 if c == 0 else -1)) % 4
            perm.append((((y % 2) * 2 + y // 2) * 2 + c, ((t % 2) * 2 + t // 2) * 2 + c))
    return lax.ppermute(a, ("yl", "yh", "c"), perm)


def ring(a, axis, way):
    n = lax.axis_size(axis)
    perm = [(i * 2 + c, (i + (way if c == 0 else -way)) % n * 2 + c) for i in range(n) for c in range(2)]
    return lax.ppermute(a, (axis, "c"), perm)


def gathered(parts, axis, order, joint, before, out=()):
    n, me = lax.axis_size(axis), lax.axis_index(axis)
    step = 1 - 2 * lax.axis_index("c")
    count, (rows, width) = len(parts), parts[0].shape
    blocks = {0: parts}
    ahead = back = parts
    for k in range(1, n // 2 + 1):
        if k == joint:
            ahead, back = [jnp.concatenate(ahead)], [jnp.concatenate(back)]
        if k in before:
            held = before[k](blocks)
            if k < n - n // 2:
                ahead, back, *_ = after(*ahead, *back, *held)
                ahead, back = [ahead], [back]
            else:
                ahead = [after(*ahead, *held)[0]]
        if k == 1 and count == 2:
            ahead, back = blocks[-1], blocks[1] = [[f, ring(parts[1], axis, w)] for f, w in zip(out, (1, -1))]
            continue
        ahead = blocks[-k] = [ring(p, axis, 1) for p in ahead]
        if k < n - n // 2:
            back = blocks[k] = [ring(p, axis, -1) for p in back]
    arrays, pieces = [], []
    for k, got in blocks.items():
        at = lax.rem(me + step * k + n, n) * count
        for i, place in enumerate(order):
            src, row = (i, 0) if len(got) == count else (0, i * rows)
            pieces.append((len(arrays) + src, row, rows, 0, (at + place) * rows))
        arrays += got
    return arrays, pieces, (n * count * rows, width), blocks


def block_at(axis, k):
    n = lax.axis_size(axis)
    return lax.rem(lax.axis_index(axis) + (1 - 2 * lax.axis_index("c")) * k + n, n)


def scattered(share, axis, first):
    n, me = lax.axis_size(axis), lax.axis_index(axis)
    step = 1 - 2 * lax.axis_index("c")
    came = []
    for way, hops, got in ((1, n // 2, first[0]), (-1, n - n // 2 - 1, first[1])):
        got = ring(got, axis, way)
        for k in range(hops - 1, 0, -1):
            got = ring(hop([got], share(lax.rem(me + way * step * k + n, n))), axis, way)
        came.append(got)
    return came


def dot(a, b, dims):
    return lax.dot_general(a, b, (dims, ((), ())), preferred_element_type=F32)


def after(first, *rest):
    return lax.optimization_barrier((first,) + rest)


def on_device(activations, out_grad, weight):
    h = lax.axis_index("yl")
    c = lax.axis_index("c")
    tokens, width = out_grad.shape
    own_tokens, features = activations.shape
    rows = weight.shape[1]
    half = rows // 2
    owners = features // rows

    low = jnp.concatenate([activations[:, d * rows : d * rows + half] for d in range(owners)], axis=1)
    high = jnp.concatenate([activations[:, d * rows + half : (d + 1) * rows] for d in range(owners)], axis=1)
    acts_mine, acts_sent = jnp.where(h == 0, low, high), jnp.where(h == 0, high, low)
    acts_sent, acts_mine, weight, out_grad = after(acts_sent, acts_mine, weight, out_grad)
    acts_got = swap(acts_sent, "yl")

    w_mine = lax.dynamic_slice_in_dim(weight[0], h * half, half, 0)
    w_sent = lax.dynamic_slice_in_dim(weight[0], (1 - h) * half, half, 0)
    out = [ring(acts_mine, "z", 1), ring(acts_mine, "z", -1)]
    *_, acts_got, w_got = after(*out, acts_got, swap(w_sent, "yl"))
    w_pair = jnp.concatenate([w_mine, w_got], axis=1)
    *_, blocks = gathered([w_pair], "x", (0,), 0, {2: lambda b: b[1]})
    near = [0, -1, 1, -2]
    ws = [blocks[k][0] for k in near]

    part = tokens // 2
    g_sent = lax.dynamic_slice_in_dim(out_grad, c * part, part, 0)
    g_got = y_ring(after(acts_got, w_got, g_sent)[2])
    first, gs = [], []

    def first_sums(blocks):
        got = after(*blocks[-2], *blocks[2], ws[-1], g_got)[-1]
        gs.extend([out_grad, got, swap(got, "c")])
        first.extend(first_sum(block_at("z", k), 2 * own_tokens, c, *gs, ws) for k in (4, -3))
        return first

    before = {2: lambda b: [w_got], 3: lambda b: [ws[-1]], 4: first_sums}
    arrays, acts_pieces, shape, blocks = gathered([acts_mine, acts_got], "z", (h, 1 - h), 2, before, out)

    ws = after(*first, *ws)[2:]
    pieces = [(i, 0, half, 0, i * half) for i in range(owners)]
    w_all = placed(ws, pieces, (owners * half, 2 * width))
    pieces = [(0, 0, tokens, 0, 0), (1, 0, part, width, c * part), (2, 0, part, width, (1 - c) * part)]
    g_pair = placed(after(*first, *gs)[2:], pieces, (tokens, 2 * width))

    def of_tokens(i):
        count = 2 * own_tokens
        return dot(lax.dynamic_slice_in_dim(g_pair, i * count, count, 0), w_all, ((1,), (1,)))

    acts_all = placed(after(*first, *arrays)[2:], acts_pieces, shape)
    came = scattered(of_tokens, "z", first)
    mine = of_tokens(lax.axis_index("z"))

    def finished(of):
        shape = jax.ShapeDtypeStruct((own_tokens, features // 2), BF16)
        return call(tokens_kernel, [of, of], came, (mine, own_tokens), [shape])[0]

    s_got = swap(finished(1 - h), "yl")
    shape = jax.ShapeDtypeStruct((own_tokens, features), BF16)
    input_grad = call(functools.partial(columns_kernel, half), [h] + [block_at("x", k) for k in near], [finished(h), s_got], None, [shape])[0]

    def of_rows(i):
        acts = lax.dynamic_slice_in_dim(acts_all, i * half, half, 1)
        return dot(acts, g_pair, ((0,), (0,)))

    came = scattered(of_rows, "x", [hop([], of_rows(block_at("x", k))) for k in (2, -1)])
    mine = of_rows(lax.axis_index("x"))
    shapes = [jax.ShapeDtypeStruct((half, width), F32), coded_shape(half, width)]
    owned, coded = call(owned_kernel, [jnp.int32(0)], came + [mine], None, shapes, [(half, width)])
    shape = jax.ShapeDtypeStruct((rows, width), F32)
    weight_grad = call(rows_kernel, [h], [owned, swap(coded, "yl")], None, [shape])[0]
    return input_grad, weight_grad[None]


def solution(mesh):
    dp, out, in_ = mesh.devices.shape
    fine = Mesh(mesh.devices.reshape(dp, out // 2, 2, 2, in_ // 2), ("x", "z", "yl", "yh", "c"))
    tokens, split = P(("x", "z", "yl"), ("yh", "c")), P(("yh", "c"), "x", ("z", "yl"))
    return jax.shard_map(
        on_device,
        mesh=fine,
        in_specs=(tokens, P("x", ("z", "yl")), split),
        out_specs=(tokens, split),
        check_vma=False,
    )
```

```python
import functools

import jax
import jax.numpy as jnp
from jax import lax
from jax.experimental import pallas as pl
from jax.experimental.pallas import tpu as pltpu
from jax.sharding import Mesh, PartitionSpec as P

F32 = jnp.float32
BF16 = jnp.bfloat16
LANES = 128
TILE = 16
SQUARINGS = 4
TOP = 2.0**7.75
TINY = 1e-30
MIB = 1024 * 1024


def encode(v, s):
    a = jnp.abs(v) * s
    for _ in range(SQUARINGS):
        a = a * a
    return jnp.where(v < 0, -a, a).astype(BF16)


def decode(y, inv):
    y = y.astype(F32)
    a = jnp.exp2(jnp.log2(jnp.abs(y)) * 0.5**SQUARINGS) * inv
    return jnp.where(y < 0, -a, a)


def inverse_scale(ref):
    return 1.0 / ref[ref.shape[0] - TILE :, :].astype(F32)


def for_tiles(rows, body, init):
    return lax.fori_loop(0, rows // TILE, lambda i, x: body(pl.multiple_of(i * TILE, TILE), x), init, unroll=2)


def write_coded(v_ref, blocks, amax, out_ref):
    rows = v_ref.shape[0]
    coded = (TOP / jnp.maximum(amax, TINY)).astype(BF16)
    s = coded.astype(F32)
    out_ref[blocks * rows :, :] = coded

    def body(r, x):
        for j in range(blocks):
            at = j * LANES
            out_ref[pl.ds(j * rows + r, TILE), :] = encode(v_ref[pl.ds(r, TILE), at : at + LANES], s)
        return x

    for_tiles(rows, body, 0)


def summed_tile(own_ref, got, invs, r, j):
    rows = own_ref.shape[0]
    v = own_ref[pl.ds(r, TILE), j * LANES : (j + 1) * LANES]
    for ref, inv in zip(got, invs):
        v = v + decode(ref[pl.ds(j * rows + r, TILE), :], inv)
    return v


def hop_kernel(n_got, idx_ref, *refs):
    got, (own_ref, out_ref, v_ref) = refs[:n_got], refs[n_got:]
    blocks = v_ref.shape[1] // LANES
    invs = [inverse_scale(ref) for ref in got]

    def body(r, amax):
        for j in range(blocks):
            v = summed_tile(own_ref, got, invs, r, j)
            v_ref[pl.ds(r, TILE), j * LANES : (j + 1) * LANES] = v
            amax = jnp.maximum(amax, jnp.abs(v))
        return amax

    amax = for_tiles(v_ref.shape[0], body, jnp.zeros((TILE, LANES), F32))
    write_coded(v_ref, blocks, amax, out_ref)


def tokens_kernel(idx_ref, f_ref, b_ref, own_ref, out_ref):
    invs = [inverse_scale(f_ref), inverse_scale(b_ref)]
    rows = out_ref.shape[0]
    at = idx_ref[1] * rows

    def body(r, x):
        for j in range(own_ref.shape[1] // LANES):
            v = own_ref[pl.ds(r, TILE), j * LANES : (j + 1) * LANES]
            for ref, inv in zip((f_ref, b_ref), invs):
                row = pl.multiple_of(j * 2 * rows + at + r, TILE)
                v = v + decode(ref[pl.ds(row, TILE), :], inv)
            out_ref[pl.ds(r, TILE), j * LANES : (j + 1) * LANES] = v.astype(BF16)
        return x

    for_tiles(rows, body, 0)


def columns_kernel(half, at_ref, mine_ref, got_ref, out_ref):
    for j in range(mine_ref.shape[1] // half):
        at = slice(j * half, (j + 1) * half)
        mine_at = pl.multiple_of((2 * at_ref[1 + j] + at_ref[0]) * half, LANES)
        got_at = pl.multiple_of((2 * at_ref[1 + j] + 1 - at_ref[0]) * half, LANES)
        out_ref[:, pl.ds(mine_at, half)] = mine_ref[:, at]
        out_ref[:, pl.ds(got_at, half)] = got_ref[:, at]


def first_kernel(at_ref, own_ref, got_ref, rest_ref, w_ref, out_ref, other_ref, v_ref):
    width = own_ref.shape[1]

    @pl.when(at_ref[2] == 1)
    def _():
        other_ref[...] = got_ref[...]

    @pl.when(at_ref[2] != 1)
    def _():
        other_ref[...] = rest_ref[...]

    v_ref[...] = dot(own_ref[...], w_ref[:, :width], ((1,), (1,))) + dot(other_ref[...], w_ref[:, width:], ((1,), (1,)))

    def body(r, amax):
        for j in range(v_ref.shape[1] // LANES):
            amax = jnp.maximum(amax, jnp.abs(v_ref[pl.ds(r, TILE), j * LANES : (j + 1) * LANES]))
        return amax

    amax = for_tiles(v_ref.shape[0], body, jnp.zeros((TILE, LANES), F32))
    write_coded(v_ref, v_ref.shape[1] // LANES, amax, out_ref)


def first_sum(i, rows, core, own, got, rest, w_all):
    per = got.shape[0] // rows
    width = own.shape[1]
    shape = (rows, w_all.shape[0])
    out = coded_shape(*shape)
    vmem = pl.BlockSpec(memory_space=pltpu.VMEM)
    part = pl.BlockSpec((rows, width), lambda j, at: (at[1], 0))
    at = [i, lax.rem(i, per), jnp.where(lax.div(i, per) == core, 1, 0)]
    return pl.pallas_call(
        first_kernel,
        grid_spec=pltpu.PrefetchScalarGridSpec(
            num_scalar_prefetch=1,
            grid=(1,),
            in_specs=[pl.BlockSpec((rows, width), lambda j, at: (at[0], 0)), part, part, vmem],
            out_specs=whole(out.shape),
            scratch_shapes=[pltpu.VMEM((rows, width), BF16), pltpu.VMEM(shape, F32)],
        ),
        out_shape=out,
        compiler_params=pltpu.CompilerParams(vmem_limit_bytes=10 * MIB),
        cost_estimate=pl.CostEstimate(
            flops=4 * width * shape[0] * shape[1], bytes_accessed=4 * out.size, transcendentals=0
        ),
    )(jnp.stack([jnp.int32(k) for k in at]), own, got, rest, w_all)


def owned_kernel(idx_ref, f_ref, b_ref, own_ref, mine_ref, out_ref, v_ref):
    invs = [inverse_scale(f_ref), inverse_scale(b_ref)]
    blocks = v_ref.shape[1] // LANES

    def body(r, amax):
        for j in range(2 * blocks):
            v = summed_tile(own_ref, (f_ref, b_ref), invs, r, j)
            if j < blocks:
                mine_ref[pl.ds(r, TILE), j * LANES : (j + 1) * LANES] = v
            else:
                v_ref[pl.ds(r, TILE), (j - blocks) * LANES : (j - blocks + 1) * LANES] = v
                amax = jnp.maximum(amax, jnp.abs(v))
        return amax

    amax = for_tiles(own_ref.shape[0], body, jnp.zeros((TILE, LANES), F32))
    write_coded(v_ref, blocks, amax, out_ref)


def rows_kernel(h_ref, mine_ref, got_ref, out_ref):
    rows = mine_ref.shape[0]
    inv = inverse_scale(got_ref)
    mine_at, got_at = h_ref[0] * rows, (1 - h_ref[0]) * rows

    def body(r, x):
        out_ref[pl.ds(pl.multiple_of(mine_at + r, TILE), TILE), :] = mine_ref[pl.ds(r, TILE), :]
        for j in range(mine_ref.shape[1] // LANES):
            v = decode(got_ref[pl.ds(j * rows + r, TILE), :], inv)
            out_ref[pl.ds(pl.multiple_of(got_at + r, TILE), TILE), j * LANES : (j + 1) * LANES] = v
        return x

    for_tiles(rows, body, 0)


def whole(shape):
    return pl.BlockSpec(shape, lambda i, idx: (0,) * len(shape))


def call(kernel, idx, wholes, block, out_shapes, scratch=()):
    in_specs, args = [whole(a.shape) for a in wholes], list(wholes)
    if block is not None:
        in_specs.append(pl.BlockSpec((block[1], block[0].shape[1]), lambda i, idx: (idx[0], 0)))
        args.append(block[0])
    size = sum(a.size * 4 for a in args) + sum(s.size * 4 for s in out_shapes)
    return pl.pallas_call(
        kernel,
        grid_spec=pltpu.PrefetchScalarGridSpec(
            num_scalar_prefetch=1,
            grid=(1,),
            in_specs=in_specs,
            out_specs=[whole(s.shape) for s in out_shapes],
            scratch_shapes=[pltpu.VMEM(s, F32) for s in scratch],
        ),
        out_shape=out_shapes,
        compiler_params=pltpu.CompilerParams(vmem_limit_bytes=10 * MIB),
        cost_estimate=pl.CostEstimate(flops=size * 8, bytes_accessed=size, transcendentals=0),
    )(jnp.stack([jnp.int32(i) for i in idx]), *args)


def placed_kernel(pieces, at_ref, *refs):
    srcs, out_ref, sems = refs[:-2], refs[-2], refs[-1]
    copies = []
    for i, (src, row, rows, col) in enumerate(pieces):
        ref = srcs[src]
        to = out_ref.at[pl.ds(pl.multiple_of(at_ref[i], LANES), rows), col : col + ref.shape[1]]
        copies.append(pltpu.make_async_copy(ref.at[row : row + rows], to, sems.at[i]))
    for copy in copies:
        copy.start()
    for copy in copies:
        copy.wait()


def placed(arrays, pieces, shape, far=0):
    fixed = [p[:4] for p in pieces]
    size = 2 * shape[0] * shape[1]
    return pl.pallas_call(
        functools.partial(placed_kernel, fixed),
        grid_spec=pltpu.PrefetchScalarGridSpec(
            num_scalar_prefetch=1,
            grid=(1,),
            in_specs=[pl.BlockSpec(memory_space=pltpu.VMEM if i >= far else pltpu.HBM) for i in range(len(arrays))],
            out_specs=pl.BlockSpec(memory_space=pltpu.VMEM),
            scratch_shapes=[pltpu.SemaphoreType.DMA((len(pieces),))],
        ),
        out_shape=jax.ShapeDtypeStruct(shape, BF16),
        compiler_params=pltpu.CompilerParams(vmem_limit_bytes=4 * MIB),
        cost_estimate=pl.CostEstimate(flops=0, bytes_accessed=2 * size, transcendentals=0),
    )(jnp.stack([jnp.int32(p[4]) for p in pieces]), *arrays)


def coded_shape(rows, width):
    return jax.ShapeDtypeStruct((width // LANES * rows + TILE, LANES), BF16)


def hop(got, mine):
    kernel = functools.partial(hop_kernel, len(got))
    return call(kernel, [jnp.int32(0)], got + [mine], None, [coded_shape(*mine.shape)], [mine.shape])[0]


def swap(a, axis):
    return lax.ppermute(a, axis, [(0, 1), (1, 0)])


def y_ring(a):
    perm = []
    for y in range(4):
        for c in range(2):
            t = (y + (1 if c == 0 else -1)) % 4
            perm.append((((y % 2) * 2 + y // 2) * 2 + c, ((t % 2) * 2 + t // 2) * 2 + c))
    return lax.ppermute(a, ("yl", "yh", "c"), perm)


def ring(a, axis, way):
    n = lax.axis_size(axis)
    perm = [(i * 2 + c, (i + (way if c == 0 else -way)) % n * 2 + c) for i in range(n) for c in range(2)]
    return lax.ppermute(a, (axis, "c"), perm)


def gathered(parts, axis, order, joint, before, known={}):
    n, me = lax.axis_size(axis), lax.axis_index(axis)
    step = 1 - 2 * lax.axis_index("c")
    count, (rows, width) = len(parts), parts[0].shape
    blocks = {0: parts}
    ahead = back = parts
    for k in range(1, n // 2 + 1):
        if k == joint:
            ahead, back = [jnp.concatenate(ahead)], [jnp.concatenate(back)]
        if k in before:
            held = before[k](blocks)
            m = len(ahead)
            tied = after(*ahead, *back, *held)
            ahead, back = list(tied[:m]), list(tied[m : 2 * m])
        if k in known:
            ahead, back = blocks[-k], blocks[k] = known[k]
            continue
        ahead = blocks[-k] = [ring(p, axis, 1) for p in ahead]
        if k < n - n // 2:
            back = blocks[k] = [ring(p, axis, -1) for p in back]
    arrays, pieces = [], []
    for k, got in blocks.items():
        at = lax.rem(me + step * k + n, n) * count
        for i, place in enumerate(order):
            src, row = (i, 0) if len(got) == count else (0, i * rows)
            pieces.append((len(arrays) + src, row, rows, 0, (at + place) * rows))
        arrays += got
    return arrays, pieces, (n * count * rows, width), blocks


def block_at(axis, k):
    n = lax.axis_size(axis)
    return lax.rem(lax.axis_index(axis) + (1 - 2 * lax.axis_index("c")) * k + n, n)


def scattered(share, axis, first):
    n, me = lax.axis_size(axis), lax.axis_index(axis)
    step = 1 - 2 * lax.axis_index("c")
    came = []
    for way, hops, got in ((1, n // 2, first[0]), (-1, n - n // 2 - 1, first[1])):
        got = ring(got, axis, way)
        for k in range(hops - 1, 0, -1):
            got = ring(hop([got], share(lax.rem(me + way * step * k + n, n))), axis, way)
        came.append(got)
    return came


def dot(a, b, dims):
    return lax.dot_general(a, b, (dims, ((), ())), preferred_element_type=F32)


def after(first, *rest):
    return lax.optimization_barrier((first,) + rest)


def on_device(activations, out_grad, weight):
    h = lax.axis_index("yl")
    c = lax.axis_index("c")
    tokens, width = out_grad.shape
    own_tokens, features = activations.shape
    rows = weight.shape[1]
    half = rows // 2
    owners = features // rows

    low = jnp.concatenate([activations[:, d * rows : d * rows + half] for d in range(owners)], axis=1)
    high = jnp.concatenate([activations[:, d * rows + half : (d + 1) * rows] for d in range(owners)], axis=1)
    acts_mine, acts_sent = jnp.where(h == 0, low, high), jnp.where(h == 0, high, low)
    acts_sent, acts_mine, weight, out_grad = after(acts_sent, acts_mine, weight, out_grad)
    acts_got = swap(acts_sent, "yl")

    w_mine = lax.dynamic_slice_in_dim(weight[0], h * half, half, 0)
    w_sent = lax.dynamic_slice_in_dim(weight[0], (1 - h) * half, half, 0)
    out = [(ring(acts_mine, "z", 1), ring(acts_mine, "z", -1))]
    out.append((ring(out[0][0], "z", 1), ring(out[0][1], "z", -1)))
    *_, acts_got, w_got = after(*out[1], acts_got, swap(w_sent, "yl"))
    other = ring(acts_got, "z", 1), ring(acts_got, "z", -1)
    known = {1: tuple([a, b] for a, b in zip(out[0], other))}
    known[2] = tuple([a, ring(b, "z", way)] for a, b, way in zip(out[1], other, (1, -1)))
    w_pair = jnp.concatenate([w_mine, w_got], axis=1)
    *_, blocks = gathered([w_pair], "x", (0,), 0, {2: lambda b: [known[2][0][1], known[2][1][1]]})
    near = [0, -1, 1, -2]
    ws = [blocks[k][0] for k in near]
    pieces = [(i, 0, half, 0, i * half) for i in range(owners)]
    w_all = placed(ws, pieces, (owners * half, 2 * width), owners - 1)

    part = tokens // 2
    g_sent = lax.dynamic_slice_in_dim(out_grad, c * part, part, 0)
    g_got = y_ring(after(acts_got, w_got, g_sent)[2])

    before = {3: lambda b: ws[1:3]}
    arrays, acts_pieces, shape, blocks = gathered([acts_mine, acts_got], "z", (h, 1 - h), 3, before, known)
    g_got = after(*blocks[-3], *blocks[3], ws[-1], g_got)[-1]
    gs = [out_grad, g_got, swap(g_got, "c")]

    first = [first_sum(block_at("z", k), 2 * own_tokens, c, *gs, w_all) for k in (4, -3)]
    pieces = [(0, 0, tokens, 0, 0), (1, 0, part, width, c * part), (2, 0, part, width, (1 - c) * part)]
    g_pair = placed(after(*first, *gs)[2:], pieces, (tokens, 2 * width))

    def of_tokens(i):
        count = 2 * own_tokens
        return dot(lax.dynamic_slice_in_dim(g_pair, i * count, count, 0), w_all, ((1,), (1,)))

    acts_all = placed(after(*first, *arrays)[2:], acts_pieces, shape)
    came = scattered(of_tokens, "z", first)
    mine = of_tokens(lax.axis_index("z"))

    def finished(of):
        shape = jax.ShapeDtypeStruct((own_tokens, features // 2), BF16)
        return call(tokens_kernel, [of, of], came, (mine, own_tokens), [shape])[0]

    s_got = swap(finished(1 - h), "yl")
    shape = jax.ShapeDtypeStruct((own_tokens, features), BF16)
    input_grad = call(functools.partial(columns_kernel, half), [h] + [block_at("x", k) for k in near], [finished(h), s_got], None, [shape])[0]

    def of_rows(i):
        acts = lax.dynamic_slice_in_dim(acts_all, i * half, half, 1)
        return dot(acts, g_pair, ((0,), (0,)))

    came = scattered(of_rows, "x", [hop([], of_rows(block_at("x", k))) for k in (2, -1)])
    mine = of_rows(lax.axis_index("x"))
    shapes = [jax.ShapeDtypeStruct((half, width), F32), coded_shape(half, width)]
    owned, coded = call(owned_kernel, [jnp.int32(0)], came + [mine], None, shapes, [(half, width)])
    shape = jax.ShapeDtypeStruct((rows, width), F32)
    weight_grad = call(rows_kernel, [h], [owned, swap(coded, "yl")], None, [shape])[0]
    return input_grad, weight_grad[None]


def solution(mesh):
    dp, out, in_ = mesh.devices.shape
    fine = Mesh(mesh.devices.reshape(dp, out // 2, 2, 2, in_ // 2), ("x", "z", "yl", "yh", "c"))
    tokens, split = P(("x", "z", "yl"), ("yh", "c")), P(("yh", "c"), "x", ("z", "yl"))
    return jax.shard_map(
        on_device,
        mesh=fine,
        in_specs=(tokens, P("x", ("z", "yl")), split),
        out_specs=(tokens, split),
        check_vma=False,
    )
```

```python
import functools

import jax
import jax.numpy as jnp
from jax import lax
from jax.experimental import pallas as pl
from jax.experimental.pallas import tpu as pltpu
from jax.sharding import Mesh, PartitionSpec as P

F32 = jnp.float32
BF16 = jnp.bfloat16
LANES = 128
TILE = 16
SQUARINGS = 4
TOP = 2.0**7.75
TINY = 1e-30
MIB = 1024 * 1024


def encode(v, s):
    a = jnp.abs(v) * s
    for _ in range(SQUARINGS):
        a = a * a
    return jnp.where(v < 0, -a, a).astype(BF16)


def decode(y, inv):
    y = y.astype(F32)
    a = jnp.exp2(jnp.log2(jnp.abs(y)) * 0.5**SQUARINGS) * inv
    return jnp.where(y < 0, -a, a)


def inverse_scale(ref):
    return 1.0 / ref[ref.shape[0] - TILE :, :].astype(F32)


def for_tiles(rows, body, init):
    return lax.fori_loop(0, rows // TILE, lambda i, x: body(pl.multiple_of(i * TILE, TILE), x), init, unroll=2)


def write_coded(v_ref, blocks, amax, out_ref):
    rows = v_ref.shape[0]
    coded = (TOP / jnp.maximum(amax, TINY)).astype(BF16)
    s = coded.astype(F32)
    out_ref[blocks * rows :, :] = coded

    def body(r, x):
        for j in range(blocks):
            at = j * LANES
            out_ref[pl.ds(j * rows + r, TILE), :] = encode(v_ref[pl.ds(r, TILE), at : at + LANES], s)
        return x

    for_tiles(rows, body, 0)


def summed_tile(own_ref, got, invs, r, j):
    rows = own_ref.shape[0]
    v = own_ref[pl.ds(r, TILE), j * LANES : (j + 1) * LANES]
    for ref, inv in zip(got, invs):
        v = v + decode(ref[pl.ds(j * rows + r, TILE), :], inv)
    return v


def hop_kernel(n_got, idx_ref, *refs):
    got, (own_ref, out_ref, v_ref) = refs[:n_got], refs[n_got:]
    blocks = v_ref.shape[1] // LANES
    invs = [inverse_scale(ref) for ref in got]

    def body(r, amax):
        for j in range(blocks):
            v = summed_tile(own_ref, got, invs, r, j)
            v_ref[pl.ds(r, TILE), j * LANES : (j + 1) * LANES] = v
            amax = jnp.maximum(amax, jnp.abs(v))
        return amax

    amax = for_tiles(v_ref.shape[0], body, jnp.zeros((TILE, LANES), F32))
    write_coded(v_ref, blocks, amax, out_ref)


def tokens_kernel(idx_ref, f_ref, b_ref, own_ref, out_ref):
    invs = [inverse_scale(f_ref), inverse_scale(b_ref)]
    rows = out_ref.shape[0]
    at = idx_ref[1] * rows

    def body(r, x):
        for j in range(own_ref.shape[1] // LANES):
            v = own_ref[pl.ds(r, TILE), j * LANES : (j + 1) * LANES]
            for ref, inv in zip((f_ref, b_ref), invs):
                row = pl.multiple_of(j * 2 * rows + at + r, TILE)
                v = v + decode(ref[pl.ds(row, TILE), :], inv)
            out_ref[pl.ds(r, TILE), j * LANES : (j + 1) * LANES] = v.astype(BF16)
        return x

    for_tiles(rows, body, 0)


def columns_kernel(half, at_ref, mine_ref, got_ref, out_ref):
    for j in range(mine_ref.shape[1] // half):
        at = slice(j * half, (j + 1) * half)
        mine_at = pl.multiple_of((2 * at_ref[1 + j] + at_ref[0]) * half, LANES)
        got_at = pl.multiple_of((2 * at_ref[1 + j] + 1 - at_ref[0]) * half, LANES)
        out_ref[:, pl.ds(mine_at, half)] = mine_ref[:, at]
        out_ref[:, pl.ds(got_at, half)] = got_ref[:, at]


def first_kernel(at_ref, g_ref, w_ref, out_ref, v_ref):
    v_ref[...] = dot(g_ref[...], w_ref[...], ((1,), (1,)))

    def body(r, amax):
        for j in range(v_ref.shape[1] // LANES):
            amax = jnp.maximum(amax, jnp.abs(v_ref[pl.ds(r, TILE), j * LANES : (j + 1) * LANES]))
        return amax

    amax = for_tiles(v_ref.shape[0], body, jnp.zeros((TILE, LANES), F32))
    write_coded(v_ref, v_ref.shape[1] // LANES, amax, out_ref)


def first_sum(i, rows, g_pair, w_all):
    width = g_pair.shape[1]
    shape = (rows, w_all.shape[0])
    out = coded_shape(*shape)
    return pl.pallas_call(
        first_kernel,
        grid_spec=pltpu.PrefetchScalarGridSpec(
            num_scalar_prefetch=1,
            grid=(1,),
            in_specs=[
                pl.BlockSpec((rows, width), lambda j, at: (at[0], 0)),
                pl.BlockSpec(memory_space=pltpu.VMEM),
            ],
            out_specs=whole(out.shape),
            scratch_shapes=[pltpu.VMEM(shape, F32)],
        ),
        out_shape=out,
        compiler_params=pltpu.CompilerParams(vmem_limit_bytes=10 * MIB),
        cost_estimate=pl.CostEstimate(
            flops=2 * width * shape[0] * shape[1], bytes_accessed=4 * out.size, transcendentals=0
        ),
    )(jnp.stack([jnp.int32(i)]), g_pair, w_all)


def owned_kernel(idx_ref, f_ref, b_ref, own_ref, mine_ref, out_ref, v_ref):
    invs = [inverse_scale(f_ref), inverse_scale(b_ref)]
    blocks = v_ref.shape[1] // LANES

    def body(r, amax):
        for j in range(2 * blocks):
            v = summed_tile(own_ref, (f_ref, b_ref), invs, r, j)
            if j < blocks:
                mine_ref[pl.ds(r, TILE), j * LANES : (j + 1) * LANES] = v
            else:
                v_ref[pl.ds(r, TILE), (j - blocks) * LANES : (j - blocks + 1) * LANES] = v
                amax = jnp.maximum(amax, jnp.abs(v))
        return amax

    amax = for_tiles(own_ref.shape[0], body, jnp.zeros((TILE, LANES), F32))
    write_coded(v_ref, blocks, amax, out_ref)


def rows_kernel(h_ref, mine_ref, got_ref, out_ref):
    rows = mine_ref.shape[0]
    inv = inverse_scale(got_ref)
    mine_at, got_at = h_ref[0] * rows, (1 - h_ref[0]) * rows

    def body(r, x):
        out_ref[pl.ds(pl.multiple_of(mine_at + r, TILE), TILE), :] = mine_ref[pl.ds(r, TILE), :]
        for j in range(mine_ref.shape[1] // LANES):
            v = decode(got_ref[pl.ds(j * rows + r, TILE), :], inv)
            out_ref[pl.ds(pl.multiple_of(got_at + r, TILE), TILE), j * LANES : (j + 1) * LANES] = v
        return x

    for_tiles(rows, body, 0)


def whole(shape):
    return pl.BlockSpec(shape, lambda i, idx: (0,) * len(shape))


def call(kernel, idx, wholes, block, out_shapes, scratch=()):
    in_specs, args = [whole(a.shape) for a in wholes], list(wholes)
    if block is not None:
        in_specs.append(pl.BlockSpec((block[1], block[0].shape[1]), lambda i, idx: (idx[0], 0)))
        args.append(block[0])
    size = sum(a.size * 4 for a in args) + sum(s.size * 4 for s in out_shapes)
    return pl.pallas_call(
        kernel,
        grid_spec=pltpu.PrefetchScalarGridSpec(
            num_scalar_prefetch=1,
            grid=(1,),
            in_specs=in_specs,
            out_specs=[whole(s.shape) for s in out_shapes],
            scratch_shapes=[pltpu.VMEM(s, F32) for s in scratch],
        ),
        out_shape=out_shapes,
        compiler_params=pltpu.CompilerParams(vmem_limit_bytes=10 * MIB),
        cost_estimate=pl.CostEstimate(flops=size * 8, bytes_accessed=size, transcendentals=0),
    )(jnp.stack([jnp.int32(i) for i in idx]), *args)


def placed_kernel(pieces, at_ref, *refs):
    srcs, out_ref, sems = refs[:-2], refs[-2], refs[-1]
    copies = []
    for i, (src, row, rows, col) in enumerate(pieces):
        ref = srcs[src]
        to = out_ref.at[pl.ds(pl.multiple_of(at_ref[i], LANES), rows), col : col + ref.shape[1]]
        copies.append(pltpu.make_async_copy(ref.at[row : row + rows], to, sems.at[i]))
    for copy in copies:
        copy.start()
    for copy in copies:
        copy.wait()


def placed(arrays, pieces, shape, far=0):
    fixed = [p[:4] for p in pieces]
    size = 2 * shape[0] * shape[1]
    return pl.pallas_call(
        functools.partial(placed_kernel, fixed),
        grid_spec=pltpu.PrefetchScalarGridSpec(
            num_scalar_prefetch=1,
            grid=(1,),
            in_specs=[pl.BlockSpec(memory_space=pltpu.VMEM if i >= far else pl.ANY) for i in range(len(arrays))],
            out_specs=pl.BlockSpec(memory_space=pltpu.VMEM),
            scratch_shapes=[pltpu.SemaphoreType.DMA((len(pieces),))],
        ),
        out_shape=jax.ShapeDtypeStruct(shape, BF16),
        compiler_params=pltpu.CompilerParams(vmem_limit_bytes=4 * MIB),
        cost_estimate=pl.CostEstimate(flops=0, bytes_accessed=2 * size, transcendentals=0),
    )(jnp.stack([jnp.int32(p[4]) for p in pieces]), *arrays)


def coded_shape(rows, width):
    return jax.ShapeDtypeStruct((width // LANES * rows + TILE, LANES), BF16)


def hop(got, mine):
    kernel = functools.partial(hop_kernel, len(got))
    return call(kernel, [jnp.int32(0)], got + [mine], None, [coded_shape(*mine.shape)], [mine.shape])[0]


def swap(a, axis):
    return lax.ppermute(a, axis, [(0, 1), (1, 0)])


def y_ring(a):
    perm = []
    for y in range(4):
        for c in range(2):
            t = (y + (1 if c == 0 else -1)) % 4
            perm.append((((y % 2) * 2 + y // 2) * 2 + c, ((t % 2) * 2 + t // 2) * 2 + c))
    return lax.ppermute(a, ("yl", "yh", "c"), perm)


def ring(a, axis, way):
    n = lax.axis_size(axis)
    perm = [(i * 2 + c, (i + (way if c == 0 else -way)) % n * 2 + c) for i in range(n) for c in range(2)]
    return lax.ppermute(a, (axis, "c"), perm)


def gathered(parts, axis, order, joint, before, known={}):
    n, me = lax.axis_size(axis), lax.axis_index(axis)
    step = 1 - 2 * lax.axis_index("c")
    count, (rows, width) = len(parts), parts[0].shape
    blocks = {0: parts}
    ahead = back = parts
    for k in range(1, n // 2 + 1):
        if k == joint:
            ahead, back = [jnp.concatenate(ahead)], [jnp.concatenate(back)]
        if k in before:
            held = before[k](blocks)
            m = len(ahead)
            tied = after(*ahead, *back, *held)
            ahead, back = list(tied[:m]), list(tied[m : 2 * m])
        if k in known:
            ahead, back = blocks[-k], blocks[k] = known[k]
            continue
        ahead = blocks[-k] = [ring(p, axis, 1) for p in ahead]
        if k < n - n // 2:
            back = blocks[k] = [ring(p, axis, -1) for p in back]
    arrays, pieces = [], []
    for k, got in blocks.items():
        at = lax.rem(me + step * k + n, n) * count
        for i, place in enumerate(order):
            src, row = (i, 0) if len(got) == count else (0, i * rows)
            pieces.append((len(arrays) + src, row, rows, 0, (at + place) * rows))
        arrays += got
    return arrays, pieces, (n * count * rows, width), blocks


def block_at(axis, k):
    n = lax.axis_size(axis)
    return lax.rem(lax.axis_index(axis) + (1 - 2 * lax.axis_index("c")) * k + n, n)


def scattered(share, axis, first):
    n, me = lax.axis_size(axis), lax.axis_index(axis)
    step = 1 - 2 * lax.axis_index("c")
    came = []
    for way, hops, got in ((1, n // 2, first[0]), (-1, n - n // 2 - 1, first[1])):
        got = ring(got, axis, way)
        for k in range(hops - 1, 0, -1):
            got = ring(hop([got], share(lax.rem(me + way * step * k + n, n))), axis, way)
        came.append(got)
    return came


def dot(a, b, dims):
    return lax.dot_general(a, b, (dims, ((), ())), preferred_element_type=F32)


def after(first, *rest):
    return lax.optimization_barrier((first,) + rest)


def on_device(activations, out_grad, weight):
    h = lax.axis_index("yl")
    c = lax.axis_index("c")
    tokens, width = out_grad.shape
    own_tokens, features = activations.shape
    rows = weight.shape[1]
    half = rows // 2
    owners = features // rows

    low = jnp.concatenate([activations[:, d * rows : d * rows + half] for d in range(owners)], axis=1)
    high = jnp.concatenate([activations[:, d * rows + half : (d + 1) * rows] for d in range(owners)], axis=1)
    acts_mine, acts_sent = jnp.where(h == 0, low, high), jnp.where(h == 0, high, low)
    acts_sent, acts_mine, weight, out_grad = after(acts_sent, acts_mine, weight, out_grad)
    acts_got = swap(acts_sent, "yl")

    w_mine = lax.dynamic_slice_in_dim(weight[0], h * half, half, 0)
    w_sent = lax.dynamic_slice_in_dim(weight[0], (1 - h) * half, half, 0)
    out = [(ring(acts_mine, "z", 1), ring(acts_mine, "z", -1))]
    out.append((ring(out[0][0], "z", 1), ring(out[0][1], "z", -1)))
    *_, acts_got, w_got = after(*out[1], acts_got, swap(w_sent, "yl"))
    other = ring(acts_got, "z", 1), ring(acts_got, "z", -1)
    known = {1: tuple([a, b] for a, b in zip(out[0], other))}
    known[2] = tuple([a, ring(b, "z", way)] for a, b, way in zip(out[1], other, (1, -1)))
    w_pair = jnp.concatenate([w_mine, w_got], axis=1)
    *_, blocks = gathered([w_pair], "x", (0,), 0, {2: lambda b: [known[2][0][1], known[2][1][1]]})
    near = [0, -1, 1, -2]
    ws = [blocks[k][0] for k in near]
    pieces = [(i, 0, half, 0, i * half) for i in range(owners)]
    w_all = placed(ws, pieces, (owners * half, 2 * width), owners - 1)

    part = tokens // 2
    g_sent = lax.dynamic_slice_in_dim(out_grad, c * part, part, 0)
    g_got = y_ring(after(acts_got, w_got, g_sent)[2])

    pairs = []

    def g_pair_of(blocks):
        got = after(blocks[-2][1], blocks[2][1], *ws[1:3], g_got)[-1]
        pieces = [(0, 0, tokens, 0, 0), (1, 0, part, width, c * part), (2, 0, part, width, (1 - c) * part)]
        pairs.append(placed([out_grad, got, swap(got, "c")], pieces, (tokens, 2 * width)))
        return pairs

    before = {3: lambda b: ws[1:3], 4: g_pair_of}
    arrays, acts_pieces, shape, blocks = gathered([acts_mine, acts_got], "z", (h, 1 - h), 3, before, known)
    (g_pair,) = pairs

    first = [first_sum(block_at("z", k), 2 * own_tokens, g_pair, w_all) for k in (4, -3)]

    def of_tokens(i):
        count = 2 * own_tokens
        return dot(lax.dynamic_slice_in_dim(g_pair, i * count, count, 0), w_all, ((1,), (1,)))

    acts_all = placed(after(*first, *arrays)[2:], acts_pieces, shape)
    came = scattered(of_tokens, "z", first)
    mine = of_tokens(lax.axis_index("z"))

    def finished(of):
        shape = jax.ShapeDtypeStruct((own_tokens, features // 2), BF16)
        return call(tokens_kernel, [of, of], came, (mine, own_tokens), [shape])[0]

    s_got = swap(finished(1 - h), "yl")
    shape = jax.ShapeDtypeStruct((own_tokens, features), BF16)
    input_grad = call(functools.partial(columns_kernel, half), [h] + [block_at("x", k) for k in near], [finished(h), s_got], None, [shape])[0]

    def of_rows(i):
        acts = lax.dynamic_slice_in_dim(acts_all, i * half, half, 1)
        return dot(acts, g_pair, ((0,), (0,)))

    came = scattered(of_rows, "x", [hop([], of_rows(block_at("x", k))) for k in (2, -1)])
    mine = of_rows(lax.axis_index("x"))
    shapes = [jax.ShapeDtypeStruct((half, width), F32), coded_shape(half, width)]
    owned, coded = call(owned_kernel, [jnp.int32(0)], came + [mine], None, shapes, [(half, width)])
    shape = jax.ShapeDtypeStruct((rows, width), F32)
    weight_grad = call(rows_kernel, [h], [owned, swap(coded, "yl")], None, [shape])[0]
    return input_grad, weight_grad[None]


def solution(mesh):
    dp, out, in_ = mesh.devices.shape
    fine = Mesh(mesh.devices.reshape(dp, out // 2, 2, 2, in_ // 2), ("x", "z", "yl", "yh", "c"))
    tokens, split = P(("x", "z", "yl"), ("yh", "c")), P(("yh", "c"), "x", ("z", "yl"))
    return jax.shard_map(
        on_device,
        mesh=fine,
        in_specs=(tokens, P("x", ("z", "yl")), split),
        out_specs=(tokens, split),
        check_vma=False,
    )
```

```python
import functools

import jax
import jax.numpy as jnp
from jax import lax
from jax.experimental import pallas as pl
from jax.experimental.pallas import tpu as pltpu
from jax.sharding import Mesh, PartitionSpec as P

F32 = jnp.float32
BF16 = jnp.bfloat16
LANES = 128
TILE = 16
SQUARINGS = 4
TOP = 2.0**7.75
TINY = 1e-30
MIB = 1024 * 1024


def encode(v, s):
    a = jnp.abs(v) * s
    for _ in range(SQUARINGS):
        a = a * a
    return jnp.where(v < 0, -a, a).astype(BF16)


def decode(y, inv):
    y = y.astype(F32)
    a = jnp.exp2(jnp.log2(jnp.abs(y)) * 0.5**SQUARINGS) * inv
    return jnp.where(y < 0, -a, a)


def inverse_scale(ref):
    return 1.0 / ref[ref.shape[0] - TILE :, :].astype(F32)


def for_tiles(rows, body, init):
    return lax.fori_loop(0, rows // TILE, lambda i, x: body(pl.multiple_of(i * TILE, TILE), x), init, unroll=2)


def write_coded(v_ref, blocks, amax, out_ref):
    rows = v_ref.shape[0]
    coded = (TOP / jnp.maximum(amax, TINY)).astype(BF16)
    s = coded.astype(F32)
    out_ref[blocks * rows :, :] = coded

    def body(r, x):
        for j in range(blocks):
            at = j * LANES
            out_ref[pl.ds(j * rows + r, TILE), :] = encode(v_ref[pl.ds(r, TILE), at : at + LANES], s)
        return x

    for_tiles(rows, body, 0)


def summed_tile(own_ref, got, invs, r, j):
    rows = own_ref.shape[0]
    v = own_ref[pl.ds(r, TILE), j * LANES : (j + 1) * LANES]
    for ref, inv in zip(got, invs):
        v = v + decode(ref[pl.ds(j * rows + r, TILE), :], inv)
    return v


def hop_kernel(n_got, idx_ref, *refs):
    got, (own_ref, out_ref, v_ref) = refs[:n_got], refs[n_got:]
    blocks = v_ref.shape[1] // LANES
    invs = [inverse_scale(ref) for ref in got]

    def body(r, amax):
        for j in range(blocks):
            v = summed_tile(own_ref, got, invs, r, j)
            v_ref[pl.ds(r, TILE), j * LANES : (j + 1) * LANES] = v
            amax = jnp.maximum(amax, jnp.abs(v))
        return amax

    amax = for_tiles(v_ref.shape[0], body, jnp.zeros((TILE, LANES), F32))
    write_coded(v_ref, blocks, amax, out_ref)


def tokens_kernel(idx_ref, f_ref, b_ref, own_ref, out_ref):
    invs = [inverse_scale(f_ref), inverse_scale(b_ref)]
    rows = out_ref.shape[0]
    at = idx_ref[1] * rows

    def body(r, x):
        for j in range(own_ref.shape[1] // LANES):
            v = own_ref[pl.ds(r, TILE), j * LANES : (j + 1) * LANES]
            for ref, inv in zip((f_ref, b_ref), invs):
                row = pl.multiple_of(j * 2 * rows + at + r, TILE)
                v = v + decode(ref[pl.ds(row, TILE), :], inv)
            out_ref[pl.ds(r, TILE), j * LANES : (j + 1) * LANES] = v.astype(BF16)
        return x

    for_tiles(rows, body, 0)


def columns_kernel(half, at_ref, mine_ref, got_ref, out_ref):
    for j in range(mine_ref.shape[1] // half):
        at = slice(j * half, (j + 1) * half)
        mine_at = pl.multiple_of((2 * at_ref[1 + j] + at_ref[0]) * half, LANES)
        got_at = pl.multiple_of((2 * at_ref[1 + j] + 1 - at_ref[0]) * half, LANES)
        out_ref[:, pl.ds(mine_at, half)] = mine_ref[:, at]
        out_ref[:, pl.ds(got_at, half)] = got_ref[:, at]


def first_kernel(at_ref, g_ref, w_ref, out_ref, v_ref):
    v_ref[...] = dot(g_ref[...], w_ref[...], ((1,), (1,)))

    def body(r, amax):
        for j in range(v_ref.shape[1] // LANES):
            amax = jnp.maximum(amax, jnp.abs(v_ref[pl.ds(r, TILE), j * LANES : (j + 1) * LANES]))
        return amax

    amax = for_tiles(v_ref.shape[0], body, jnp.zeros((TILE, LANES), F32))
    write_coded(v_ref, v_ref.shape[1] // LANES, amax, out_ref)


def first_sum(i, rows, g_pair, w_all):
    width = g_pair.shape[1]
    shape = (rows, w_all.shape[0])
    out = coded_shape(*shape)
    return pl.pallas_call(
        first_kernel,
        grid_spec=pltpu.PrefetchScalarGridSpec(
            num_scalar_prefetch=1,
            grid=(1,),
            in_specs=[
                pl.BlockSpec((rows, width), lambda j, at: (at[0], 0)),
                pl.BlockSpec(memory_space=pltpu.VMEM),
            ],
            out_specs=whole(out.shape),
            scratch_shapes=[pltpu.VMEM(shape, F32)],
        ),
        out_shape=out,
        compiler_params=pltpu.CompilerParams(vmem_limit_bytes=10 * MIB),
        cost_estimate=pl.CostEstimate(
            flops=2 * width * shape[0] * shape[1], bytes_accessed=4 * out.size, transcendentals=0
        ),
    )(jnp.stack([jnp.int32(i)]), g_pair, w_all)


def owned_kernel(idx_ref, f_ref, b_ref, own_ref, mine_ref, out_ref, v_ref):
    invs = [inverse_scale(f_ref), inverse_scale(b_ref)]
    blocks = v_ref.shape[1] // LANES

    def body(r, amax):
        for j in range(2 * blocks):
            v = summed_tile(own_ref, (f_ref, b_ref), invs, r, j)
            if j < blocks:
                mine_ref[pl.ds(r, TILE), j * LANES : (j + 1) * LANES] = v
            else:
                v_ref[pl.ds(r, TILE), (j - blocks) * LANES : (j - blocks + 1) * LANES] = v
                amax = jnp.maximum(amax, jnp.abs(v))
        return amax

    amax = for_tiles(own_ref.shape[0], body, jnp.zeros((TILE, LANES), F32))
    write_coded(v_ref, blocks, amax, out_ref)


def rows_kernel(h_ref, mine_ref, got_ref, out_ref):
    rows = mine_ref.shape[0]
    inv = inverse_scale(got_ref)
    mine_at, got_at = h_ref[0] * rows, (1 - h_ref[0]) * rows

    def body(r, x):
        out_ref[pl.ds(pl.multiple_of(mine_at + r, TILE), TILE), :] = mine_ref[pl.ds(r, TILE), :]
        for j in range(mine_ref.shape[1] // LANES):
            v = decode(got_ref[pl.ds(j * rows + r, TILE), :], inv)
            out_ref[pl.ds(pl.multiple_of(got_at + r, TILE), TILE), j * LANES : (j + 1) * LANES] = v
        return x

    for_tiles(rows, body, 0)


def whole(shape):
    return pl.BlockSpec(shape, lambda i, idx: (0,) * len(shape))


def call(kernel, idx, wholes, block, out_shapes, scratch=()):
    in_specs, args = [whole(a.shape) for a in wholes], list(wholes)
    if block is not None:
        in_specs.append(pl.BlockSpec((block[1], block[0].shape[1]), lambda i, idx: (idx[0], 0)))
        args.append(block[0])
    size = sum(a.size * 4 for a in args) + sum(s.size * 4 for s in out_shapes)
    return pl.pallas_call(
        kernel,
        grid_spec=pltpu.PrefetchScalarGridSpec(
            num_scalar_prefetch=1,
            grid=(1,),
            in_specs=in_specs,
            out_specs=[whole(s.shape) for s in out_shapes],
            scratch_shapes=[pltpu.VMEM(s, F32) for s in scratch],
        ),
        out_shape=out_shapes,
        compiler_params=pltpu.CompilerParams(vmem_limit_bytes=10 * MIB),
        cost_estimate=pl.CostEstimate(flops=size * 8, bytes_accessed=size, transcendentals=0),
    )(jnp.stack([jnp.int32(i) for i in idx]), *args)


def placed_kernel(pieces, at_ref, *refs):
    srcs, out_ref, sems = refs[:-2], refs[-2], refs[-1]
    copies = []
    for i, (src, row, rows, col) in enumerate(pieces):
        ref = srcs[src]
        to = out_ref.at[pl.ds(pl.multiple_of(at_ref[i], LANES), rows), col : col + ref.shape[1]]
        copies.append(pltpu.make_async_copy(ref.at[row : row + rows], to, sems.at[i]))
    for copy in copies:
        copy.start()
    for copy in copies:
        copy.wait()


def placed(arrays, pieces, shape, far=0):
    fixed = [p[:4] for p in pieces]
    size = 2 * shape[0] * shape[1]
    return pl.pallas_call(
        functools.partial(placed_kernel, fixed),
        grid_spec=pltpu.PrefetchScalarGridSpec(
            num_scalar_prefetch=1,
            grid=(1,),
            in_specs=[pl.BlockSpec(memory_space=pltpu.VMEM if i >= far else pl.ANY) for i in range(len(arrays))],
            out_specs=pl.BlockSpec(memory_space=pltpu.VMEM),
            scratch_shapes=[pltpu.SemaphoreType.DMA((len(pieces),))],
        ),
        out_shape=jax.ShapeDtypeStruct(shape, BF16),
        compiler_params=pltpu.CompilerParams(vmem_limit_bytes=4 * MIB),
        cost_estimate=pl.CostEstimate(flops=0, bytes_accessed=2 * size, transcendentals=0),
    )(jnp.stack([jnp.int32(p[4]) for p in pieces]), *arrays)


def coded_shape(rows, width):
    return jax.ShapeDtypeStruct((width // LANES * rows + TILE, LANES), BF16)


def hop(got, mine):
    kernel = functools.partial(hop_kernel, len(got))
    return call(kernel, [jnp.int32(0)], got + [mine], None, [coded_shape(*mine.shape)], [mine.shape])[0]


def swap(a, axis):
    return lax.ppermute(a, axis, [(0, 1), (1, 0)])


def y_ring(a):
    perm = []
    for y in range(4):
        for c in range(2):
            t = (y + (1 if c == 0 else -1)) % 4
            perm.append((((y % 2) * 2 + y // 2) * 2 + c, ((t % 2) * 2 + t // 2) * 2 + c))
    return lax.ppermute(a, ("yl", "yh", "c"), perm)


def ring(a, axis, way):
    n = lax.axis_size(axis)
    perm = [(i * 2 + c, (i + (way if c == 0 else -way)) % n * 2 + c) for i in range(n) for c in range(2)]
    return lax.ppermute(a, (axis, "c"), perm)


def gathered(parts, axis, order, joint, before, known={}):
    n, me = lax.axis_size(axis), lax.axis_index(axis)
    step = 1 - 2 * lax.axis_index("c")
    count, (rows, width) = len(parts), parts[0].shape
    blocks = {0: parts}
    ahead = back = parts
    for k in range(1, n // 2 + 1):
        if k == joint:
            ahead, back = [jnp.concatenate(ahead)], [jnp.concatenate(back)]
        if k in before:
            held = before[k](blocks)
            m = len(ahead)
            tied = after(*ahead, *back, *held)
            ahead, back = list(tied[:m]), list(tied[m : 2 * m])
        if k in known:
            ahead, back = blocks[-k], blocks[k] = known[k]
            continue
        ahead = blocks[-k] = [ring(p, axis, 1) for p in ahead]
        if k < n - n // 2:
            back = blocks[k] = [ring(p, axis, -1) for p in back]
    arrays, pieces = [], []
    for k, got in blocks.items():
        at = lax.rem(me + step * k + n, n) * count
        for i, place in enumerate(order):
            src, row = (i, 0) if len(got) == count else (0, i * rows)
            pieces.append((len(arrays) + src, row, rows, 0, (at + place) * rows))
        arrays += got
    return arrays, pieces, (n * count * rows, width), blocks


def block_at(axis, k):
    n = lax.axis_size(axis)
    return lax.rem(lax.axis_index(axis) + (1 - 2 * lax.axis_index("c")) * k + n, n)


def scattered(share, axis, first):
    n, me = lax.axis_size(axis), lax.axis_index(axis)
    step = 1 - 2 * lax.axis_index("c")
    came, second = [], []
    for way, hops, got in ((1, n // 2, first[0]), (-1, n - n // 2 - 1, first[1])):
        got = ring(got, axis, way)
        for k in range(hops - 1, 0, -1):
            sent = hop([got], share(lax.rem(me + way * step * k + n, n)))
            if k == hops - 1:
                second.append(sent)
            got = ring(sent, axis, way)
        came.append(got)
    return came, second


def dot(a, b, dims):
    return lax.dot_general(a, b, (dims, ((), ())), preferred_element_type=F32)


def after(first, *rest):
    return lax.optimization_barrier((first,) + rest)


def on_device(activations, out_grad, weight):
    h = lax.axis_index("yl")
    c = lax.axis_index("c")
    tokens, width = out_grad.shape
    own_tokens, features = activations.shape
    rows = weight.shape[1]
    half = rows // 2
    owners = features // rows

    low = jnp.concatenate([activations[:, d * rows : d * rows + half] for d in range(owners)], axis=1)
    high = jnp.concatenate([activations[:, d * rows + half : (d + 1) * rows] for d in range(owners)], axis=1)
    acts_mine, acts_sent = jnp.where(h == 0, low, high), jnp.where(h == 0, high, low)
    acts_sent, acts_mine, weight, out_grad = after(acts_sent, acts_mine, weight, out_grad)
    acts_got = swap(acts_sent, "yl")

    w_mine = lax.dynamic_slice_in_dim(weight[0], h * half, half, 0)
    w_sent = lax.dynamic_slice_in_dim(weight[0], (1 - h) * half, half, 0)
    out = [(ring(acts_mine, "z", 1), ring(acts_mine, "z", -1))]
    out.append((ring(out[0][0], "z", 1), ring(out[0][1], "z", -1)))
    *_, acts_got, w_got = after(*out[1], acts_got, swap(w_sent, "yl"))
    other = ring(acts_got, "z", 1), ring(acts_got, "z", -1)
    known = {1: tuple([a, b] for a, b in zip(out[0], other))}
    known[2] = tuple([a, ring(b, "z", way)] for a, b, way in zip(out[1], other, (1, -1)))
    w_pair = jnp.concatenate([w_mine, w_got], axis=1)
    *_, blocks = gathered([w_pair], "x", (0,), 0, {2: lambda b: [known[2][0][1], known[2][1][1]]})
    near = [0, -1, 1, -2]
    ws = [blocks[k][0] for k in near]
    pieces = [(i, 0, half, 0, i * half) for i in range(owners)]
    w_all = placed(ws, pieces, (owners * half, 2 * width), owners - 1)

    part = tokens // 2
    g_sent = lax.dynamic_slice_in_dim(out_grad, c * part, part, 0)
    g_got = y_ring(after(acts_got, w_got, g_sent)[2])

    pairs = []

    def g_pair_of(blocks):
        got = after(blocks[-2][1], blocks[2][1], *ws[1:3], g_got)[-1]
        pieces = [(0, 0, tokens, 0, 0), (1, 0, part, width, c * part), (2, 0, part, width, (1 - c) * part)]
        pairs.append(placed([out_grad, got, swap(got, "c")], pieces, (tokens, 2 * width)))
        return pairs

    before = {3: lambda b: ws[1:3], 4: g_pair_of}
    arrays, acts_pieces, shape, blocks = gathered([acts_mine, acts_got], "z", (h, 1 - h), 3, before, known)
    (g_pair,) = pairs

    first = [first_sum(block_at("z", k), 2 * own_tokens, g_pair, w_all) for k in (4, -3)]

    def of_tokens(i):
        count = 2 * own_tokens
        return dot(lax.dynamic_slice_in_dim(g_pair, i * count, count, 0), w_all, ((1,), (1,)))

    came, second = scattered(of_tokens, "z", first)
    acts_all = placed(after(*second, *arrays)[2:], acts_pieces, shape)
    mine = of_tokens(lax.axis_index("z"))

    def finished(of):
        shape = jax.ShapeDtypeStruct((own_tokens, features // 2), BF16)
        return call(tokens_kernel, [of, of], came, (mine, own_tokens), [shape])[0]

    s_got = swap(finished(1 - h), "yl")
    shape = jax.ShapeDtypeStruct((own_tokens, features), BF16)
    input_grad = call(functools.partial(columns_kernel, half), [h] + [block_at("x", k) for k in near], [finished(h), s_got], None, [shape])[0]

    def of_rows(i):
        acts = lax.dynamic_slice_in_dim(acts_all, i * half, half, 1)
        return dot(acts, g_pair, ((0,), (0,)))

    came, _ = scattered(of_rows, "x", [hop([], of_rows(block_at("x", k))) for k in (2, -1)])
    mine = of_rows(lax.axis_index("x"))
    shapes = [jax.ShapeDtypeStruct((half, width), F32), coded_shape(half, width)]
    owned, coded = call(owned_kernel, [jnp.int32(0)], came + [mine], None, shapes, [(half, width)])
    shape = jax.ShapeDtypeStruct((rows, width), F32)
    weight_grad = call(rows_kernel, [h], [owned, swap(coded, "yl")], None, [shape])[0]
    return input_grad, weight_grad[None]


def solution(mesh):
    dp, out, in_ = mesh.devices.shape
    fine = Mesh(mesh.devices.reshape(dp, out // 2, 2, 2, in_ // 2), ("x", "z", "yl", "yh", "c"))
    tokens, split = P(("x", "z", "yl"), ("yh", "c")), P(("yh", "c"), "x", ("z", "yl"))
    return jax.shard_map(
        on_device,
        mesh=fine,
        in_specs=(tokens, P("x", ("z", "yl")), split),
        out_specs=(tokens, split),
        check_vma=False,
    )
```

```python
import functools

import jax
import jax.numpy as jnp
from jax import lax
from jax.experimental import pallas as pl
from jax.experimental.pallas import tpu as pltpu
from jax.sharding import Mesh, PartitionSpec as P

F32 = jnp.float32
BF16 = jnp.bfloat16
LANES = 128
TILE = 16
SQUARINGS = 4
TOP = 2.0**7.75
TINY = 1e-30
MIB = 1024 * 1024


def encode(v, s):
    a = jnp.abs(v) * s
    for _ in range(SQUARINGS):
        a = a * a
    return jnp.where(v < 0, -a, a).astype(BF16)


def decode(y, inv):
    y = y.astype(F32)
    a = jnp.exp2(jnp.log2(jnp.abs(y)) * 0.5**SQUARINGS) * inv
    return jnp.where(y < 0, -a, a)


def inverse_scale(ref):
    return 1.0 / ref[ref.shape[0] - TILE :, :].astype(F32)


def for_tiles(rows, body, init):
    return lax.fori_loop(0, rows // TILE, lambda i, x: body(pl.multiple_of(i * TILE, TILE), x), init, unroll=2)


def write_coded(v_ref, blocks, amax, out_ref):
    rows = v_ref.shape[0]
    coded = (TOP / jnp.maximum(amax, TINY)).astype(BF16)
    s = coded.astype(F32)
    out_ref[blocks * rows :, :] = coded

    def body(r, x):
        for j in range(blocks):
            at = j * LANES
            out_ref[pl.ds(j * rows + r, TILE), :] = encode(v_ref[pl.ds(r, TILE), at : at + LANES], s)
        return x

    for_tiles(rows, body, 0)


def summed_tile(own_ref, got, invs, r, j):
    rows = own_ref.shape[0]
    v = own_ref[pl.ds(r, TILE), j * LANES : (j + 1) * LANES]
    for ref, inv in zip(got, invs):
        v = v + decode(ref[pl.ds(j * rows + r, TILE), :], inv)
    return v


def hop_kernel(n_got, idx_ref, *refs):
    got, (own_ref, out_ref, v_ref) = refs[:n_got], refs[n_got:]
    blocks = v_ref.shape[1] // LANES
    invs = [inverse_scale(ref) for ref in got]

    def body(r, amax):
        for j in range(blocks):
            v = summed_tile(own_ref, got, invs, r, j)
            v_ref[pl.ds(r, TILE), j * LANES : (j + 1) * LANES] = v
            amax = jnp.maximum(amax, jnp.abs(v))
        return amax

    amax = for_tiles(v_ref.shape[0], body, jnp.zeros((TILE, LANES), F32))
    write_coded(v_ref, blocks, amax, out_ref)


def tokens_kernel(idx_ref, f_ref, b_ref, own_ref, out_ref):
    invs = [inverse_scale(f_ref), inverse_scale(b_ref)]
    rows = out_ref.shape[0]
    at = idx_ref[1] * rows

    def body(r, x):
        for j in range(own_ref.shape[1] // LANES):
            v = own_ref[pl.ds(r, TILE), j * LANES : (j + 1) * LANES]
            for ref, inv in zip((f_ref, b_ref), invs):
                row = pl.multiple_of(j * 2 * rows + at + r, TILE)
                v = v + decode(ref[pl.ds(row, TILE), :], inv)
            out_ref[pl.ds(r, TILE), j * LANES : (j + 1) * LANES] = v.astype(BF16)
        return x

    for_tiles(rows, body, 0)


def columns_kernel(half, at_ref, mine_ref, got_ref, out_ref):
    for j in range(mine_ref.shape[1] // half):
        at = slice(j * half, (j + 1) * half)
        mine_at = pl.multiple_of((2 * at_ref[1 + j] + at_ref[0]) * half, LANES)
        got_at = pl.multiple_of((2 * at_ref[1 + j] + 1 - at_ref[0]) * half, LANES)
        out_ref[:, pl.ds(mine_at, half)] = mine_ref[:, at]
        out_ref[:, pl.ds(got_at, half)] = got_ref[:, at]


def first_kernel(at_ref, g_ref, w_ref, out_ref, v_ref):
    v_ref[...] = dot(g_ref[...], w_ref[...], ((1,), (1,)))

    def body(r, amax):
        for j in range(v_ref.shape[1] // LANES):
            amax = jnp.maximum(amax, jnp.abs(v_ref[pl.ds(r, TILE), j * LANES : (j + 1) * LANES]))
        return amax

    amax = for_tiles(v_ref.shape[0], body, jnp.zeros((TILE, LANES), F32))
    write_coded(v_ref, v_ref.shape[1] // LANES, amax, out_ref)


def first_sum(i, rows, g_pair, w_all):
    width = g_pair.shape[1]
    shape = (rows, w_all.shape[0])
    out = coded_shape(*shape)
    return pl.pallas_call(
        first_kernel,
        grid_spec=pltpu.PrefetchScalarGridSpec(
            num_scalar_prefetch=1,
            grid=(1,),
            in_specs=[
                pl.BlockSpec((rows, width), lambda j, at: (at[0], 0)),
                pl.BlockSpec(memory_space=pltpu.VMEM),
            ],
            out_specs=whole(out.shape),
            scratch_shapes=[pltpu.VMEM(shape, F32)],
        ),
        out_shape=out,
        compiler_params=pltpu.CompilerParams(vmem_limit_bytes=10 * MIB),
        cost_estimate=pl.CostEstimate(
            flops=2 * width * shape[0] * shape[1], bytes_accessed=4 * out.size, transcendentals=0
        ),
    )(jnp.stack([jnp.int32(i)]), g_pair, w_all)


def owned_kernel(idx_ref, f_ref, b_ref, own_ref, mine_ref, out_ref, v_ref):
    invs = [inverse_scale(f_ref), inverse_scale(b_ref)]
    blocks = v_ref.shape[1] // LANES

    def body(r, amax):
        for j in range(2 * blocks):
            v = summed_tile(own_ref, (f_ref, b_ref), invs, r, j)
            if j < blocks:
                mine_ref[pl.ds(r, TILE), j * LANES : (j + 1) * LANES] = v
            else:
                v_ref[pl.ds(r, TILE), (j - blocks) * LANES : (j - blocks + 1) * LANES] = v
                amax = jnp.maximum(amax, jnp.abs(v))
        return amax

    amax = for_tiles(own_ref.shape[0], body, jnp.zeros((TILE, LANES), F32))
    write_coded(v_ref, blocks, amax, out_ref)


def rows_kernel(h_ref, mine_ref, got_ref, out_ref):
    rows = mine_ref.shape[0]
    inv = inverse_scale(got_ref)
    mine_at, got_at = h_ref[0] * rows, (1 - h_ref[0]) * rows

    def body(r, x):
        out_ref[pl.ds(pl.multiple_of(mine_at + r, TILE), TILE), :] = mine_ref[pl.ds(r, TILE), :]
        for j in range(mine_ref.shape[1] // LANES):
            v = decode(got_ref[pl.ds(j * rows + r, TILE), :], inv)
            out_ref[pl.ds(pl.multiple_of(got_at + r, TILE), TILE), j * LANES : (j + 1) * LANES] = v
        return x

    for_tiles(rows, body, 0)


def whole(shape):
    return pl.BlockSpec(shape, lambda i, idx: (0,) * len(shape))


def call(kernel, idx, wholes, block, out_shapes, scratch=()):
    in_specs, args = [whole(a.shape) for a in wholes], list(wholes)
    if block is not None:
        in_specs.append(pl.BlockSpec((block[1], block[0].shape[1]), lambda i, idx: (idx[0], 0)))
        args.append(block[0])
    size = sum(a.size * 4 for a in args) + sum(s.size * 4 for s in out_shapes)
    return pl.pallas_call(
        kernel,
        grid_spec=pltpu.PrefetchScalarGridSpec(
            num_scalar_prefetch=1,
            grid=(1,),
            in_specs=in_specs,
            out_specs=[whole(s.shape) for s in out_shapes],
            scratch_shapes=[pltpu.VMEM(s, F32) for s in scratch],
        ),
        out_shape=out_shapes,
        compiler_params=pltpu.CompilerParams(vmem_limit_bytes=10 * MIB),
        cost_estimate=pl.CostEstimate(flops=size * 8, bytes_accessed=size, transcendentals=0),
    )(jnp.stack([jnp.int32(i) for i in idx]), *args)


def placed_kernel(pieces, at_ref, *refs):
    srcs, out_ref, sems = refs[:-2], refs[-2], refs[-1]
    copies = []
    for i, (src, row, rows, col) in enumerate(pieces):
        ref = srcs[src]
        to = out_ref.at[pl.ds(pl.multiple_of(at_ref[i], LANES), rows), col : col + ref.shape[1]]
        copies.append(pltpu.make_async_copy(ref.at[row : row + rows], to, sems.at[i]))
    for copy in copies:
        copy.start()
    for copy in copies:
        copy.wait()


def placed(arrays, pieces, shape, far=0):
    fixed = [p[:4] for p in pieces]
    size = 2 * shape[0] * shape[1]
    return pl.pallas_call(
        functools.partial(placed_kernel, fixed),
        grid_spec=pltpu.PrefetchScalarGridSpec(
            num_scalar_prefetch=1,
            grid=(1,),
            in_specs=[pl.BlockSpec(memory_space=pltpu.VMEM if i >= far else pl.ANY) for i in range(len(arrays))],
            out_specs=pl.BlockSpec(memory_space=pltpu.VMEM),
            scratch_shapes=[pltpu.SemaphoreType.DMA((len(pieces),))],
        ),
        out_shape=jax.ShapeDtypeStruct(shape, BF16),
        compiler_params=pltpu.CompilerParams(vmem_limit_bytes=4 * MIB),
        cost_estimate=pl.CostEstimate(flops=0, bytes_accessed=2 * size, transcendentals=0),
    )(jnp.stack([jnp.int32(p[4]) for p in pieces]), *arrays)


def coded_shape(rows, width):
    return jax.ShapeDtypeStruct((width // LANES * rows + TILE, LANES), BF16)


def hop(got, mine):
    kernel = functools.partial(hop_kernel, len(got))
    return call(kernel, [jnp.int32(0)], got + [mine], None, [coded_shape(*mine.shape)], [mine.shape])[0]


def swap(a, axis):
    return lax.ppermute(a, axis, [(0, 1), (1, 0)])


def y_ring(a):
    perm = []
    for y in range(4):
        for c in range(2):
            t = (y + (1 if c == 0 else -1)) % 4
            perm.append((((y % 2) * 2 + y // 2) * 2 + c, ((t % 2) * 2 + t // 2) * 2 + c))
    return lax.ppermute(a, ("yl", "yh", "c"), perm)


def ring(a, axis, way):
    n = lax.axis_size(axis)
    perm = [(i * 2 + c, (i + (way if c == 0 else -way)) % n * 2 + c) for i in range(n) for c in range(2)]
    return lax.ppermute(a, (axis, "c"), perm)


def gathered(parts, axis, order, joint, before, known={}):
    n, me = lax.axis_size(axis), lax.axis_index(axis)
    step = 1 - 2 * lax.axis_index("c")
    count, (rows, width) = len(parts), parts[0].shape
    blocks = {0: parts}
    ahead = back = parts
    for k in range(1, n // 2 + 1):
        if k == joint:
            ahead, back = [jnp.concatenate(ahead)], [jnp.concatenate(back)]
        if k in before:
            held = before[k](blocks)
            m = len(ahead)
            tied = after(*ahead, *back, *held)
            ahead, back = list(tied[:m]), list(tied[m : 2 * m])
        if k in known:
            ahead, back = blocks[-k], blocks[k] = known[k]
            continue
        ahead = blocks[-k] = [ring(p, axis, 1) for p in ahead]
        if k < n - n // 2:
            back = blocks[k] = [ring(p, axis, -1) for p in back]
    arrays, pieces = [], []
    for k, got in blocks.items():
        at = lax.rem(me + step * k + n, n) * count
        for i, place in enumerate(order):
            src, row = (i, 0) if len(got) == count else (0, i * rows)
            pieces.append((len(arrays) + src, row, rows, 0, (at + place) * rows))
        arrays += got
    return arrays, pieces, (n * count * rows, width), blocks


def block_at(axis, k):
    n = lax.axis_size(axis)
    return lax.rem(lax.axis_index(axis) + (1 - 2 * lax.axis_index("c")) * k + n, n)


def scattered(share, axis, first):
    n, me = lax.axis_size(axis), lax.axis_index(axis)
    step = 1 - 2 * lax.axis_index("c")
    came, second = [], []
    for way, hops, got in ((1, n // 2, first[0]), (-1, n - n // 2 - 1, first[1])):
        got = ring(got, axis, way)
        for k in range(hops - 1, 0, -1):
            sent = hop([got], share(lax.rem(me + way * step * k + n, n)))
            if k == hops - 1:
                second.append(sent)
            got = ring(sent, axis, way)
        came.append(got)
    return came, second


def dot(a, b, dims):
    return lax.dot_general(a, b, (dims, ((), ())), preferred_element_type=F32)


def after(first, *rest):
    return lax.optimization_barrier((first,) + rest)


def on_device(activations, out_grad, weight):
    h = lax.axis_index("yl")
    c = lax.axis_index("c")
    tokens, width = out_grad.shape
    own_tokens, features = activations.shape
    rows = weight.shape[1]
    half = rows // 2
    owners = features // rows

    low = jnp.concatenate([activations[:, d * rows : d * rows + half] for d in range(owners)], axis=1)
    high = jnp.concatenate([activations[:, d * rows + half : (d + 1) * rows] for d in range(owners)], axis=1)
    acts_mine, acts_sent = jnp.where(h == 0, low, high), jnp.where(h == 0, high, low)
    acts_sent, acts_mine, weight, out_grad = after(acts_sent, acts_mine, weight, out_grad)
    acts_got = swap(acts_sent, "yl")

    w_mine = lax.dynamic_slice_in_dim(weight[0], h * half, half, 0)
    w_sent = lax.dynamic_slice_in_dim(weight[0], (1 - h) * half, half, 0)
    out = [(ring(acts_mine, "z", 1), ring(acts_mine, "z", -1))]
    out.append((ring(out[0][0], "z", 1), ring(out[0][1], "z", -1)))
    *_, acts_got, w_got = after(*out[1], acts_got, swap(w_sent, "yl"))
    other = ring(acts_got, "z", 1), ring(acts_got, "z", -1)
    known = {1: tuple([a, b] for a, b in zip(out[0], other))}
    known[2] = tuple([a, ring(b, "z", way)] for a, b, way in zip(out[1], other, (1, -1)))
    w_pair = jnp.concatenate([w_mine, w_got], axis=1)
    *_, blocks = gathered([w_pair], "x", (0,), 0, {2: lambda b: [known[2][0][1], known[2][1][1]]})
    near = [0, -1, 1, -2]
    ws = [blocks[k][0] for k in near]

    part = tokens // 2
    g_sent = lax.dynamic_slice_in_dim(out_grad, c * part, part, 0)
    g_got = y_ring(after(acts_got, w_got, g_sent)[2])

    pairs = []

    def g_pair_of(blocks):
        got = after(blocks[-2][1], blocks[2][1], *ws[1:3], g_got)[-1]
        pieces = [(0, 0, tokens, 0, 0), (1, 0, part, width, c * part), (2, 0, part, width, (1 - c) * part)]
        pairs.append(placed([out_grad, got, swap(got, "c")], pieces, (tokens, 2 * width)))
        return pairs

    before = {3: lambda b: ws[1:3], 4: g_pair_of}
    arrays, acts_pieces, shape, blocks = gathered([acts_mine, acts_got], "z", (h, 1 - h), 3, before, known)
    (g_pair,) = pairs

    pieces = [(i, 0, half, 0, i * half) for i in range(owners)]
    w_all = placed(ws[:-1] + [after(g_pair, ws[-1])[1]], pieces, (owners * half, 2 * width), owners - 1)
    first = [first_sum(block_at("z", k), 2 * own_tokens, g_pair, w_all) for k in (4, -3)]

    def of_tokens(i):
        count = 2 * own_tokens
        return dot(lax.dynamic_slice_in_dim(g_pair, i * count, count, 0), w_all, ((1,), (1,)))

    came, second = scattered(of_tokens, "z", first)
    acts_all = placed(after(*second, *arrays)[2:], acts_pieces, shape)
    mine = of_tokens(lax.axis_index("z"))

    def finished(of):
        shape = jax.ShapeDtypeStruct((own_tokens, features // 2), BF16)
        return call(tokens_kernel, [of, of], came, (mine, own_tokens), [shape])[0]

    s_got = swap(finished(1 - h), "yl")
    shape = jax.ShapeDtypeStruct((own_tokens, features), BF16)
    input_grad = call(functools.partial(columns_kernel, half), [h] + [block_at("x", k) for k in near], [finished(h), s_got], None, [shape])[0]

    def of_rows(i):
        acts = lax.dynamic_slice_in_dim(acts_all, i * half, half, 1)
        return dot(acts, g_pair, ((0,), (0,)))

    came, _ = scattered(of_rows, "x", [hop([], of_rows(block_at("x", k))) for k in (2, -1)])
    mine = of_rows(lax.axis_index("x"))
    shapes = [jax.ShapeDtypeStruct((half, width), F32), coded_shape(half, width)]
    owned, coded = call(owned_kernel, [jnp.int32(0)], came + [mine], None, shapes, [(half, width)])
    shape = jax.ShapeDtypeStruct((rows, width), F32)
    weight_grad = call(rows_kernel, [h], [owned, swap(coded, "yl")], None, [shape])[0]
    return input_grad, weight_grad[None]


def solution(mesh):
    dp, out, in_ = mesh.devices.shape
    fine = Mesh(mesh.devices.reshape(dp, out // 2, 2, 2, in_ // 2), ("x", "z", "yl", "yh", "c"))
    tokens, split = P(("x", "z", "yl"), ("yh", "c")), P(("yh", "c"), "x", ("z", "yl"))
    return jax.shard_map(
        on_device,
        mesh=fine,
        in_specs=(tokens, P("x", ("z", "yl")), split),
        out_specs=(tokens, split),
        check_vma=False,
    )
```

```python
import functools

import jax
import jax.numpy as jnp
from jax import lax
from jax.experimental import pallas as pl
from jax.experimental.pallas import tpu as pltpu
from jax.sharding import Mesh, PartitionSpec as P

F32 = jnp.float32
BF16 = jnp.bfloat16
LANES = 128
TILE = 16
SQUARINGS = 4
TOP = 2.0**7.75
TINY = 1e-30
MIB = 1024 * 1024


def encode(v, s):
    a = jnp.abs(v) * s
    for _ in range(SQUARINGS):
        a = a * a
    return jnp.where(v < 0, -a, a).astype(BF16)


def decode(y, inv):
    y = y.astype(F32)
    a = jnp.exp2(jnp.log2(jnp.abs(y)) * 0.5**SQUARINGS) * inv
    return jnp.where(y < 0, -a, a)


def inverse_scale(ref):
    return 1.0 / ref[ref.shape[0] - TILE :, :].astype(F32)


def for_tiles(rows, body, init):
    return lax.fori_loop(0, rows // TILE, lambda i, x: body(pl.multiple_of(i * TILE, TILE), x), init, unroll=2)


def write_coded(v_ref, blocks, amax, out_ref):
    rows = v_ref.shape[0]
    coded = (TOP / jnp.maximum(amax, TINY)).astype(BF16)
    s = coded.astype(F32)
    out_ref[blocks * rows :, :] = coded

    def body(r, x):
        for j in range(blocks):
            at = j * LANES
            out_ref[pl.ds(j * rows + r, TILE), :] = encode(v_ref[pl.ds(r, TILE), at : at + LANES], s)
        return x

    for_tiles(rows, body, 0)


def summed_tile(own_ref, got, invs, r, j):
    rows = own_ref.shape[0]
    v = own_ref[pl.ds(r, TILE), j * LANES : (j + 1) * LANES]
    for ref, inv in zip(got, invs):
        v = v + decode(ref[pl.ds(j * rows + r, TILE), :], inv)
    return v


def hop_kernel(n_got, idx_ref, *refs):
    got, (own_ref, out_ref, v_ref) = refs[:n_got], refs[n_got:]
    blocks = v_ref.shape[1] // LANES
    invs = [inverse_scale(ref) for ref in got]

    def body(r, amax):
        for j in range(blocks):
            v = summed_tile(own_ref, got, invs, r, j)
            v_ref[pl.ds(r, TILE), j * LANES : (j + 1) * LANES] = v
            amax = jnp.maximum(amax, jnp.abs(v))
        return amax

    amax = for_tiles(v_ref.shape[0], body, jnp.zeros((TILE, LANES), F32))
    write_coded(v_ref, blocks, amax, out_ref)


def tokens_kernel(idx_ref, f_ref, b_ref, own_ref, out_ref):
    invs = [inverse_scale(f_ref), inverse_scale(b_ref)]
    rows = out_ref.shape[0]
    at = idx_ref[1] * rows

    def body(r, x):
        for j in range(own_ref.shape[1] // LANES):
            v = own_ref[pl.ds(r, TILE), j * LANES : (j + 1) * LANES]
            for ref, inv in zip((f_ref, b_ref), invs):
                row = pl.multiple_of(j * 2 * rows + at + r, TILE)
                v = v + decode(ref[pl.ds(row, TILE), :], inv)
            out_ref[pl.ds(r, TILE), j * LANES : (j + 1) * LANES] = v.astype(BF16)
        return x

    for_tiles(rows, body, 0)


def columns_kernel(half, at_ref, mine_ref, got_ref, out_ref):
    for j in range(mine_ref.shape[1] // half):
        at = slice(j * half, (j + 1) * half)
        mine_at = pl.multiple_of((2 * at_ref[1 + j] + at_ref[0]) * half, LANES)
        got_at = pl.multiple_of((2 * at_ref[1 + j] + 1 - at_ref[0]) * half, LANES)
        out_ref[:, pl.ds(mine_at, half)] = mine_ref[:, at]
        out_ref[:, pl.ds(got_at, half)] = got_ref[:, at]


def first_kernel(at_ref, g_ref, near_ref, last_ref, out_ref, v_ref):
    v_ref[:, : near_ref.shape[0]] = dot(g_ref[...], near_ref[...], ((1,), (1,)))
    v_ref[:, near_ref.shape[0] :] = dot(g_ref[...], last_ref[...], ((1,), (1,)))

    def body(r, amax):
        for j in range(v_ref.shape[1] // LANES):
            amax = jnp.maximum(amax, jnp.abs(v_ref[pl.ds(r, TILE), j * LANES : (j + 1) * LANES]))
        return amax

    amax = for_tiles(v_ref.shape[0], body, jnp.zeros((TILE, LANES), F32))
    write_coded(v_ref, v_ref.shape[1] // LANES, amax, out_ref)


def first_sum(i, rows, g_pair, near, last):
    width = g_pair.shape[1]
    shape = (rows, near.shape[0] + last.shape[0])
    out = coded_shape(*shape)
    return pl.pallas_call(
        first_kernel,
        grid_spec=pltpu.PrefetchScalarGridSpec(
            num_scalar_prefetch=1,
            grid=(1,),
            in_specs=[
                pl.BlockSpec((rows, width), lambda j, at: (at[0], 0)),
                pl.BlockSpec(memory_space=pltpu.VMEM),
                pl.BlockSpec(memory_space=pltpu.VMEM),
            ],
            out_specs=whole(out.shape),
            scratch_shapes=[pltpu.VMEM(shape, F32)],
        ),
        out_shape=out,
        compiler_params=pltpu.CompilerParams(vmem_limit_bytes=10 * MIB),
        cost_estimate=pl.CostEstimate(
            flops=2 * width * shape[0] * shape[1], bytes_accessed=4 * out.size, transcendentals=0
        ),
    )(jnp.stack([jnp.int32(i)]), g_pair, near, last)


def owned_kernel(idx_ref, f_ref, b_ref, own_ref, mine_ref, out_ref, v_ref):
    invs = [inverse_scale(f_ref), inverse_scale(b_ref)]
    blocks = v_ref.shape[1] // LANES

    def body(r, amax):
        for j in range(2 * blocks):
            v = summed_tile(own_ref, (f_ref, b_ref), invs, r, j)
            if j < blocks:
                mine_ref[pl.ds(r, TILE), j * LANES : (j + 1) * LANES] = v
            else:
                v_ref[pl.ds(r, TILE), (j - blocks) * LANES : (j - blocks + 1) * LANES] = v
                amax = jnp.maximum(amax, jnp.abs(v))
        return amax

    amax = for_tiles(own_ref.shape[0], body, jnp.zeros((TILE, LANES), F32))
    write_coded(v_ref, blocks, amax, out_ref)


def rows_kernel(h_ref, mine_ref, got_ref, out_ref):
    rows = mine_ref.shape[0]
    inv = inverse_scale(got_ref)
    mine_at, got_at = h_ref[0] * rows, (1 - h_ref[0]) * rows

    def body(r, x):
        out_ref[pl.ds(pl.multiple_of(mine_at + r, TILE), TILE), :] = mine_ref[pl.ds(r, TILE), :]
        for j in range(mine_ref.shape[1] // LANES):
            v = decode(got_ref[pl.ds(j * rows + r, TILE), :], inv)
            out_ref[pl.ds(pl.multiple_of(got_at + r, TILE), TILE), j * LANES : (j + 1) * LANES] = v
        return x

    for_tiles(rows, body, 0)


def whole(shape):
    return pl.BlockSpec(shape, lambda i, idx: (0,) * len(shape))


def call(kernel, idx, wholes, block, out_shapes, scratch=()):
    in_specs, args = [whole(a.shape) for a in wholes], list(wholes)
    if block is not None:
        in_specs.append(pl.BlockSpec((block[1], block[0].shape[1]), lambda i, idx: (idx[0], 0)))
        args.append(block[0])
    size = sum(a.size * 4 for a in args) + sum(s.size * 4 for s in out_shapes)
    return pl.pallas_call(
        kernel,
        grid_spec=pltpu.PrefetchScalarGridSpec(
            num_scalar_prefetch=1,
            grid=(1,),
            in_specs=in_specs,
            out_specs=[whole(s.shape) for s in out_shapes],
            scratch_shapes=[pltpu.VMEM(s, F32) for s in scratch],
        ),
        out_shape=out_shapes,
        compiler_params=pltpu.CompilerParams(vmem_limit_bytes=10 * MIB),
        cost_estimate=pl.CostEstimate(flops=size * 8, bytes_accessed=size, transcendentals=0),
    )(jnp.stack([jnp.int32(i) for i in idx]), *args)


def placed_kernel(pieces, at_ref, *refs):
    srcs, out_ref, sems = refs[:-2], refs[-2], refs[-1]
    copies = []
    for i, (src, row, rows, col) in enumerate(pieces):
        ref = srcs[src]
        to = out_ref.at[pl.ds(pl.multiple_of(at_ref[i], LANES), rows), col : col + ref.shape[1]]
        copies.append(pltpu.make_async_copy(ref.at[row : row + rows], to, sems.at[i]))
    for copy in copies:
        copy.start()
    for copy in copies:
        copy.wait()


def placed(arrays, pieces, shape, far=0):
    fixed = [p[:4] for p in pieces]
    size = 2 * shape[0] * shape[1]
    return pl.pallas_call(
        functools.partial(placed_kernel, fixed),
        grid_spec=pltpu.PrefetchScalarGridSpec(
            num_scalar_prefetch=1,
            grid=(1,),
            in_specs=[pl.BlockSpec(memory_space=pltpu.VMEM if i >= far else pl.ANY) for i in range(len(arrays))],
            out_specs=pl.BlockSpec(memory_space=pltpu.VMEM),
            scratch_shapes=[pltpu.SemaphoreType.DMA((len(pieces),))],
        ),
        out_shape=jax.ShapeDtypeStruct(shape, BF16),
        compiler_params=pltpu.CompilerParams(vmem_limit_bytes=4 * MIB),
        cost_estimate=pl.CostEstimate(flops=0, bytes_accessed=2 * size, transcendentals=0),
    )(jnp.stack([jnp.int32(p[4]) for p in pieces]), *arrays)


def coded_shape(rows, width):
    return jax.ShapeDtypeStruct((width // LANES * rows + TILE, LANES), BF16)


def hop(got, mine):
    kernel = functools.partial(hop_kernel, len(got))
    return call(kernel, [jnp.int32(0)], got + [mine], None, [coded_shape(*mine.shape)], [mine.shape])[0]


def swap(a, axis):
    return lax.ppermute(a, axis, [(0, 1), (1, 0)])


def y_ring(a):
    perm = []
    for y in range(4):
        for c in range(2):
            t = (y + (1 if c == 0 else -1)) % 4
            perm.append((((y % 2) * 2 + y // 2) * 2 + c, ((t % 2) * 2 + t // 2) * 2 + c))
    return lax.ppermute(a, ("yl", "yh", "c"), perm)


def ring(a, axis, way):
    n = lax.axis_size(axis)
    perm = [(i * 2 + c, (i + (way if c == 0 else -way)) % n * 2 + c) for i in range(n) for c in range(2)]
    return lax.ppermute(a, (axis, "c"), perm)


def gathered(parts, axis, order, joint, before, known={}):
    n, me = lax.axis_size(axis), lax.axis_index(axis)
    step = 1 - 2 * lax.axis_index("c")
    count, (rows, width) = len(parts), parts[0].shape
    blocks = {0: parts}
    ahead = back = parts
    for k in range(1, n // 2 + 1):
        if k == joint:
            ahead, back = [jnp.concatenate(ahead)], [jnp.concatenate(back)]
        if k in before:
            held = before[k](blocks)
            m = len(ahead)
            tied = after(*ahead, *back, *held)
            ahead, back = list(tied[:m]), list(tied[m : 2 * m])
        if k in known:
            ahead, back = blocks[-k], blocks[k] = known[k]
            continue
        ahead = blocks[-k] = [ring(p, axis, 1) for p in ahead]
        if k < n - n // 2:
            back = blocks[k] = [ring(p, axis, -1) for p in back]
    arrays, pieces = [], []
    for k, got in blocks.items():
        at = lax.rem(me + step * k + n, n) * count
        for i, place in enumerate(order):
            src, row = (i, 0) if len(got) == count else (0, i * rows)
            pieces.append((len(arrays) + src, row, rows, 0, (at + place) * rows))
        arrays += got
    return arrays, pieces, (n * count * rows, width), blocks


def block_at(axis, k):
    n = lax.axis_size(axis)
    return lax.rem(lax.axis_index(axis) + (1 - 2 * lax.axis_index("c")) * k + n, n)


def scattered(share, axis, first):
    n, me = lax.axis_size(axis), lax.axis_index(axis)
    step = 1 - 2 * lax.axis_index("c")
    came, second = [], []
    for way, hops, got in ((1, n // 2, first[0]), (-1, n - n // 2 - 1, first[1])):
        got = ring(got, axis, way)
        for k in range(hops - 1, 0, -1):
            sent = hop([got], share(lax.rem(me + way * step * k + n, n)))
            if k == hops - 1:
                second.append(sent)
            got = ring(sent, axis, way)
        came.append(got)
    return came, second


def dot(a, b, dims):
    return lax.dot_general(a, b, (dims, ((), ())), preferred_element_type=F32)


def after(first, *rest):
    return lax.optimization_barrier((first,) + rest)


def on_device(activations, out_grad, weight):
    h = lax.axis_index("yl")
    c = lax.axis_index("c")
    tokens, width = out_grad.shape
    own_tokens, features = activations.shape
    rows = weight.shape[1]
    half = rows // 2
    owners = features // rows

    low = jnp.concatenate([activations[:, d * rows : d * rows + half] for d in range(owners)], axis=1)
    high = jnp.concatenate([activations[:, d * rows + half : (d + 1) * rows] for d in range(owners)], axis=1)
    acts_mine, acts_sent = jnp.where(h == 0, low, high), jnp.where(h == 0, high, low)
    acts_sent, acts_mine, weight, out_grad = after(acts_sent, acts_mine, weight, out_grad)
    acts_got = swap(acts_sent, "yl")

    w_mine = lax.dynamic_slice_in_dim(weight[0], h * half, half, 0)
    w_sent = lax.dynamic_slice_in_dim(weight[0], (1 - h) * half, half, 0)
    out = [(ring(acts_mine, "z", 1), ring(acts_mine, "z", -1))]
    out.append((ring(out[0][0], "z", 1), ring(out[0][1], "z", -1)))
    *_, acts_got, w_got = after(*out[1], acts_got, swap(w_sent, "yl"))
    other = ring(acts_got, "z", 1), ring(acts_got, "z", -1)
    known = {1: tuple([a, b] for a, b in zip(out[0], other))}
    known[2] = tuple([a, ring(b, "z", way)] for a, b, way in zip(out[1], other, (1, -1)))
    w_pair = jnp.concatenate([w_mine, w_got], axis=1)
    *_, blocks = gathered([w_pair], "x", (0,), 0, {2: lambda b: [known[2][0][1], known[2][1][1]]})
    near = [0, -1, 1, -2]
    ws = [blocks[k][0] for k in near]

    part = tokens // 2
    g_sent = lax.dynamic_slice_in_dim(out_grad, c * part, part, 0)
    g_got = y_ring(after(acts_got, w_got, g_sent)[2])

    pairs = []

    def g_pair_of(blocks):
        got = after(blocks[-2][1], blocks[2][1], *ws[1:3], g_got)[-1]
        pieces = [(0, 0, tokens, 0, 0), (1, 0, part, width, c * part), (2, 0, part, width, (1 - c) * part)]
        pairs.append(placed([out_grad, got, swap(got, "c")], pieces, (tokens, 2 * width)))
        return pairs

    before = {3: lambda b: ws[1:3], 4: g_pair_of}
    arrays, acts_pieces, shape, blocks = gathered([acts_mine, acts_got], "z", (h, 1 - h), 3, before, known)
    (g_pair,) = pairs

    pieces = [(i, 0, half, 0, i * half) for i in range(owners - 1)]
    w_near = placed(ws[:-1], pieces, ((owners - 1) * half, 2 * width), owners - 1)
    *_, w_last = after(g_pair, w_near, ws[-1])
    first = [first_sum(block_at("z", k), 2 * own_tokens, g_pair, w_near, w_last) for k in (4, -3)]
    w_all = jnp.concatenate(after(*first, w_near, w_last)[2:])

    def of_tokens(i):
        count = 2 * own_tokens
        return dot(lax.dynamic_slice_in_dim(g_pair, i * count, count, 0), w_all, ((1,), (1,)))

    came, second = scattered(of_tokens, "z", first)
    acts_all = placed(after(*second, *arrays)[2:], acts_pieces, shape)
    mine = of_tokens(lax.axis_index("z"))

    def finished(of):
        shape = jax.ShapeDtypeStruct((own_tokens, features // 2), BF16)
        return call(tokens_kernel, [of, of], came, (mine, own_tokens), [shape])[0]

    s_got = swap(finished(1 - h), "yl")
    shape = jax.ShapeDtypeStruct((own_tokens, features), BF16)
    input_grad = call(functools.partial(columns_kernel, half), [h] + [block_at("x", k) for k in near], [finished(h), s_got], None, [shape])[0]

    def of_rows(i):
        acts = lax.dynamic_slice_in_dim(acts_all, i * half, half, 1)
        return dot(acts, g_pair, ((0,), (0,)))

    came, _ = scattered(of_rows, "x", [hop([], of_rows(block_at("x", k))) for k in (2, -1)])
    mine = of_rows(lax.axis_index("x"))
    shapes = [jax.ShapeDtypeStruct((half, width), F32), coded_shape(half, width)]
    owned, coded = call(owned_kernel, [jnp.int32(0)], came + [mine], None, shapes, [(half, width)])
    shape = jax.ShapeDtypeStruct((rows, width), F32)
    weight_grad = call(rows_kernel, [h], [owned, swap(coded, "yl")], None, [shape])[0]
    return input_grad, weight_grad[None]


def solution(mesh):
    dp, out, in_ = mesh.devices.shape
    fine = Mesh(mesh.devices.reshape(dp, out // 2, 2, 2, in_ // 2), ("x", "z", "yl", "yh", "c"))
    tokens, split = P(("x", "z", "yl"), ("yh", "c")), P(("yh", "c"), "x", ("z", "yl"))
    return jax.shard_map(
        on_device,
        mesh=fine,
        in_specs=(tokens, P("x", ("z", "yl")), split),
        out_specs=(tokens, split),
        check_vma=False,
    )
```
